32 devices in a mesh: dp: 2 (over y), row: 4 (over x, core), col: 4 (over z).
Axes of the slice: x: 2, y: 2, z: 4, core: 2. Of those that a mesh axis runs over, the one named last changes fastest.
Arguments:
- hidden_in: bfloat16 [8192, 1536], P(('dp', 'row', 'col')), may hold values from -6 to 6
- norm_gain_attn: float32 [1536], replicated, may hold values from 0.1 to 1.9
- norm_gain_moe: float32 [1536], replicated, may hold values from 0.1 to 1.9
- w_qkv: bfloat16 [1536, 2560], P(('dp', 'row'), 'col'), may hold values from -0.15625 to 0.15625
- w_out: bfloat16 [1536, 1536], P(('dp', 'row'), 'col'), may hold values from -1.25 to 1.25
- router: float32 [1536, 32], replicated, may hold values from -0.078125 to 0.078125
- w_in: bfloat16 [32, 1536, 1024], P(('row', 'col')), may hold values from -0.15625 to 0.15625
- w_down: bfloat16 [32, 512, 1536], P(('row', 'col')), may hold values from -1 to 1
- lengths: int32 [8, 8], P(('dp', 'row')), may hold values from 1 to 512, 1024 in all within a row
- routes: int32 [8192, 8], P(('dp', 'row', 'col')), may hold values from 0 to 31, all different within a row; in each aligned block of 256 rows (0 to 255, 256 to 511, ...) at most 128 rows name the same one
- out_grad: bfloat16 [8192, 1536], P(('dp', 'row', 'col')), may hold values from -6 to 6
Outputs:
- result: float32 [8192, 1536], P(('dp', 'row', 'col'))
- grad_hidden: float32 [8192, 1536], P(('dp', 'row', 'col'))
- grad_norm_attn: float32 [1536], replicated
- grad_norm_moe: float32 [1536], replicated
- grad_w_qkv: float32 [1536, 2560], P(('dp', 'row'), 'col')
- grad_w_out: float32 [1536, 1536], P(('dp', 'row'), 'col')
- grad_router: float32 [1536, 32], replicated
- grad_w_in: float32 [32, 1536, 1024], P(('row', 'col'))
- grad_w_down: float32 [32, 512, 1536], P(('row', 'col'))
The draws below stay inside these ranges and needn't reach their ends.
Inputs may be any that keep to these rules, and one draw needn't show every extreme that they name: Each row holds the lengths of 8 packed sequences in order, summing to 1024; the longest is exactly 512. `routes`: each row names 8 different experts; among the 256 rows of one device no expert is named by more than 128 rows, a bound that some block reaches.
All inputs are finite; a program needn't handle non-finite values.
Results may differ from the reference program's by a relative error of at most 0.019.
Values may be sent and summed in bfloat16 or wider, within the bound.
No kernel may reach another device: no remote copies, remote signals or barrier semaphores. Data moves between devices by JAX's collectives and lax.ppermute only.
A program may use at most 256 MiB of HBM per device.

```python
import functools
import math
import jax
import jax.numpy as jnp
import numpy as np
from jax import lax

D = 1536
HEADS = 24
KV_HEADS = 8
HD = 64
FFE = 512
TOP = 8
TOK_DEV = 256
REP = 3
QKVW = 2560
BLOCK_TOK = 1024
BLOCKS = 8
TOKENS = 8192
SEQ_MAX = 512
SEQS = 8
EXPERTS = 32
CAP = 128


def block_scale(rng, shape, pieces, low, largest):
    def one(axis_at, blocks):
        steps = jax.random.uniform(jax.random.fold_in(jax.random.fold_in(rng, 6), axis_at), (blocks,), jnp.float32, low / len(pieces), largest / len(pieces))
        return jnp.repeat(jnp.exp(steps), shape[axis_at] // blocks).reshape((-1,) + (1,) * (len(shape) - axis_at - 1))

    factor_of = one(*pieces[0])
    for cut in pieces[1:]:
        factor_of = factor_of * one(*cut)
    return factor_of


def split_up(number_of, total, bound, lean):
    loads = [(1 << 20) // math.isqrt(grade ** lean) + 1 for grade in range(2, number_of + 1)]
    spare, given = total - bound - (number_of - 1), [1] * (number_of - 1)
    while spare > 0:
        free = [i for i in range(number_of - 1) if given[i] < bound]
        mass, left = sum([loads[i] for i in free]), spare
        for i in free:
            extra = min(bound - given[i], max(1, left * loads[i] // mass), spare)
            given[i] = given[i] + extra
            spare = spare - extra
    return np.array([bound] + given)


def uneven_parts(stream_key, count, total, bound, skew):
    if count == 2:
        one = jax.random.randint(stream_key, (), max(1, total - bound), min(bound, total - 1) + 1)
        return jnp.stack([one, total - one])
    tallies = jnp.asarray(split_up(count, total, bound, skew), jnp.int32)
    twos = (count - 1) // 2
    donor, receiver = tallies[1:1 + 2 * twos:2], tallies[2:2 + 2 * twos:2]
    room = jnp.minimum(donor - 1, bound - receiver)
    shifted = jax.random.randint(jax.random.fold_in(stream_key, 1), (twos,), 0, 1 << 20) % (room + 1)
    tallies = tallies.at[1:1 + 2 * twos:2].set(donor - shifted).at[2:2 + 2 * twos:2].set(receiver + shifted)
    return tallies[jax.random.permutation(jax.random.fold_in(stream_key, 2), count)]


def assign_block(key, own, number, rows, count, top, bound, skew):
    order = jax.random.permutation(key, count)
    crowded, usual = portions_of(count, rows * top, bound, skew, True), portions_of(count, rows * top, bound, skew, False)
    places = jnp.arange(count)

    def named(sizes, offset_by):
        used = int((sizes > 0).sum())
        fixed = max(1, used // 4)
        shifted = fixed + (places - fixed + offset_by * (used - fixed)) % max(1, count - fixed)
        return jnp.zeros((count,), jnp.int32).at[order[jnp.where(places < fixed, places, shifted)]].set(jnp.asarray(sizes, jnp.int32))

    sizes = jnp.where(number % 4 == 0, named(crowded, number // 4), named(usual, number - number // 4 - 1))
    mixed = jax.random.permutation(jax.random.fold_in(own, 3), count)
    giver, sink = mixed[0:count // 2 * 2:2], mixed[1:count // 2 * 2:2]
    room = jnp.minimum(sizes[giver] - 1, bound - sizes[sink]) // 2
    room = jnp.where((giver == order[0]) | (sink == order[0]) | (sizes[sink] == 0), 0, jnp.maximum(room, 0))
    shifted = jax.random.randint(jax.random.fold_in(own, 4), (count // 2,), 0, 1 << 20) % (room + 1)
    sizes = sizes.at[giver].add(-shifted).at[sink].add(shifted)
    members = jnp.searchsorted(jnp.cumsum(sizes), jnp.arange(rows * top), side="right").astype(jnp.int32)
    table = members.reshape(top, rows).T
    table = table[jax.random.permutation(jax.random.fold_in(own, 1), rows)]
    offset_by = jax.random.randint(jax.random.fold_in(own, 2), (rows, 1), 0, top)
    return jnp.take_along_axis(table, (jnp.arange(top)[None, :] + offset_by) % top, axis=1)


def portions_of(amount, total, bound, slope, full):
    loads = [(1 << 20) // math.isqrt(rank ** slope) + 1 for rank in range(1, amount + 1)]
    largest = bound if full else min(bound, max(-(-total // amount), total * loads[0] // sum(loads)))
    least = 1 if total - largest >= amount - 1 else 0
    given, surplus = [largest] + [least] * (amount - 1), total - largest - least * (amount - 1)
    while surplus > 0:
        free = [i for i in range(1, amount) if given[i] < largest] or [i for i in range(1, amount) if given[i] < bound]
        mass, remaining = sum([loads[i] for i in free]), surplus
        for i in free:
            extra = min(bound - given[i], max(1, remaining * loads[i] // mass), surplus)
            given[i] = given[i] + extra
            surplus = surplus - extra
    return np.array(given)


def gaussian(stream_key, shape, spread, limit, cuts=(), kind=jnp.bfloat16):
    array = jax.random.normal(stream_key, shape, jnp.float32) * spread
    if len(cuts) > 0:
        array = block_scale(stream_key, shape, cuts, -0.22, 0.18) * array
    return jnp.clip(array, min=-limit, max=limit).astype(kind)


def setup_inputs(seed: int = 0) -> dict:
    streams_of = jax.random.split(jax.random.key(seed), 12)
    hidden_in = gaussian(streams_of[0], (TOKENS, D), 1.0, 6.0, ((0, 32),))
    norm_gain_attn = jnp.clip(1.0 + 0.18 * jax.random.normal(streams_of[1], (D,), jnp.float32), 0.1, 1.9)
    norm_gain_moe = jnp.clip(1.0 + 0.18 * jax.random.normal(streams_of[2], (D,), jnp.float32), 0.1, 1.9)
    w_qkv = gaussian(streams_of[3], (D, QKVW), D ** -0.5, 0.15625, ((0, 8), (1, 4)))
    w_out = gaussian(streams_of[4], (D, HEADS * HD), (HEADS * HD // 64) ** -0.5, 1.25, ((0, 8), (1, 4)))
    router = gaussian(streams_of[5], (D, EXPERTS), (4 * D) ** -0.5, 0.078125, (), jnp.float32)
    w_in = gaussian(streams_of[6], (EXPERTS, D, 2 * FFE), D ** -0.5, 0.15625, ((0, 16),))
    w_down = gaussian(streams_of[7], (EXPERTS, FFE, D), (FFE // 16) ** -0.5, 1.0, ((0, 16),))
    lengths = jax.vmap(lambda own: uneven_parts(own, SEQS, BLOCK_TOK, SEQ_MAX, 2))(jax.random.split(streams_of[8], BLOCKS)).reshape((BLOCKS, SEQS)).astype(jnp.int32)
    routes_keys = jax.random.split(jax.random.fold_in(streams_of[9], 1), TOKENS // TOK_DEV)
    routes_turns = jax.random.permutation(jax.random.fold_in(streams_of[9], 3), TOKENS // TOK_DEV)
    routes = jax.vmap(lambda own, number: assign_block(jax.random.fold_in(streams_of[9], 2), own, number, TOK_DEV, EXPERTS, TOP, CAP, 1))(routes_keys, routes_turns).reshape((TOKENS, TOP))
    out_grad = gaussian(streams_of[10], (TOKENS, D), 1.0, 6.0, ((0, 32),))
    return {"hidden_in": hidden_in, "norm_gain_attn": norm_gain_attn, "norm_gain_moe": norm_gain_moe, "w_qkv": w_qkv, "w_out": w_out, "router": router, "w_in": w_in, "w_down": w_down, "lengths": lengths, "routes": routes, "out_grad": out_grad}


EPSILON = 1e-06
HIGHEST = lax.Precision.HIGHEST
MASKED_SCORE = -1e+30

@jax.custom_vjp
def low(v):
    return lax.optimization_barrier(v.astype(jnp.bfloat16)).astype(jnp.float32)

@jax.custom_vjp
def low_back(v):
    return v

def low_keep(v):
    return (low(v), None)

def low_pass(kept, grad):
    return (grad,)

def back_keep(v):
    return (v, None)

def back_low(kept, grad):
    return (low(grad),)
low.defvjp(low_keep, low_pass)
low_back.defvjp(back_keep, back_low)

def high_dot(left_op, right_op):
    return jnp.dot(left_op, right_op, precision=HIGHEST, preferred_element_type=jnp.float32)

def rope_tables(positions, head_dim):
    freq_index = jnp.arange(head_dim // 2, dtype=jnp.float32)
    inverse = jnp.exp(freq_index * (-2.0 * math.log(10000.0) / head_dim))
    angles = positions.astype(jnp.float32)[:, None] * inverse[None, :]
    angles = jnp.concatenate([angles, angles], axis=1)
    return (jnp.cos(angles), jnp.sin(angles))

def rotate(values, cos_table, sin_table):
    middle_dim = values.shape[-1] // 2
    turned = jnp.concatenate([-values[..., middle_dim:], values[..., :middle_dim]], axis=-1)
    cos_shape = (cos_table.shape[0],) + (1,) * (values.ndim - 2) + (cos_table.shape[1],)
    return values * cos_table.reshape(cos_shape) + turned * sin_table.reshape(cos_shape)

def seq_layout(block_lengths, block_tok):
    seq_ends = jnp.cumsum(block_lengths)
    starts = seq_ends - block_lengths
    places = jnp.arange(block_tok, dtype=jnp.int32)
    segment = lax.optimization_barrier(jnp.sum((places[:, None] >= seq_ends[None, :]).astype(jnp.int32), axis=1))
    owners = segment[:, None] == jnp.arange(block_lengths.shape[0], dtype=jnp.int32)[None, :]
    offset = lax.optimization_barrier(jnp.sum(jnp.where(owners, starts[None, :], 0), axis=1))
    return (places - offset, segment)

def norm_apply(row_vals, gain_vec):
    scale_row = lax.rsqrt(lax.optimization_barrier(jnp.mean(row_vals * row_vals, axis=1, keepdims=True)) + EPSILON)
    return row_vals * scale_row * gain_vec

def attend_block(packed, gain_vec, qkv_w, out_w):
    block_rows, block_lengths = packed
    normed = low(norm_apply(block_rows, gain_vec))
    mixed_cols = low_back(high_dot(normed, qkv_w)).reshape(BLOCK_TOK, KV_HEADS, (REP + 2) * HD)
    query_cols = mixed_cols[:, :, :REP * HD].reshape(BLOCK_TOK, HEADS, HD)
    key_cols = mixed_cols[:, :, REP * HD:(REP + 1) * HD]
    value_cols = low(mixed_cols[:, :, (REP + 1) * HD:])
    positions, segment = seq_layout(block_lengths, BLOCK_TOK)
    cos_table, sin_table = rope_tables(positions, HD)
    queries = low(rotate(query_cols, cos_table, sin_table)).reshape(BLOCK_TOK, KV_HEADS, REP, HD)
    key_rot = low(rotate(key_cols, cos_table, sin_table))
    scores = low_back(jnp.einsum('qgrd,kgd->grqk', queries, key_rot, precision=HIGHEST) * HD ** (-0.5))
    places = jnp.arange(BLOCK_TOK, dtype=jnp.int32)
    allowed = (segment[:, None] == segment[None, :]) & (places[:, None] >= places[None, :])
    soft_w = jax.nn.softmax(jnp.where(allowed, scores, MASKED_SCORE), axis=-1)
    mixed_heads = jnp.einsum('grqk,kgd->qgrd', low(soft_w), value_cols, precision=HIGHEST)
    heads_low = low(low_back(mixed_heads.reshape(BLOCK_TOK, HEADS * HD)))
    return low_back(high_dot(heads_low, out_w.T))

def expert_term(normed, gate_flat, row_ids, front_w, back_w):
    is_valid = row_ids >= 0
    safe_ids = jnp.maximum(row_ids, 0)
    tok_ids = safe_ids // TOP
    row_vals = low_back(jnp.where(is_valid[:, None], normed[tok_ids], 0.0))
    gate_up = low_back(high_dot(row_vals, front_w))
    activated = low(jax.nn.silu(gate_up[:, :FFE]) * gate_up[:, FFE:])
    out_rows = low(low_back(high_dot(activated, back_w)))
    weight = jnp.where(is_valid, gate_flat[safe_ids], 0.0)
    return jnp.zeros((TOKENS, D), jnp.float32).at[tok_ids].add(weight[:, None] * out_rows)

def route_table(routes):
    groups = TOKENS // TOK_DEV
    flat_ids = routes.reshape(groups, TOK_DEV * TOP)
    expert_ids = jnp.arange(EXPERTS, dtype=jnp.int32)
    onehot = (flat_ids[:, :, None] == expert_ids[None, None, :]).astype(jnp.int32)
    before = jnp.cumsum(onehot, axis=1) - onehot
    slot_ids = lax.optimization_barrier(jnp.sum(before * onehot, axis=2))
    group_ids = jnp.arange(groups, dtype=jnp.int32)[:, None]
    entry_ids = jnp.arange(TOK_DEV * TOP, dtype=jnp.int32)[None, :]
    target = (flat_ids * groups + group_ids) * CAP + slot_ids
    source = group_ids * (TOK_DEV * TOP) + entry_ids
    slot_table = jnp.full((EXPERTS * groups * CAP,), -1, jnp.int32).at[target.reshape(-1)].set(source.reshape(-1))
    return slot_table.reshape(EXPERTS, groups * CAP)

def layer_forward(hidden, gain_attn, gain_moe, qkv_w, out_w, router_w, in_w, down_w, lengths, routes, slot_table):
    block_fn = jax.checkpoint(functools.partial(attend_block, gain_vec=gain_attn, qkv_w=qkv_w, out_w=out_w))
    attn_out = lax.map(block_fn, (hidden.reshape(BLOCKS, BLOCK_TOK, D), lengths))
    middle = hidden + attn_out.reshape(TOKENS, D)
    normed = low(norm_apply(middle, gain_moe))
    logits = high_dot(normed, router_w)
    gate_probs = jax.nn.softmax(jnp.take_along_axis(logits, routes, axis=1), axis=1)
    term_fn = jax.checkpoint(functools.partial(expert_term, normed, gate_probs.reshape(-1)))

    def expert_step(total_out, packed):
        row_ids, front_w, back_w = packed
        return (total_out + term_fn(row_ids, front_w, back_w), None)
    moe_sum, unused = lax.scan(expert_step, jnp.zeros((TOKENS, D), jnp.float32), (slot_table, in_w, down_w))
    return middle + moe_sum

def reference(hidden_in, norm_gain_attn, norm_gain_moe, w_qkv, w_out, router, w_in, w_down, lengths, routes, out_grad):
    slot_table = route_table(routes)

    def closed(hidden, gain_attn, gain_moe, qkv_w, out_w, router_w, in_w, down_w):
        return layer_forward(hidden, gain_attn, gain_moe, qkv_w, out_w, router_w, in_w, down_w, lengths, routes, slot_table)
    result, pullback = jax.vjp(closed, hidden_in.astype(jnp.float32), norm_gain_attn, norm_gain_moe, w_qkv.astype(jnp.float32), w_out.astype(jnp.float32), router, w_in.astype(jnp.float32), w_down.astype(jnp.float32))
    gradients = pullback(out_grad.astype(jnp.float32))
    return (result, gradients[0], gradients[1], gradients[2], gradients[3], gradients[4], gradients[5], gradients[6], gradients[7])
```

```python
import functools
import math

import jax
import jax.numpy as jnp
from jax import lax
from jax.experimental import pallas as pl
from jax.experimental.pallas import tpu as pltpu
from jax.sharding import PartitionSpec as P

HD = 64
FFE = 512
TOP = 8
REP = 3
SEQ_MAX = 512

EPSILON = 1e-06
HIGHEST = lax.Precision.HIGHEST
MASKED_SCORE = -1e30
F32 = jnp.float32
BF16 = jnp.bfloat16


def dot_nn(left, right):
    return lax.dot_general(left, right, (((1,), (0,)), ((), ())), preferred_element_type=F32)


def dot_nt(left, right):
    return lax.dot_general(left, right, (((1,), (1,)), ((), ())), preferred_element_type=F32)


def dot_tn(left, right):
    return lax.dot_general(left, right, (((0,), (0,)), ((), ())), preferred_element_type=F32)


def moe_body(
    cap, tile, tiles,
    first_ref, x_ref, dy_ref, rt_ref, rs_ref, win_ref, wdn_ref,
    res_ref, gn_ref, dg_ref, dwi_ref, dwd_ref,
    buf, gate, slot, run, offs, acc_i, acc_d,
):
    step = pl.program_id(0)
    sources = slot.shape[1]
    tok, feat = x_ref.shape
    experts = rs_ref.shape[0] // 3
    local = buf.shape[0]
    ff = wdn_ref.shape[1]

    def one_hot(srow):
        places = lax.broadcasted_iota(jnp.int32, (cap, tok), 0).astype(F32)
        return srow == places

    @pl.when(step < sources)
    def _gather():
        x = x_ref[...]
        dy = dy_ref[...]

        @pl.when(step == 0)
        def _():
            for e in range(local):
                run[e] = 0

        thirds = dot_nt(rs_ref[...], x)
        logits = (thirds[2 * experts :] + thirds[experts : 2 * experts]) + thirds[:experts]
        ids = lax.broadcasted_iota(jnp.int32, (experts, tok), 0)
        rt = rt_ref[0]
        used = ids == rt[0:1]
        for k in range(1, rt.shape[0]):
            used = used | (ids == rt[k : k + 1])
        top = jnp.max(jnp.where(used, logits, MASKED_SCORE), axis=0, keepdims=True)
        terms = jnp.where(used, jnp.exp(logits - top), 0.0)
        gates = terms / jnp.sum(terms, axis=0, keepdims=True)
        before = (
            lax.broadcasted_iota(jnp.int32, (tok, tok), 0)
            < lax.broadcasted_iota(jnp.int32, (tok, tok), 1)
        )
        used_f = jnp.where(used, 1.0, 0.0)
        rank = dot_nn(used_f.astype(BF16), jnp.where(before, 1.0, 0.0).astype(BF16))
        for e in range(local):
            mine = ids == first_ref[0] + e
            grow = jnp.sum(jnp.where(mine, gates, 0.0), axis=0, keepdims=True)
            srow = jnp.sum(jnp.where(mine & used, rank + 1.0, 0.0), axis=0, keepdims=True) - 1.0
            hot = one_hot(srow)
            hot_b = jnp.where(hot, 1.0, 0.0).astype(BF16)
            off = pl.multiple_of(run[e], 16)
            buf[e, pl.ds(off, cap), :feat] = dot_nn(hot_b, x).astype(BF16)
            buf[e, pl.ds(off, cap), feat:] = dot_nn(hot_b, dy).astype(BF16)
            gcol = jnp.sum(jnp.where(hot, grow, 0.0), axis=1, keepdims=True)
            gate[e, pl.ds(off, cap), :] = jnp.broadcast_to(gcol, (cap, 128))
            slot[e, pl.ds(step, 1), :] = srow
            offs[e, step] = off
            count = jnp.sum(jnp.where(mine, used_f, 0.0)).astype(jnp.int32)
            run[e] = off + ((count + 15) & -16)

        @pl.when(step == sources - 1)
        def _():
            for e in range(local):
                end = pl.multiple_of(run[e], 16)
                buf[e, pl.ds(end, tile), :] = jnp.zeros((tile, 2 * feat), BF16)
                gate[e, pl.ds(end, tile), :] = jnp.zeros((tile, 128), F32)

    work = step - sources
    e = work // tiles
    j = work % tiles

    @pl.when((work >= 0) & (work < local * tiles))
    def _experts():
        @pl.when(j == 0)
        def _():
            acc_i[...] = jnp.zeros_like(acc_i)
            acc_d[...] = jnp.zeros_like(acc_d)

        @pl.when(j * tile < run[e])
        def _():
            at = pl.ds(pl.multiple_of(j * tile, tile), tile)
            rows = buf[e, at, :feat]
            grads = buf[e, at, feat:]
            g = gate[e, at, 0:1]
            a = dot_nn(rows, win_ref[0, :, :ff])
            b = dot_nn(rows, win_ref[0, :, ff:])
            ga = dot_nt(grads, wdn_ref[0])
            sig = 1.0 / (1.0 + jnp.exp(-a))
            silu = a * sig
            act = silu * b
            gate[e, at, :] = jnp.broadcast_to(
                jnp.sum(act * ga, axis=1, keepdims=True), (tile, 128)
            )
            gag = g * ga
            da = (gag * b * (sig * (1.0 + a * (1.0 - sig)))).astype(BF16)
            db = (gag * silu).astype(BF16)
            act_g = (g * act).astype(BF16)
            acc_d[...] += dot_tn(act_g, grads)
            acc_i[:, :ff] += dot_tn(rows, da)
            acc_i[:, ff:] += dot_tn(rows, db)
            buf[e, at, :feat] = dot_nn(act_g, wdn_ref[0]).astype(BF16)
            buf[e, at, feat:] = (
                dot_nt(da, win_ref[0, :, :ff]) + dot_nt(db, win_ref[0, :, ff:])
            ).astype(BF16)

        @pl.when(j == tiles - 1)
        def _():
            dwi_ref[0] = acc_i[...].astype(BF16)
            dwd_ref[0] = acc_d[...].astype(BF16)

    back = work - local * tiles

    @pl.when(back >= 0)
    def _scatter():
        total = None
        for e in range(local):
            srow = slot[e, pl.ds(back, 1), :]
            hot = one_hot(srow)
            off = pl.multiple_of(offs[e, back], 16)
            hot_b = jnp.where(hot, 1.0, 0.0).astype(BF16)
            term = dot_tn(hot_b, buf[e, pl.ds(off, cap), :])
            total = term if total is None else total + term
            dcol = gate[e, pl.ds(off, cap), 0:1]
            dg_ref[0, e : e + 1, :] = jnp.sum(jnp.where(hot, dcol, 0.0), axis=0, keepdims=True)
        dg_ref[0, local:, :] = jnp.zeros((dg_ref.shape[1] - local, tok), F32)
        res_ref[...] = total[:, :feat].astype(BF16)
        gn_ref[...] = total[:, feat:].astype(BF16)


def moe_experts(first, x_all, dy_all, rt_all, router_parts, w_in, w_down, cap):
    sources, top, tok = rt_all.shape
    feat = x_all.shape[1]
    local, _, ff2 = w_in.shape
    ff = ff2 // 2
    tile = min(256, sources * cap)
    tiles = sources * cap // tile
    room = sources * cap + max(tile, cap)
    steps = 2 * sources + local * tiles

    def src(i, first_ref):
        return (jnp.minimum(i, sources - 1), 0)

    def src3(i, first_ref):
        return (jnp.minimum(i, sources - 1), 0, 0)

    def exp3(i, first_ref):
        return (jnp.clip((i - sources) // tiles, 0, local - 1), 0, 0)

    def dst(i, first_ref):
        return (jnp.maximum(i - sources - local * tiles, 0), 0)

    def dst3(i, first_ref):
        return (jnp.maximum(i - sources - local * tiles, 0), 0, 0)

    pairs = sources * tok * top * local // (experts_of(router_parts))
    flops = 2 * pairs * feat * ff * 9
    return pl.pallas_call(
        functools.partial(moe_body, cap, tile, tiles),
        grid_spec=pltpu.PrefetchScalarGridSpec(
            num_scalar_prefetch=1,
            grid=(steps,),
            in_specs=[
                pl.BlockSpec((tok, feat), src),
                pl.BlockSpec((tok, feat), src),
                pl.BlockSpec((1, top, tok), src3),
                pl.BlockSpec(router_parts.shape, lambda i, f: (0, 0)),
                pl.BlockSpec((1, feat, ff2), exp3, pipeline_mode=pl.Buffered(1)),
                pl.BlockSpec((1, ff, feat), exp3, pipeline_mode=pl.Buffered(1)),
            ],
            out_specs=[
                pl.BlockSpec((tok, feat), dst),
                pl.BlockSpec((tok, feat), dst),
                pl.BlockSpec((1, 8, tok), dst3),
                pl.BlockSpec((1, feat, ff2), exp3, pipeline_mode=pl.Buffered(1)),
                pl.BlockSpec((1, ff, feat), exp3, pipeline_mode=pl.Buffered(1)),
            ],
            scratch_shapes=[
                pltpu.VMEM((local, room, 2 * feat), BF16),
                pltpu.VMEM((local, room, 128), F32),
                pltpu.VMEM((local, sources, tok), F32),
                pltpu.SMEM((local,), jnp.int32),
                pltpu.SMEM((local, sources), jnp.int32),
                pltpu.VMEM((feat, ff2), F32),
                pltpu.VMEM((ff, feat), F32),
            ],
        ),
        out_shape=[
            jax.ShapeDtypeStruct(x_all.shape, BF16),
            jax.ShapeDtypeStruct(x_all.shape, BF16),
            jax.ShapeDtypeStruct((sources, 8, tok), F32),
            jax.ShapeDtypeStruct(w_in.shape, BF16),
            jax.ShapeDtypeStruct(w_down.shape, BF16),
        ],
        compiler_params=pltpu.CompilerParams(vmem_limit_bytes=60 * 1024 * 1024),
        cost_estimate=pl.CostEstimate(
            flops=flops, bytes_accessed=5 * x_all.size * 2, transcendentals=0
        ),
        name="moe_experts",
    )(first, x_all, dy_all, rt_all, router_parts, w_in, w_down)


def experts_of(router_parts):
    return router_parts.shape[0] // 3


def split_router(router):
    flat = router.T
    one = flat.astype(BF16)
    rest = flat - one.astype(F32)
    two = rest.astype(BF16)
    three = (rest - two.astype(F32)).astype(BF16)
    return jnp.concatenate([one, two, three], axis=0)


def lane_low(shape):
    return lax.broadcasted_iota(jnp.int32, shape, 1) < HD


def twist(tile_vals):
    width = tile_vals.shape[1]
    lane = lax.broadcasted_iota(jnp.int32, tile_vals.shape, 1)
    ahead = pltpu.roll(tile_vals, width - HD // 2, 1)
    behind = pltpu.roll(tile_vals, HD // 2, 1)
    return jnp.where(lane % HD < HD // 2, -ahead, behind)


def both_halves(tile_vals, low):
    kept = jnp.where(lane_low(tile_vals.shape) == low, tile_vals, 0.0)
    return kept + pltpu.roll(kept, HD, 1)


def head_places():
    per = REP + 2
    def at(index):
        return (index // 2, index % 2 == 0)
    groups = []
    for g in range(2):
        base = g * per
        groups.append(
            ([at(base + r) for r in range(REP)], at(base + REP), at(base + REP + 1))
        )
    return groups


def chunk_span(a, tok):
    reach = -(-(SEQ_MAX - 1) // tok)
    return max(0, a - reach) * tok, (a + 1) * tok


def mask_bias(start_row, a, tok):
    low, high = chunk_span(a, tok)
    shape = (high - low, tok)
    keys = lax.broadcasted_iota(jnp.int32, shape, 0) + low
    queries = lax.broadcasted_iota(jnp.int32, shape, 1) + a * tok
    allowed = (keys >= start_row) & (keys <= queries)
    return jnp.where(allowed, 0.0, MASKED_SCORE)


def attn_forward_body(
    chunks, here_ref, *refs,
):
    ins, (w_ref, cos_ref, sin_ref, start_ref, qkv_ref, kk_ref, vv_ref, lse_ref, heads_ref) = (
        refs[:chunks],
        refs[chunks:],
    )
    tok = ins[0].shape[0]
    here = here_ref[0]
    places = head_places()
    for k in range(chunks):
        a = lax.rem(here + (chunks - k), chunks)
        at = pl.ds(pl.multiple_of(a * tok, tok), tok)
        mixed = dot_nn(ins[k][...], w_ref[...])
        cos = cos_ref[at, :]
        sin = sin_ref[at, :]
        tiles = [mixed[:, 128 * i : 128 * (i + 1)] for i in range(mixed.shape[1] // 128)]
        turned = [t * cos + twist(t) * sin for t in tiles]
        for g, (queries, key, value) in enumerate(places):
            for r, (tile_at, low) in enumerate(queries):
                part = jnp.where(lane_low(tiles[0].shape) == low, turned[tile_at], 0.0)
                slot = 128 * (g * REP + r)
                qkv_ref[at, slot : slot + 128] = part.astype(BF16)
            kk_ref[at, 128 * g : 128 * (g + 1)] = both_halves(turned[key[0]], key[1]).astype(BF16)
            vv_ref[at, 128 * g : 128 * (g + 1)] = both_halves(tiles[value[0]], value[1]).astype(BF16)
    for a in range(chunks):
        low_key, high_key = chunk_span(a, tok)
        bias = mask_bias(start_ref[a : a + 1, :], a, tok)
        out = [None] * REP
        for g, (queries, _, _) in enumerate(places):
            keys = kk_ref[low_key:high_key, 128 * g : 128 * (g + 1)]
            vals = vv_ref[low_key:high_key, 128 * g : 128 * (g + 1)]
            for r in range(REP):
                head = g * REP + r
                q = qkv_ref[a * tok : (a + 1) * tok, 128 * head : 128 * (head + 1)]
                scores = dot_nt(keys, q) * HD ** (-0.5) + bias
                top = jnp.max(scores, axis=0, keepdims=True)
                terms = jnp.exp(scores - top)
                total = jnp.sum(terms, axis=0, keepdims=True)
                probs = (terms * (1.0 / total)).astype(BF16)
                lse_ref[head, a : a + 1, :] = top + jnp.log(total)
                mix = dot_tn(probs, vals)
                t = head // 2
                low = lane_low(mix.shape)
                out[t] = mix if head % 2 == 0 else jnp.where(low, out[t], mix)
        to = pl.ds(pl.multiple_of(lax.rem(here + (chunks - a), chunks) * tok, tok), tok)
        for t in range(REP):
            heads_ref[to, 128 * t : 128 * (t + 1)] = out[t].astype(BF16)


def attn_forward(here, parts, w_cols, cos, sin, starts):
    chunks = len(parts)
    tok, feat = parts[0].shape
    total = chunks * tok
    cols = w_cols.shape[1]
    return pl.pallas_call(
        functools.partial(attn_forward_body, chunks),
        in_specs=[pl.BlockSpec(memory_space=pltpu.SMEM)]
        + [pl.BlockSpec(memory_space=pltpu.VMEM)] * (chunks + 4),
        out_specs=[pl.BlockSpec(memory_space=pltpu.VMEM)] * 5,
        out_shape=[
            jax.ShapeDtypeStruct((total, 128 * 2 * REP), BF16),
            jax.ShapeDtypeStruct((total, 256), BF16),
            jax.ShapeDtypeStruct((total, 256), BF16),
            jax.ShapeDtypeStruct((2 * REP, 8, tok), F32),
            jax.ShapeDtypeStruct((total, 2 * REP * HD), BF16),
        ],
        compiler_params=pltpu.CompilerParams(vmem_limit_bytes=48 * 1024 * 1024),
        cost_estimate=pl.CostEstimate(
            flops=2 * total * feat * cols * 4, bytes_accessed=8 * total * cols, transcendentals=0
        ),
        name="attn_forward",
    )(here, *parts, w_cols, cos, sin, starts)


def attn_backward_body(
    chunks, here_ref, grads_ref, q_ref, kk_ref, vv_ref, lse_ref, cos_ref, sin_ref, start_ref,
    out_ref, dk, dv, dq,
):
    tok = q_ref.shape[0] // chunks
    here = here_ref[0]
    dk[...] = jnp.zeros_like(dk)
    dv[...] = jnp.zeros_like(dv)
    for a in range(chunks):
        low_key, high_key = chunk_span(a, tok)
        bias = mask_bias(start_ref[a : a + 1, :], a, tok)
        at = pl.ds(pl.multiple_of(lax.rem(here + (chunks - a), chunks) * tok, tok), tok)
        for g in range(2):
            keys = kk_ref[low_key:high_key, 128 * g : 128 * (g + 1)]
            vals = vv_ref[low_key:high_key, 128 * g : 128 * (g + 1)]
            for r in range(REP):
                head = g * REP + r
                q = q_ref[a * tok : (a + 1) * tok, 128 * head : 128 * (head + 1)]
                t, is_low = head // 2, head % 2 == 0
                pair = grads_ref[at, 128 * t : 128 * (t + 1)]
                grad = jnp.where(lane_low(pair.shape) == is_low, pair, jnp.zeros_like(pair))
                scores = dot_nt(keys, q) * HD ** (-0.5) + bias
                probs = jnp.exp(scores - lse_ref[head, a : a + 1, :])
                grad_probs = dot_nt(vals, grad)
                dv[low_key:high_key, 128 * g : 128 * (g + 1)] += dot_nn(probs.astype(BF16), grad)
                inner = jnp.sum(probs * grad_probs, axis=0, keepdims=True)
                grad_scores = (probs * (grad_probs - inner)).astype(BF16)
                dk[low_key:high_key, 128 * g : 128 * (g + 1)] += dot_nn(grad_scores, q)
                part = dot_tn(grad_scores, keys)
                here_at = slice(128 * t, 128 * (t + 1))
                rows = slice(a * tok, (a + 1) * tok)
                if is_low:
                    dq[rows, here_at] = part
                else:
                    dq[rows, here_at] = jnp.where(lane_low(part.shape), dq[rows, here_at], part)
    for a in range(chunks):
        rows = slice(a * tok, (a + 1) * tok)
        to = pl.ds(pl.multiple_of(lax.rem(here + (chunks - a), chunks) * tok, tok), tok)
        cos = cos_ref[rows, :]
        sin = sin_ref[rows, :]

        def back(vals):
            return (vals * cos - twist(vals) * sin) * HD ** (-0.5)

        def whole(vals):
            return vals + pltpu.roll(vals, HD, 1)

        low = lane_low((tok, 128))
        keys = [back(whole(dk[rows, 128 * g : 128 * (g + 1)])) for g in range(2)]
        vals = [whole(dv[rows, 128 * g : 128 * (g + 1)]) for g in range(2)]
        qs = [back(dq[rows, 128 * t : 128 * (t + 1)]) for t in range(REP)]
        tiles = [
            qs[0],
            jnp.where(low, qs[1], keys[0]),
            jnp.where(low, vals[0], qs[1]),
            qs[2],
            jnp.where(low, keys[1], vals[1]),
        ]
        for i, vals_of in enumerate(tiles):
            out_ref[to, 128 * i : 128 * (i + 1)] = vals_of.astype(BF16)


def attn_backward(here, grads, q_rows, key_rows, value_rows, lse, cos, sin, starts, chunks):
    total = q_rows.shape[0]
    cols = 2 * (REP + 2) * HD
    return pl.pallas_call(
        functools.partial(attn_backward_body, chunks),
        in_specs=[pl.BlockSpec(memory_space=pltpu.SMEM)]
        + [pl.BlockSpec(memory_space=pltpu.VMEM)] * 8,
        out_specs=pl.BlockSpec(memory_space=pltpu.VMEM),
        out_shape=jax.ShapeDtypeStruct((total, cols), BF16),
        scratch_shapes=[
            pltpu.VMEM((total, 256), F32),
            pltpu.VMEM((total, 256), F32),
            pltpu.VMEM((total, 2 * REP * HD), F32),
        ],
        compiler_params=pltpu.CompilerParams(vmem_limit_bytes=48 * 1024 * 1024),
        cost_estimate=pl.CostEstimate(
            flops=12 * total * total * cols, bytes_accessed=8 * total * cols, transcendentals=0
        ),
        name="attn_backward",
    )(here, grads, q_rows, key_rows, value_rows, lse, cos, sin, starts)


def rope_rows(positions):
    freq_index = jnp.arange(HD // 2, dtype=F32)
    inverse = jnp.exp(freq_index * (-2.0 * math.log(10000.0) / HD))
    angles = positions.astype(F32)[:, None] * inverse[None, :]
    return jnp.tile(jnp.cos(angles), (1, 4)), jnp.tile(jnp.sin(angles), (1, 4))


def seq_layout(block_lengths, block_tok):
    seq_ends = jnp.cumsum(block_lengths)
    starts = seq_ends - block_lengths
    places = jnp.arange(block_tok, dtype=jnp.int32)
    segment = jnp.sum((places[:, None] >= seq_ends[None, :]).astype(jnp.int32), axis=1)
    owners = segment[:, None] == jnp.arange(block_lengths.shape[0], dtype=jnp.int32)[None, :]
    offset = jnp.sum(jnp.where(owners, starts[None, :], 0), axis=1)
    return places - offset, offset


def norm_apply(row_vals, gain_vec):
    scale_row = lax.rsqrt(jnp.mean(row_vals * row_vals, axis=1, keepdims=True) + EPSILON)
    return row_vals * scale_row * gain_vec


def norm_back(row_vals, gain_vec, grad):
    scale_row = lax.rsqrt(jnp.mean(row_vals * row_vals, axis=1, keepdims=True) + EPSILON)
    weighted = grad * gain_vec
    inner = jnp.mean(weighted * row_vals, axis=1, keepdims=True)
    return scale_row * weighted - row_vals * (scale_row * scale_row * scale_row * inner)


def shift(values, axis, by):
    size = lax.axis_size(axis)
    return lax.ppermute(values, axis, [(i, (i + by) % size) for i in range(size)])


def swap(values, axis, bit):
    size = lax.axis_size(axis)
    return lax.ppermute(values, axis, [(i, i ^ bit) for i in range(size)])


def sum_everywhere(values, axes):
    for axis in axes:
        bit = 1
        while bit < lax.axis_size(axis):
            values = values + swap(values, axis, bit)
            bit *= 2
    return values


def shards(
    hidden_in,
    norm_gain_attn,
    norm_gain_moe,
    w_qkv,
    w_out,
    router,
    w_in,
    w_down,
    lengths,
    routes,
    out_grad,
):
    tok, feat = hidden_in.shape
    cols = lax.axis_size("col")
    rows = lax.axis_size("row")
    block_tok = tok * cols
    experts = router.shape[1]
    sources = rows * cols
    local = w_in.shape[0]
    cap = tok * TOP * 2 // experts
    head_cols = w_out.shape[1]
    plane = ("row", "col")
    here = lax.axis_index("col").astype(jnp.int32).reshape(1)
    first = (lax.axis_index(plane) * local).astype(jnp.int32).reshape(1)
    rows_in = hidden_in.astype(F32)
    grad_out = out_grad.astype(F32)

    normed_attn = norm_apply(rows_in, norm_gain_attn).astype(BF16)
    parts = [normed_attn]
    for _ in range(cols - 1):
        parts.append(shift(parts[-1], "col", 1))
    qkv_own = lax.all_gather(w_qkv, ("dp", "row"), axis=0, tiled=True)
    out_line = jnp.concatenate([w_out] + [shift(w_out, "col", -k) for k in range(1, cols)], axis=1)
    out_full = lax.all_gather(out_line, ("dp", "row"), axis=0, tiled=True)
    dy_all = lax.all_gather(out_grad, plane, axis=0, tiled=True)
    rt_all = lax.all_gather(routes.T, plane, axis=0)

    positions, seq_start = seq_layout(lengths[0], block_tok)
    cos, sin = rope_rows(positions)
    starts = jnp.pad(seq_start.reshape(cols, tok), ((0, -cols % 8), (0, 0)))
    q_rows, key_rows, value_rows, lse, heads_block = attn_forward(
        here, parts, qkv_own, cos, sin, starts
    )
    heads = jnp.concatenate(
        [
            shift(heads_block[k * tok : (k + 1) * tok], "col", -k) if k else heads_block[:tok]
            for k in range(cols)
        ],
        axis=1,
    )
    middle = rows_in + dot_nt(heads, out_full)
    normed_moe = norm_apply(middle, norm_gain_moe).astype(BF16)

    x_all = lax.all_gather(normed_moe, plane, axis=0, tiled=True)
    res_part, gn_part, dg, dwi, dwd = moe_experts(
        first, x_all, dy_all, rt_all, split_router(router), w_in, w_down, cap
    )
    if lax.axis_size("dp") == 2:
        grad_w_in = dwi.astype(F32) + swap(dwi, "dp", 1).astype(F32)
        grad_w_down = dwd.astype(F32) + swap(dwd, "dp", 1).astype(F32)
    else:
        grad_w_in = lax.psum(dwi, "dp").astype(F32)
        grad_w_down = lax.psum(dwd, "dp").astype(F32)

    normed_wide = normed_moe.astype(F32)
    logits = jnp.dot(normed_wide, router, precision=HIGHEST, preferred_element_type=F32)
    expert_ids = jnp.arange(experts, dtype=jnp.int32)
    used = jnp.any(routes[:, :, None] == expert_ids[None, None, :], axis=1)
    top = jnp.max(jnp.where(used, logits, MASKED_SCORE), axis=1, keepdims=True)
    terms = jnp.where(used, jnp.exp(logits - top), 0.0)
    gates = terms / jnp.sum(terms, axis=1, keepdims=True)
    dg_back = lax.all_to_all(dg, plane, split_axis=0, concat_axis=0, tiled=True)
    grad_gates = dg_back[:, :local].reshape(experts, tok).T
    grad_logits = gates * (grad_gates - jnp.sum(gates * grad_gates, axis=1, keepdims=True))
    router_term = lax.dot_general(
        grad_logits, router, (((1,), (1,)), ((), ())), precision=HIGHEST, preferred_element_type=F32
    )
    grad_router = lax.dot_general(
        normed_wide, grad_logits, (((0,), (0,)), ((), ())), precision=HIGHEST, preferred_element_type=F32
    )

    gn = lax.psum_scatter(gn_part, plane, scatter_dimension=0, tiled=True)
    grad_nm = gn.astype(F32) + router_term
    grad_middle = grad_out + norm_back(middle, norm_gain_moe, grad_nm)
    middle_scale = lax.rsqrt(jnp.mean(middle * middle, axis=1, keepdims=True) + EPSILON)
    gain_moe_part = jnp.sum(grad_nm * middle * middle_scale, axis=0)
    grad_attn = grad_middle.astype(BF16)

    grad_heads = dot_nn(grad_attn, out_full).astype(BF16)
    grads_block = jnp.concatenate(
        [
            shift(grad_heads[:, k * head_cols : (k + 1) * head_cols], "col", k)
            if k
            else grad_heads[:, :head_cols]
            for k in range(cols)
        ],
        axis=0,
    )
    res = lax.psum_scatter(res_part, plane, scatter_dimension=0, tiled=True)
    result = middle + res.astype(F32)

    grad_mixed = attn_backward(
        here, grads_block, q_rows, key_rows, value_rows, lse, cos, sin, starts, cols
    )
    mixed_back = [
        shift(grad_mixed[k * tok : (k + 1) * tok], "col", -k) if k else grad_mixed[:tok]
        for k in range(cols)
    ]
    qkv_line = jnp.concatenate([shift(w_qkv, "col", -k) for k in range(1, cols)], axis=1)
    qkv_rest = lax.all_gather(qkv_line, ("dp", "row"), axis=0, tiled=True)
    grad_na = dot_nt(mixed_back[0], qkv_own) + dot_nt(
        jnp.concatenate(mixed_back[1:], axis=1), qkv_rest
    )
    grad_hidden = grad_middle + norm_back(rows_in, norm_gain_attn, grad_na)

    block_rows = jnp.concatenate(parts, axis=0)
    w_qkv_part = dot_tn(block_rows, grad_mixed)
    gain_attn_part = jnp.sum(w_qkv_part * qkv_own.astype(F32), axis=1) / norm_gain_attn
    grad_parts = [grad_attn]
    for _ in range(cols - 1):
        grad_parts.append(shift(grad_parts[-1], "col", 1))
    w_out_part = dot_tn(jnp.concatenate(grad_parts, axis=0), heads_block)

    grad_w_qkv = lax.psum_scatter(
        w_qkv_part.astype(BF16), ("dp", "row"), scatter_dimension=0, tiled=True
    ).astype(F32)
    grad_w_out = lax.psum_scatter(
        w_out_part.astype(BF16), ("dp", "row"), scatter_dimension=0, tiled=True
    ).astype(F32)
    axes = ("row", "col", "dp")
    grad_router_all = sum_everywhere(grad_router, axes)
    gains = sum_everywhere(jnp.stack([gain_attn_part, gain_moe_part]), axes)
    return (
        result,
        grad_hidden,
        gains[0],
        gains[1],
        grad_w_qkv,
        grad_w_out,
        grad_router_all,
        grad_w_in,
        grad_w_down,
    )


def solution(mesh):
    in_specs = (
        P(("dp", "row", "col"), None),
        P(),
        P(),
        P(("dp", "row"), "col"),
        P(("dp", "row"), "col"),
        P(),
        P(("row", "col"), None, None),
        P(("row", "col"), None, None),
        P(("dp", "row"), None),
        P(("dp", "row", "col"), None),
        P(("dp", "row", "col"), None),
    )
    out_specs = (
        P(("dp", "row", "col"), None),
        P(("dp", "row", "col"), None),
        P(),
        P(),
        P(("dp", "row"), "col"),
        P(("dp", "row"), "col"),
        P(),
        P(("row", "col"), None, None),
        P(("row", "col"), None, None),
    )
    return jax.shard_map(shards, mesh=mesh, in_specs=in_specs, out_specs=out_specs, check_vma=False)
```

```python
import functools
import math

import jax
import jax.numpy as jnp
from jax import lax
from jax.experimental import pallas as pl
from jax.experimental.pallas import tpu as pltpu
from jax.sharding import PartitionSpec as P

HD = 64
FFE = 512
TOP = 8
REP = 3
SEQ_MAX = 512

EPSILON = 1e-06
HIGHEST = lax.Precision.HIGHEST
MASKED_SCORE = -1e30
F32 = jnp.float32
BF16 = jnp.bfloat16


def dot_nn(left, right):
    return lax.dot_general(left, right, (((1,), (0,)), ((), ())), preferred_element_type=F32)


def dot_nt(left, right):
    return lax.dot_general(left, right, (((1,), (1,)), ((), ())), preferred_element_type=F32)


def dot_tn(left, right):
    return lax.dot_general(left, right, (((0,), (0,)), ((), ())), preferred_element_type=F32)


def hot_rows(srow, cap, tok):
    places = lax.broadcasted_iota(jnp.int32, (cap, tok), 0).astype(F32)
    return srow == places


def one_zero(mask):
    return jnp.where(mask, 1.0, 0.0).astype(BF16)


def front_body(
    cap, tile, tiles, group, sources,
    first_ref, ids_ref, *refs,
):
    x_refs = refs[:sources]
    (
        rt_ref, rs_ref, win_ref, wdn_ref, res_ref, rows_ref, gate_ref, slot_ref, offs_ref,
        buf, gate, run, arena, sems,
    ) = refs[sources:]
    step = pl.program_id(0)
    tok, feat = arena.shape[1:]
    experts = rs_ref.shape[0] // 3
    local = buf.shape[0]
    ff = wdn_ref.shape[1]
    first_work = sources // group

    def fetch(at):
        where = at % 2 * group
        return [
            pltpu.make_async_copy(x_refs[at * group + s], arena.at[where + s], sems.at[where + s])
            for s in range(group)
        ]

    @pl.when(step < first_work)
    def _gather():
        @pl.when(step == 0)
        def _():
            for e in range(local):
                run[e] = 0
            for copy in fetch(0) + fetch(1):
                copy.start()

        here = step % 2 * group
        for s in range(group):
            pltpu.make_async_copy(x_refs[0], arena.at[here + s], sems.at[here + s]).wait()

        ids = lax.broadcasted_iota(jnp.int32, (experts, tok), 0)
        before = one_zero(
            lax.broadcasted_iota(jnp.int32, (tok, tok), 0)
            < lax.broadcasted_iota(jnp.int32, (tok, tok), 1)
        )
        srows, grows, counts = [], [], []
        for s in range(group):
            thirds = dot_nt(rs_ref[...], arena[here + s])
            logits = (thirds[2 * experts :] + thirds[experts : 2 * experts]) + thirds[:experts]
            rt = rt_ref[ids_ref[0, step * group + s]]
            used = ids == rt[0:1]
            for k in range(1, rt.shape[0]):
                used = used | (ids == rt[k : k + 1])
            top = jnp.max(jnp.where(used, logits, MASKED_SCORE), axis=0, keepdims=True)
            terms = jnp.where(used, jnp.exp(logits - top), 0.0)
            gates = terms / jnp.sum(terms, axis=0, keepdims=True)
            used_f = jnp.where(used, 1.0, 0.0)
            rank = dot_nn(used_f.astype(BF16), before)
            for e in range(local):
                mine = ids == first_ref[0] + e
                grows.append(jnp.sum(jnp.where(mine, gates, 0.0), axis=0, keepdims=True))
                srow = jnp.sum(jnp.where(mine & used, rank + 1.0, 0.0), axis=0, keepdims=True) - 1.0
                srows.append(srow)
                counts.append(jnp.max(srow).astype(jnp.int32) + 1)
        offs = []
        ends = [run[e] for e in range(local)]
        for s in range(group):
            for e in range(local):
                offs.append(pl.multiple_of(ends[e], 16))
                offs_ref[e, step * group + s] = ends[e]
                ends[e] = ends[e] + ((counts[s * local + e] + 15) & -16)
        for e in range(local):
            run[e] = ends[e]
        for s in range(group):
            hots = [hot_rows(srows[s * local + e], cap, tok) for e in range(local)]
            picked = dot_nn(one_zero(jnp.concatenate(hots, axis=0)), arena[here + s]).astype(BF16)
            for e in range(local):
                at = pl.ds(offs[s * local + e], cap)
                slot_ref[e, pl.ds(step * group + s, 1), :] = srows[s * local + e]
                gcol = jnp.sum(
                    jnp.where(hots[e], grows[s * local + e], 0.0), axis=1, keepdims=True
                )
                gate[e, at, :] = jnp.broadcast_to(gcol, (cap, 128))
                buf[e, at, :] = picked[e * cap : (e + 1) * cap]

        for later in range(2, first_work):

            @pl.when(step + 2 == later)
            def _(later=later):
                for copy in fetch(later):
                    copy.start()

        @pl.when(step == first_work - 1)
        def _():
            for e in range(local):
                end = pl.multiple_of(run[e], 16)
                offs_ref[e, sources] = run[e]
                buf[e, pl.ds(end, tile), :] = jnp.zeros((tile, feat), BF16)
                gate[e, pl.ds(end, tile), :] = jnp.zeros((tile, 128), F32)

    work = step - first_work
    e = work // tiles
    j = work % tiles

    @pl.when((work >= 0) & (work < local * tiles))
    def _experts():
        @pl.when(j * tile < run[e])
        def _():
            at = pl.ds(pl.multiple_of(j * tile, tile), tile)
            rows = buf[e, at, :]
            g = gate[e, at, :]
            rows_ref[0] = rows
            gate_ref[0] = g
            a = dot_nn(rows, win_ref[0, :, :ff])
            b = dot_nn(rows, win_ref[0, :, ff:])
            act_g = (g[:, 0:1] * (a / (1.0 + jnp.exp(-a)) * b)).astype(BF16)
            buf[e, at, :] = dot_nn(act_g, wdn_ref[0]).astype(BF16)

    back = work - local * tiles

    @pl.when(back >= 0)
    def _scatter():
        for s in range(group):
            source = ids_ref[1, back * group + s]
            hots, terms = [], []
            for e in range(local):
                hots.append(hot_rows(slot_ref[e, pl.ds(source, 1), :], cap, tok))
                off = pl.multiple_of(offs_ref[e, source], 16)
                terms.append(buf[e, pl.ds(off, cap), :])
            total = dot_tn(
                one_zero(jnp.concatenate(hots, axis=0)), jnp.concatenate(terms, axis=0)
            )
            res_ref[s * tok : (s + 1) * tok, :] = total.astype(BF16)


def moe_front(first, ids, x_parts, rt_all, router_parts, w_in, w_down, cap, group):
    sources, top, tok = rt_all.shape
    feat = x_parts[0].shape[1]
    local, _, ff2 = w_in.shape
    ff = ff2 // 2
    most = sources * cap
    tile = min(256, most)
    tiles = most // tile
    room = most + max(tile, cap)
    steps = sources // group
    middle = local * tiles

    def exp3(i, f, ids):
        return (jnp.clip((i - steps) // tiles, 0, local - 1), 0, 0)

    def tile3(i, f, ids):
        at = jnp.clip(i - steps, 0, middle - 1)
        return (at // tiles, at % tiles, 0)

    return pl.pallas_call(
        functools.partial(front_body, cap, tile, tiles, group, sources),
        grid_spec=pltpu.PrefetchScalarGridSpec(
            num_scalar_prefetch=2,
            grid=(2 * steps + middle,),
            in_specs=[pl.BlockSpec(memory_space=pl.ANY)] * sources
            + [
                pl.BlockSpec(rt_all.shape, lambda i, f, ids: (0, 0, 0)),
                pl.BlockSpec(router_parts.shape, lambda i, f, ids: (0, 0)),
                pl.BlockSpec((1, feat, ff2), exp3),
                pl.BlockSpec((1, ff, feat), exp3),
            ],
            out_specs=[
                pl.BlockSpec(
                    (group * tok, feat), lambda i, f, ids: (jnp.maximum(i - steps - middle, 0), 0)
                ),
                pl.BlockSpec((1, tile, feat), tile3),
                pl.BlockSpec((1, tile, 128), tile3),
                pl.BlockSpec((local, sources, tok), lambda i, f, ids: (0, 0, 0)),
                pl.BlockSpec(memory_space=pltpu.SMEM),
            ],
            scratch_shapes=[
                pltpu.VMEM((local, room, feat), BF16),
                pltpu.VMEM((local, room, 128), F32),
                pltpu.SMEM((local,), jnp.int32),
                pltpu.VMEM((2 * group, tok, feat), BF16),
                pltpu.SemaphoreType.DMA((2 * group,)),
            ],
        ),
        out_shape=[
            jax.ShapeDtypeStruct((sources * tok, feat), BF16),
            jax.ShapeDtypeStruct((local, most, feat), BF16),
            jax.ShapeDtypeStruct((local, most, 128), F32),
            jax.ShapeDtypeStruct((local, sources, tok), F32),
            jax.ShapeDtypeStruct((local, sources + 1), jnp.int32),
        ],
        compiler_params=pltpu.CompilerParams(vmem_limit_bytes=56 * 1024 * 1024),
        cost_estimate=pl.CostEstimate(
            flops=2 * most * feat * ff * 3, bytes_accessed=10 * most * feat, transcendentals=0
        ),
        name="moe_front",
    )(first, ids, *x_parts, rt_all, router_parts, w_in, w_down)


def back_tile(rows, grads, g, win_ref, wdn_ref, acc_i, acc_d):
    ff = wdn_ref.shape[1]
    a = dot_nn(rows, win_ref[0, :, :ff])
    b = dot_nn(rows, win_ref[0, :, ff:])
    ga = dot_nt(grads, wdn_ref[0])
    sig = 1.0 / (1.0 + jnp.exp(-a))
    silu = a * sig
    act = silu * b
    gate_grad = jnp.sum(act * ga, axis=1, keepdims=True)
    gag = g * ga
    da = (gag * b * (sig * (1.0 + a * (1.0 - sig)))).astype(BF16)
    db = (gag * silu).astype(BF16)
    act_g = (g * act).astype(BF16)
    acc_d[...] += dot_tn(act_g, grads)
    acc_i[:, :ff] += dot_tn(rows, da)
    acc_i[:, ff:] += dot_tn(rows, db)
    pair = dot_nt(da, win_ref[0, :, :ff]) + dot_nt(db, win_ref[0, :, ff:])
    return pair.astype(BF16), gate_grad


def piece_shapes(feat, ff):
    return [(ff // 2, feat)] * 2 + [(feat // 4, 2 * ff)] * 4


def write_pieces(acc_i, acc_d, refs):
    downs = acc_d.shape[0] // 2
    ins = acc_i.shape[0] // 4
    for p in range(2):
        refs[p][...] = acc_d[p * downs : (p + 1) * downs, :].astype(BF16)
    for p in range(4):
        refs[2 + p][...] = acc_i[p * ins : (p + 1) * ins, :].astype(BF16)


def back_first_body(
    cap, tile, tiles, group,
    offs_ref, ids_ref, *refs,
):
    dy_refs = refs[:group]
    (slot_ref, rows_ref, gate_ref, win_ref, wdn_ref, pair_ref, gg_ref, other_ref, *piece_refs, buf, acc_i, acc_d) = refs[group:]
    step = pl.program_id(0)
    sources = slot_ref.shape[1]
    local = buf.shape[0]
    tok, feat = dy_refs[0].shape
    first_work = sources // group

    @pl.when(step < first_work)
    def _gather():
        for s in range(group):
            source = step * group + s
            hots = [hot_rows(slot_ref[e, pl.ds(source, 1), :], cap, tok) for e in range(local)]
            picked = dot_nn(
                one_zero(jnp.concatenate(hots, axis=0)), dy_refs[s][...]
            ).astype(BF16)
            for e in range(local):
                off = pl.multiple_of(offs_ref[e, source], 16)
                buf[e, pl.ds(off, cap), :] = picked[e * cap : (e + 1) * cap]

        @pl.when(step == first_work - 1)
        def _():
            for e in range(local):
                end = pl.multiple_of(offs_ref[e, sources], 16)
                buf[e, pl.ds(end, tile), :] = jnp.zeros((tile, feat), BF16)
            acc_i[...] = jnp.zeros_like(acc_i)
            acc_d[...] = jnp.zeros_like(acc_d)

    j = step - first_work

    @pl.when(j >= 0)
    def _experts():
        at = pl.ds(pl.multiple_of(j * tile, tile), tile)

        @pl.when(j * tile < offs_ref[1, sources])
        def _():
            other_ref[0] = buf[1, at, :]

        @pl.when(j * tile < offs_ref[0, sources])
        def _():
            pair, gate_grad = back_tile(
                rows_ref[0], buf[0, at, :], gate_ref[0, :, 0:1], win_ref, wdn_ref, acc_i, acc_d
            )
            pair_ref[...] = pair
            gg_ref[...] = jnp.broadcast_to(gate_grad, (tile, 128))

        @pl.when(j * tile >= offs_ref[0, sources])
        def _():
            pair_ref[...] = jnp.zeros_like(pair_ref)
            gg_ref[...] = jnp.zeros_like(gg_ref)

        @pl.when(j == tiles - 1)
        def _():
            write_pieces(acc_i, acc_d, piece_refs)


def used_tile(j, offs, e, sources, tile):
    return jnp.clip(j, 0, jnp.maximum((offs[e, sources] + (tile - 1)) // tile - 1, 0))


def moe_back_first(offs, ids, dy_all, slot, rows, gate, w_in, w_down, cap, group):
    local, sources, tok = slot.shape
    most, feat = rows.shape[1:]
    ff2 = w_in.shape[2]
    ff = ff2 // 2
    tile = min(256, most)
    tiles = most // tile
    room = most + max(tile, cap)
    steps = sources // group

    def in_tile(i, offs, ids):
        return (0, used_tile(i - steps, offs, 0, sources, tile), 0)

    def out_tile(i, offs, ids):
        return (jnp.maximum(i - steps, 0), 0)

    def other_tile(i, offs, ids):
        return (0, used_tile(i - steps, offs, 1, sources, tile), 0)

    def source(s):
        return lambda i, offs, ids: (ids[2, jnp.minimum(i, steps - 1) * group + s], 0)

    return pl.pallas_call(
        functools.partial(back_first_body, cap, tile, tiles, group),
        grid_spec=pltpu.PrefetchScalarGridSpec(
            num_scalar_prefetch=2,
            grid=(steps + tiles,),
            in_specs=[pl.BlockSpec((tok, feat), source(s)) for s in range(group)]
            + [
                pl.BlockSpec(slot.shape, lambda i, offs, ids: (0, 0, 0)),
                pl.BlockSpec((1, tile, feat), in_tile),
                pl.BlockSpec((1, tile, 128), in_tile),
                pl.BlockSpec((1, feat, ff2), lambda i, offs, ids: (0, 0, 0)),
                pl.BlockSpec((1, ff, feat), lambda i, offs, ids: (0, 0, 0)),
            ],
            out_specs=[
                pl.BlockSpec((tile, feat), out_tile),
                pl.BlockSpec((tile, 128), out_tile),
                pl.BlockSpec((1, tile, feat), other_tile),
                *[pl.BlockSpec(s, lambda i, offs, ids: (0, 0)) for s in piece_shapes(feat, ff)],
            ],
            scratch_shapes=[
                pltpu.VMEM((local, room, feat), BF16),
                pltpu.VMEM((feat, ff2), F32),
                pltpu.VMEM((ff, feat), F32),
            ],
        ),
        out_shape=[
            jax.ShapeDtypeStruct((most, feat), BF16),
            jax.ShapeDtypeStruct((most, 128), F32),
            jax.ShapeDtypeStruct((1, most, feat), BF16),
            *[jax.ShapeDtypeStruct(s, BF16) for s in piece_shapes(feat, ff)],
        ],
        compiler_params=pltpu.CompilerParams(vmem_limit_bytes=56 * 1024 * 1024),
        cost_estimate=pl.CostEstimate(
            flops=2 * most * feat * ff * 4, bytes_accessed=5 * dy_all.size * 2, transcendentals=0
        ),
        name="moe_back_first",
    )(offs, ids, *[dy_all] * group, slot, rows, gate, w_in, w_down)


def back_last_body(
    cap, tile, tiles, group,
    offs_ref, ids_ref, slot_ref, rows_ref, grads_ref, gate_ref, win_ref, wdn_ref, pair0_ref, gg0_ref,
    far_ref, near_ref, dg_ref, *rest,
):
    *piece_refs, buf, gg, acc_i, acc_d = rest
    step = pl.program_id(0)
    sources, tok = slot_ref.shape[1:]
    feat = far_ref.shape[1]

    @pl.when(step == 0)
    def _():
        acc_i[...] = jnp.zeros_like(acc_i)
        acc_d[...] = jnp.zeros_like(acc_d)

    @pl.when(step < tiles)
    def _experts():
        at = pl.ds(pl.multiple_of(step * tile, tile), tile)

        @pl.when(step * tile < offs_ref[1, sources])
        def _():
            pair, gate_grad = back_tile(
                rows_ref[0], grads_ref[0], gate_ref[0, :, 0:1], win_ref, wdn_ref, acc_i, acc_d
            )
            buf[at, :] = pair
            gg[at, :] = jnp.broadcast_to(gate_grad, (tile, 128))

        @pl.when(step * tile >= offs_ref[1, sources])
        def _():
            buf[at, :] = jnp.zeros((tile, feat), BF16)
            gg[at, :] = jnp.zeros((tile, 128), F32)

        @pl.when(step == tiles - 1)
        def _():
            write_pieces(acc_i, acc_d, piece_refs)

    back = step - tiles

    @pl.when(back >= 0)
    def _scatter():
        for s in range(group):
            source = lax.rem(back * group + s + sources // 2, sources)
            to = ids_ref[3, source]
            hots, terms = [], []
            for e, (pair, grads) in enumerate(((pair0_ref, gg0_ref), (buf, gg))):
                hot = hot_rows(slot_ref[e, pl.ds(source, 1), :], cap, tok)
                at = pl.ds(pl.multiple_of(offs_ref[e, source], 16), cap)
                hots.append(hot)
                terms.append(pair[at, :])
                dg_ref[to, e : e + 1, :] = jnp.sum(
                    jnp.where(hot, grads[at, 0:1], 0.0), axis=0, keepdims=True
                )
            dg_ref[to, 2:, :] = jnp.zeros((dg_ref.shape[1] - 2, tok), F32)
            total = dot_tn(
                one_zero(jnp.concatenate(hots, axis=0)), jnp.concatenate(terms, axis=0)
            )
            total = total.astype(BF16)

            @pl.when(back < sources // (2 * group))
            def _(total=total, s=s):
                far_ref[s * tok : (s + 1) * tok, :] = total

            @pl.when(back >= sources // (2 * group))
            def _(total=total, s=s):
                near_ref[s * tok : (s + 1) * tok, :] = total


def moe_back_last(offs, ids, slot, rows, grads, gate, w_in, w_down, pair0, gg0, cap, group):
    local, sources, tok = slot.shape
    most, feat = rows.shape[1:]
    ff2 = w_in.shape[2]
    ff = ff2 // 2
    tile = min(256, most)
    tiles = most // tile
    steps = sources // group

    def in_tile(i, offs, ids):
        return (1, used_tile(i, offs, 1, sources, tile), 0)

    def own_tile(i, offs, ids):
        return (0, used_tile(i, offs, 1, sources, tile), 0)

    def whole(i, offs, ids):
        return (0, 0)

    def far(i, offs, ids):
        return (jnp.clip(i - tiles, 0, steps // 2 - 1), 0)

    def near(i, offs, ids):
        return (jnp.clip(i - tiles - steps // 2, 0, steps // 2 - 1), 0)

    return pl.pallas_call(
        functools.partial(back_last_body, cap, tile, tiles, group),
        grid_spec=pltpu.PrefetchScalarGridSpec(
            num_scalar_prefetch=2,
            grid=(steps + tiles,),
            in_specs=[
                pl.BlockSpec(slot.shape, lambda i, offs, ids: (0, 0, 0)),
                pl.BlockSpec((1, tile, feat), in_tile),
                pl.BlockSpec((1, tile, feat), own_tile),
                pl.BlockSpec((1, tile, 128), in_tile),
                pl.BlockSpec((1, feat, ff2), lambda i, offs, ids: (1, 0, 0)),
                pl.BlockSpec((1, ff, feat), lambda i, offs, ids: (1, 0, 0)),
                pl.BlockSpec((most, feat), whole),
                pl.BlockSpec((most, 128), whole),
            ],
            out_specs=[
                pl.BlockSpec((group * tok, feat), far),
                pl.BlockSpec((group * tok, feat), near),
                pl.BlockSpec((sources, 8, tok), lambda i, offs, ids: (0, 0, 0)),
                *[pl.BlockSpec(s, whole) for s in piece_shapes(feat, ff)],
            ],
            scratch_shapes=[
                pltpu.VMEM((most, feat), BF16),
                pltpu.VMEM((most, 128), F32),
                pltpu.VMEM((feat, ff2), F32),
                pltpu.VMEM((ff, feat), F32),
            ],
        ),
        out_shape=[
            jax.ShapeDtypeStruct((sources // 2 * tok, feat), BF16),
            jax.ShapeDtypeStruct((sources // 2 * tok, feat), BF16),
            jax.ShapeDtypeStruct((sources, 8, tok), F32),
            *[jax.ShapeDtypeStruct(s, BF16) for s in piece_shapes(feat, ff)],
        ],
        compiler_params=pltpu.CompilerParams(vmem_limit_bytes=56 * 1024 * 1024),
        cost_estimate=pl.CostEstimate(
            flops=2 * most * feat * ff * 4, bytes_accessed=10 * most * feat, transcendentals=0
        ),
        name="moe_back_last",
    )(offs, ids, slot, rows, grads, gate, w_in, w_down, pair0, gg0)


def split_router(router):
    flat = router.T
    one = flat.astype(BF16)
    rest = flat - one.astype(F32)
    two = rest.astype(BF16)
    three = (rest - two.astype(F32)).astype(BF16)
    return jnp.concatenate([one, two, three], axis=0)


def add_body(pieces, *refs):
    step = pl.program_id(0)
    own, far, out_ref = refs[:pieces], refs[pieces : 2 * pieces], refs[-1]
    for p in range(pieces):

        @pl.when(step == p)
        def _(p=p):
            out_ref[0] = own[p][...].astype(F32) + far[p][...].astype(F32)


def add_pairs(own, far, index, local, held=None):
    pieces = len(own)
    rows, width = own[0].shape
    return pl.pallas_call(
        functools.partial(add_body, pieces),
        grid=(pieces,),
        in_specs=[pl.BlockSpec((rows, width), lambda i: (0, 0), pipeline_mode=pl.Buffered(1))]
        * (2 * pieces)
        + ([] if held is None else [pl.BlockSpec(memory_space=pl.ANY)]),
        out_specs=pl.BlockSpec((1, rows, width), lambda i: (index, i, 0)),
        out_shape=jax.ShapeDtypeStruct((local, pieces * rows, width), F32),
        input_output_aliases={} if held is None else {2 * pieces: 0},
        compiler_params=pltpu.CompilerParams(vmem_limit_bytes=40 * 1024 * 1024),
        cost_estimate=pl.CostEstimate(
            flops=pieces * rows * width, bytes_accessed=8 * pieces * rows * width, transcendentals=0
        ),
        name="add_pairs",
    )(*own, *far, *([] if held is None else [held]))


def lane_low(shape):
    return lax.broadcasted_iota(jnp.int32, shape, 1) < HD


def twist(tile_vals):
    width = tile_vals.shape[1]
    lane = lax.broadcasted_iota(jnp.int32, tile_vals.shape, 1)
    ahead = pltpu.roll(tile_vals, width - HD // 2, 1)
    behind = pltpu.roll(tile_vals, HD // 2, 1)
    return jnp.where(lane % HD < HD // 2, -ahead, behind)


def both_halves(tile_vals, low):
    kept = jnp.where(lane_low(tile_vals.shape) == low, tile_vals, 0.0)
    return kept + pltpu.roll(kept, HD, 1)


def head_places():
    per = REP + 2
    def at(index):
        return (index // 2, index % 2 == 0)
    groups = []
    for g in range(2):
        base = g * per
        groups.append(
            ([at(base + r) for r in range(REP)], at(base + REP), at(base + REP + 1))
        )
    return groups


def chunk_span(a, tok):
    reach = -(-(SEQ_MAX - 1) // tok)
    return max(0, a - reach) * tok, (a + 1) * tok


def mask_bias(start_row, a, tok):
    low, high = chunk_span(a, tok)
    shape = (high - low, tok)
    keys = lax.broadcasted_iota(jnp.int32, shape, 0) + low
    queries = lax.broadcasted_iota(jnp.int32, shape, 1) + a * tok
    allowed = (keys >= start_row) & (keys <= queries)
    return jnp.where(allowed, 0.0, MASKED_SCORE)


def attn_forward_body(
    chunks, here_ref, *refs,
):
    ins, (w_ref, cos_ref, sin_ref, start_ref, qkv_ref, kk_ref, vv_ref, lse_ref, heads_ref) = (
        refs[:chunks],
        refs[chunks:],
    )
    tok = ins[0].shape[0]
    here = here_ref[0]
    places = head_places()
    for k in range(chunks):
        a = lax.rem(here + (chunks - k), chunks)
        at = pl.ds(pl.multiple_of(a * tok, tok), tok)
        mixed = dot_nn(ins[k][...], w_ref[...])
        cos = cos_ref[at, :]
        sin = sin_ref[at, :]
        tiles = [mixed[:, 128 * i : 128 * (i + 1)] for i in range(mixed.shape[1] // 128)]
        turned = [t * cos + twist(t) * sin for t in tiles]
        for g, (queries, key, value) in enumerate(places):
            for r, (tile_at, low) in enumerate(queries):
                part = jnp.where(lane_low(tiles[0].shape) == low, turned[tile_at], 0.0)
                slot = 128 * (g * REP + r)
                qkv_ref[at, slot : slot + 128] = part.astype(BF16)
            kk_ref[at, 128 * g : 128 * (g + 1)] = both_halves(turned[key[0]], key[1]).astype(BF16)
            vv_ref[at, 128 * g : 128 * (g + 1)] = both_halves(tiles[value[0]], value[1]).astype(BF16)
    for a in range(chunks):
        low_key, high_key = chunk_span(a, tok)
        bias = mask_bias(start_ref[a : a + 1, :], a, tok)
        out = [None] * REP
        for g, (queries, _, _) in enumerate(places):
            keys = kk_ref[low_key:high_key, 128 * g : 128 * (g + 1)]
            vals = vv_ref[low_key:high_key, 128 * g : 128 * (g + 1)]
            for r in range(REP):
                head = g * REP + r
                q = qkv_ref[a * tok : (a + 1) * tok, 128 * head : 128 * (head + 1)]
                scores = dot_nt(keys, q) * HD ** (-0.5) + bias
                top = jnp.max(scores, axis=0, keepdims=True)
                terms = jnp.exp(scores - top)
                total = jnp.sum(terms, axis=0, keepdims=True)
                probs = (terms * (1.0 / total)).astype(BF16)
                lse_ref[head, a : a + 1, :] = top + jnp.log(total)
                mix = dot_tn(probs, vals)
                t = head // 2
                low = lane_low(mix.shape)
                out[t] = mix if head % 2 == 0 else jnp.where(low, out[t], mix)
        for t in range(REP):
            heads_ref[a * tok : (a + 1) * tok, 128 * t : 128 * (t + 1)] = out[t].astype(BF16)


def attn_forward(here, parts, w_cols, cos, sin, starts):
    chunks = len(parts)
    tok, feat = parts[0].shape
    total = chunks * tok
    cols = w_cols.shape[1]
    return pl.pallas_call(
        functools.partial(attn_forward_body, chunks),
        in_specs=[pl.BlockSpec(memory_space=pltpu.SMEM)]
        + [pl.BlockSpec(memory_space=pltpu.VMEM)] * (chunks + 4),
        out_specs=[pl.BlockSpec(memory_space=pltpu.VMEM)] * 5,
        out_shape=[
            jax.ShapeDtypeStruct((total, 128 * 2 * REP), BF16),
            jax.ShapeDtypeStruct((total, 256), BF16),
            jax.ShapeDtypeStruct((total, 256), BF16),
            jax.ShapeDtypeStruct((2 * REP, 8, tok), F32),
            jax.ShapeDtypeStruct((total, 2 * REP * HD), BF16),
        ],
        compiler_params=pltpu.CompilerParams(vmem_limit_bytes=48 * 1024 * 1024),
        cost_estimate=pl.CostEstimate(
            flops=2 * total * feat * cols * 4, bytes_accessed=8 * total * cols, transcendentals=0
        ),
        name="attn_forward",
    )(here, *parts, w_cols, cos, sin, starts)


def attn_backward_body(
    chunks, here_ref, grads_ref, q_ref, kk_ref, vv_ref, lse_ref, cos_ref, sin_ref, start_ref,
    out_ref, turned_ref, dk, dv, dq,
):
    tok = q_ref.shape[0] // chunks
    here = here_ref[0]
    dk[...] = jnp.zeros_like(dk)
    dv[...] = jnp.zeros_like(dv)
    for a in range(chunks):
        low_key, high_key = chunk_span(a, tok)
        bias = mask_bias(start_ref[a : a + 1, :], a, tok)
        for g in range(2):
            keys = kk_ref[low_key:high_key, 128 * g : 128 * (g + 1)]
            vals = vv_ref[low_key:high_key, 128 * g : 128 * (g + 1)]
            for r in range(REP):
                head = g * REP + r
                q = q_ref[a * tok : (a + 1) * tok, 128 * head : 128 * (head + 1)]
                t, is_low = head // 2, head % 2 == 0
                pair = grads_ref[a * tok : (a + 1) * tok, 128 * t : 128 * (t + 1)]
                grad = jnp.where(lane_low(pair.shape) == is_low, pair, jnp.zeros_like(pair))
                scores = dot_nt(keys, q) * HD ** (-0.5) + bias
                probs = jnp.exp(scores - lse_ref[head, a : a + 1, :])
                grad_probs = dot_nt(vals, grad)
                dv[low_key:high_key, 128 * g : 128 * (g + 1)] += dot_nn(probs.astype(BF16), grad)
                inner = jnp.sum(probs * grad_probs, axis=0, keepdims=True)
                grad_scores = (probs * (grad_probs - inner)).astype(BF16)
                dk[low_key:high_key, 128 * g : 128 * (g + 1)] += dot_nn(grad_scores, q)
                part = dot_tn(grad_scores, keys)
                here_at = slice(128 * t, 128 * (t + 1))
                rows = slice(a * tok, (a + 1) * tok)
                if is_low:
                    dq[rows, here_at] = part
                else:
                    dq[rows, here_at] = jnp.where(lane_low(part.shape), dq[rows, here_at], part)
    for a in range(chunks):
        rows = slice(a * tok, (a + 1) * tok)
        to = pl.ds(pl.multiple_of(lax.rem(here + (chunks - a), chunks) * tok, tok), tok)
        cos = cos_ref[rows, :]
        sin = sin_ref[rows, :]

        def back(vals):
            return (vals * cos - twist(vals) * sin) * HD ** (-0.5)

        def whole(vals):
            return vals + pltpu.roll(vals, HD, 1)

        low = lane_low((tok, 128))
        keys = [back(whole(dk[rows, 128 * g : 128 * (g + 1)])) for g in range(2)]
        vals = [whole(dv[rows, 128 * g : 128 * (g + 1)]) for g in range(2)]
        qs = [back(dq[rows, 128 * t : 128 * (t + 1)]) for t in range(REP)]
        tiles = [
            qs[0],
            jnp.where(low, qs[1], keys[0]),
            jnp.where(low, vals[0], qs[1]),
            qs[2],
            jnp.where(low, keys[1], vals[1]),
        ]
        for i, vals_of in enumerate(tiles):
            out_ref[rows, 128 * i : 128 * (i + 1)] = vals_of.astype(BF16)
            turned_ref[to, 128 * i : 128 * (i + 1)] = vals_of.astype(BF16)


def attn_backward(here, grads, q_rows, key_rows, value_rows, lse, cos, sin, starts, chunks):
    total = q_rows.shape[0]
    cols = 2 * (REP + 2) * HD
    return pl.pallas_call(
        functools.partial(attn_backward_body, chunks),
        in_specs=[pl.BlockSpec(memory_space=pltpu.SMEM)]
        + [pl.BlockSpec(memory_space=pltpu.VMEM)] * 8,
        out_specs=[pl.BlockSpec(memory_space=pltpu.VMEM)] * 2,
        out_shape=[jax.ShapeDtypeStruct((total, cols), BF16)] * 2,
        scratch_shapes=[
            pltpu.VMEM((total, 256), F32),
            pltpu.VMEM((total, 256), F32),
            pltpu.VMEM((total, 2 * REP * HD), F32),
        ],
        compiler_params=pltpu.CompilerParams(vmem_limit_bytes=48 * 1024 * 1024),
        cost_estimate=pl.CostEstimate(
            flops=12 * total * total * cols, bytes_accessed=8 * total * cols, transcendentals=0
        ),
        name="attn_backward",
    )(here, grads, q_rows, key_rows, value_rows, lse, cos, sin, starts)


def rope_rows(positions):
    freq_index = jnp.arange(HD // 2, dtype=F32)
    inverse = jnp.exp(freq_index * (-2.0 * math.log(10000.0) / HD))
    angles = positions.astype(F32)[:, None] * inverse[None, :]
    return jnp.tile(jnp.cos(angles), (1, 4)), jnp.tile(jnp.sin(angles), (1, 4))


def seq_layout(block_lengths, block_tok):
    seq_ends = jnp.cumsum(block_lengths)
    starts = seq_ends - block_lengths
    places = jnp.arange(block_tok, dtype=jnp.int32)
    segment = jnp.sum((places[:, None] >= seq_ends[None, :]).astype(jnp.int32), axis=1)
    owners = segment[:, None] == jnp.arange(block_lengths.shape[0], dtype=jnp.int32)[None, :]
    offset = jnp.sum(jnp.where(owners, starts[None, :], 0), axis=1)
    return places - offset, offset


def norm_apply(row_vals, gain_vec):
    scale_row = lax.rsqrt(jnp.mean(row_vals * row_vals, axis=1, keepdims=True) + EPSILON)
    return row_vals * scale_row * gain_vec


def norm_back(row_vals, gain_vec, grad):
    scale_row = lax.rsqrt(jnp.mean(row_vals * row_vals, axis=1, keepdims=True) + EPSILON)
    weighted = grad * gain_vec
    inner = jnp.mean(weighted * row_vals, axis=1, keepdims=True)
    return scale_row * weighted - row_vals * (scale_row * scale_row * scale_row * inner)


def shift(values, axis, by):
    size = lax.axis_size(axis)
    return lax.ppermute(values, axis, [(i, (i + by) % size) for i in range(size)])


def swap(values, axis, bit):
    size = lax.axis_size(axis)
    return lax.ppermute(values, axis, [(i, i ^ bit) for i in range(size)])


def plane_places(row, col):
    rows, cols = lax.axis_size("row"), lax.axis_size("col")
    index = jnp.arange(rows * cols, dtype=jnp.int32)
    core, side, back = index // (2 * cols), index // cols % 2, index % cols
    return row ^ (core + 2 * side), (col - back + cols) % cols


def gather_small_steps(row, col):
    rows = lax.axis_size("row")
    steps = []
    for axis in ("row", "col"):
        bit = 1
        while bit < lax.axis_size(axis):
            steps.append(
                lambda v, axis=axis, bit=bit: jnp.concatenate([v, swap(v, axis, bit)], axis=0)
            )
            bit *= 2
    from_row, from_col = plane_places(row, col)
    return steps, (from_row ^ row) + rows * (from_col ^ col)


def in_step(stages, *chains):
    values = [value for value, _ in chains]
    for stage in range(stages):
        for index, (_, steps) in enumerate(chains):
            mine = steps[stage : stage + 1] if stage + 1 < stages else steps[stage:]
            for step in mine:
                values[index] = step(values[index])
        values = list(lax.optimization_barrier(tuple(values)))
    return values


def ring_steps(by):
    return [lambda held: held + [shift(held[-1], "col", by)]] * (lax.axis_size("col") - 1)


def gather_plane(values, beside, steps):
    cols = lax.axis_size("col")
    line, across = [values], []
    for k in range(cols):
        side = swap(line[k], "row", 2)
        later = shift(line[k], "col", 1) if k + 1 < cols else None
        for step in steps[k : k + 1] if k + 1 < cols else steps[k:]:
            beside = step(beside)
        side, later, beside = lax.optimization_barrier((side, later, beside))
        line.append(later)
        across.append(side)
    own = line[:cols] + across
    return own + [swap(part, "row", 1) for part in own], beside


def after(values, *earlier):
    return lax.optimization_barrier((values, *earlier))[0]


def gather_rows_steps(row):
    dps = lax.axis_size("dp")
    dp = lax.axis_index("dp").astype(jnp.int32)
    places = []
    bit = 1
    while bit < dps:
        places.append(("dp", bit, dp // bit % 2, 0))
        bit *= 2
    places += [("row", 2, row // 2, 1), ("row", 1, row % 2, 2)]

    def send(values, axis, bit):
        return swap(values, axis, bit)

    def join(values, other, place, dim):
        return jnp.where(
            place == 0,
            jnp.concatenate([values, other], axis=dim),
            jnp.concatenate([other, values], axis=dim),
        )

    return [
        (functools.partial(send, axis=a, bit=b), functools.partial(join, place=p, dim=d))
        for a, b, p, d in places
    ]


def sum_rows_steps(row):
    dps = lax.axis_size("dp")
    dp = lax.axis_index("dp").astype(jnp.int32)
    places = [("row", 1, row % 2, 2), ("row", 2, row // 2, 1)]
    bit = dps // 2
    while bit:
        places.append(("dp", bit, dp // bit % 2, 0))
        bit //= 2

    def cut(values, place, dim):
        half = values.shape[dim] // 2
        return [
            lax.dynamic_slice_in_dim(values, at * half, half, dim) for at in (place, 1 - place)
        ]

    def add(halves, axis, bit):
        kept, given = halves
        return (kept.astype(F32) + swap(given, axis, bit).astype(F32)).astype(BF16)

    return [
        (functools.partial(cut, place=p, dim=d), functools.partial(add, axis=a, bit=b))
        for a, b, p, d in places
    ]


def sum_steps():
    steps = []
    for axis in ("row", "col", "dp"):
        bit = 1
        while bit < lax.axis_size(axis):
            steps.append(lambda v, axis=axis, bit=bit: v + swap(v, axis, bit))
            bit *= 2
    return steps


def shards(
    hidden_in,
    norm_gain_attn,
    norm_gain_moe,
    w_qkv,
    w_out,
    router,
    w_in,
    w_down,
    lengths,
    routes,
    out_grad,
):
    tok, feat = hidden_in.shape
    cols = lax.axis_size("col")
    rows = lax.axis_size("row")
    block_tok = tok * cols
    experts = router.shape[1]
    sources = rows * cols
    local = w_in.shape[0]
    cap = tok * TOP * 2 // experts
    head_cols = w_out.shape[1]
    group = 4
    plane = ("row", "col")
    col = lax.axis_index("col").astype(jnp.int32)
    row = lax.axis_index("row").astype(jnp.int32)
    here = col.reshape(1)
    first = ((row * cols + col) * local).reshape(1)
    rows_in = hidden_in.astype(F32)
    grad_out = out_grad.astype(F32)

    normed_attn = norm_apply(rows_in, norm_gain_attn).astype(BF16)
    row_steps = gather_rows_steps(row)
    small_steps, rt_ids = gather_small_steps(row, col)
    parts, out_line, qkv_own = in_step(
        cols - 1,
        ([normed_attn], ring_steps(1)),
        ([w_out], ring_steps(-1)),
        (w_qkv[None, None, None], [lambda v, s=s, j=j: j(v, s(v)) for s, j in row_steps]),
    )
    qkv_own = qkv_own.reshape(feat, -1)
    qkv_all = lax.all_gather(
        after(w_qkv, parts[2]), ("col", "dp", "row"), axis=0, tiled=True
    ).reshape(cols, feat, -1)
    out_line = jnp.concatenate(out_line, axis=1)
    out_line = jnp.concatenate([out_line, out_line], axis=1)
    out_line = lax.dynamic_slice_in_dim(
        out_line, (cols - col) % cols * head_cols, cols * head_cols, 1
    )[None, None, None]

    positions, seq_start = seq_layout(lengths[0], block_tok)
    cos, sin = rope_rows(positions)
    starts = jnp.pad(seq_start.reshape(cols, tok), ((0, -cols % 8), (0, 0)))
    q_rows, key_rows, value_rows, lse, heads_block = attn_forward(
        here, parts, qkv_own, cos, sin, starts
    )
    for send, join in row_steps[:-3]:
        out_line = join(out_line, send(out_line))
    (send_dp, join_dp), (send_side, join_side), (send_core, join_core) = row_steps[-3:]
    heads_block, other = lax.optimization_barrier((heads_block, send_dp(out_line)))
    out_line = join_dp(out_line, other)
    heads = lax.all_to_all(
        heads_block.reshape(cols, tok, head_cols), "col", split_axis=0, concat_axis=0, tiled=True
    )
    heads, other = lax.optimization_barrier((heads, send_side(out_line)))
    heads = jnp.concatenate([heads[k] for k in range(cols)], axis=1)
    out_line = join_side(out_line, other)
    out_full = join_core(out_line, send_core(out_line)).reshape(feat, -1)
    middle = rows_in + dot_nt(heads, out_full)
    normed_moe = norm_apply(middle, norm_gain_moe).astype(BF16)

    x_parts, rt_all = gather_plane(normed_moe, routes.T[None], small_steps)
    dy_all = lax.all_gather(after(out_grad, x_parts[cols - 2]), plane, axis=0, tiled=True)
    from_row, from_col = plane_places(row, col)
    whole_ids = from_row * cols + from_col
    index = jnp.arange(sources, dtype=jnp.int32)
    twist_row, back_col = index // cols ^ row, (col - index % cols + cols) % cols
    places = (twist_row % 2 * 2 + twist_row // 2) * cols + back_col
    ids = jnp.stack([rt_ids, places, whole_ids, whole_ids])

    res_part, rows_kept, gate, slot, offs = moe_front(
        first, ids, x_parts, rt_all, split_router(router), w_in, w_down, cap, group
    )
    res = lax.psum_scatter(res_part, plane, scatter_dimension=0, tiled=True)
    pair0, gg0, dy_kept, *own0 = moe_back_first(
        offs, ids, dy_all, slot, rows_kept, gate, w_in, w_down, cap, group
    )
    paired = lax.axis_size("dp") == 2
    pieces = len(own0)
    own, far = list(own0), []

    def exchange(count, *earlier):
        if not paired:
            return []
        at = len(far)
        sent = [swap(after(piece, *earlier), "dp", 1) for piece in own[at : at + count]]
        far.extend(sent)
        return sent

    def arrived(values, sent):
        if sent:
            values, kept = lax.optimization_barrier((values, sent))
            far[len(far) - len(sent) :] = kept
        return values

    sent = exchange(2, pair0)
    gn_far, gn_near, dg, *own1 = moe_back_last(
        offs, ids, slot, rows_kept, dy_kept, gate, w_in, w_down, pair0, gg0, cap, group
    )
    own += own1
    gn_far = arrived(gn_far, sent)

    from_far = swap(gn_far, "row", 1)
    sent = exchange(1, gn_far)
    from_far = arrived(from_far, sent)

    def near_terms(k, source):
        terms = []
        for index in (cols + k, k):
            at = slice(index * tok, (index + 1) * tok)
            terms.append((gn_near[at].astype(F32) + source[at].astype(F32)).astype(BF16))
        return terms

    gn, terms = None, near_terms(cols - 1, from_far)
    for k in range(cols - 1, -1, -1):
        side = swap(terms[0], "row", 2)
        sent = exchange(1, terms[0])
        total = terms[1].astype(F32)
        if gn is not None:
            total = total + shift(gn, "col", -1).astype(F32)
        terms = near_terms(k - 1, after(from_far, terms[0])) if k else None
        if k == cols - 1:
            normed_wide = normed_moe.astype(F32)
            logits = jnp.dot(
                normed_wide, router, precision=HIGHEST, preferred_element_type=F32
            )
            expert_ids = jnp.arange(experts, dtype=jnp.int32)
            used = jnp.any(routes[:, :, None] == expert_ids[None, None, :], axis=1)
            top = jnp.max(jnp.where(used, logits, MASKED_SCORE), axis=1, keepdims=True)
            exps = jnp.where(used, jnp.exp(logits - top), 0.0)
            gates = exps / jnp.sum(exps, axis=1, keepdims=True)
            dg_back = lax.all_to_all(
                after(dg, from_far), plane, split_axis=0, concat_axis=0, tiled=True
            )
            side, gates, dg_back = lax.optimization_barrier((side, gates, dg_back))
        if k == cols - 2:
            grad_gates = after(dg_back, gates)[:, :local].reshape(experts, tok).T
            grad_logits = gates * (
                grad_gates - jnp.sum(gates * grad_gates, axis=1, keepdims=True)
            )
            router_term = lax.dot_general(
                grad_logits,
                router,
                (((1,), (1,)), ((), ())),
                precision=HIGHEST,
                preferred_element_type=F32,
            )
            side, router_term, grad_logits = lax.optimization_barrier(
                (side, router_term, grad_logits)
            )
        if k == cols - 3:
            grad_router = lax.dot_general(
                grad_logits,
                normed_wide,
                (((0,), (0,)), ((), ())),
                precision=HIGHEST,
                preferred_element_type=F32,
            )
            side, grad_router = lax.optimization_barrier((side, grad_router))
        if k == 1:
            side, res = lax.optimization_barrier((side, res))
        total, side, terms = arrived(lax.optimization_barrier((total, side, terms)), sent)
        gn = total + side.astype(F32)
        if k:
            gn = gn.astype(BF16)

    grad_nm = gn + router_term
    grad_middle = grad_out + norm_back(middle, norm_gain_moe, grad_nm)
    grad_attn = grad_middle.astype(BF16)
    grad_heads = dot_nn(grad_attn, out_full).astype(BF16)

    sum_out, sum_all = sum_rows_steps(row), sum_steps()
    sent = exchange(1, gn)
    grads_block = lax.all_to_all(
        jnp.stack([grad_heads[:, k * head_cols : (k + 1) * head_cols] for k in range(cols)]),
        "col",
        split_axis=0,
        concat_axis=0,
        tiled=True,
    )
    w_out_sum = dot_tn(after(grad_attn, grad_heads), heads).astype(BF16)
    w_out_sum = sum_out[0][0](w_out_sum.reshape(-1, 2, 2, w_out.shape[0], feat))
    small = sum_all[1](sum_all[0](after(grad_router, grad_heads)))
    w_out_sum = sum_out[1][0](sum_out[0][1](w_out_sum))
    grads_block, w_out_sum, small = arrived(
        lax.optimization_barrier((grads_block, w_out_sum, small)), sent
    )

    sent = exchange(1, grads_block)
    w_out_sum = sum_out[1][1](w_out_sum)
    small = sum_all[3](sum_all[2](small))
    grad_mixed, turned_mixed = attn_backward(
        here, grads_block.reshape(cols * tok, head_cols), q_rows, key_rows, value_rows, lse,
        cos, sin, starts, cols,
    )
    grad_mixed, turned_mixed, w_out_sum, small = arrived(
        lax.optimization_barrier((grad_mixed, turned_mixed, w_out_sum, small)), sent
    )

    mixed_back = lax.all_to_all(
        grad_mixed.reshape(cols, tok, -1), "col", split_axis=0, concat_axis=0, tiled=True
    )
    sent = exchange(1, grad_mixed)
    w_qkv_part = dot_tn(jnp.concatenate(parts, axis=0), turned_mixed)
    w_qkv_part = arrived(w_qkv_part, sent)
    sent = exchange(1, w_qkv_part)
    for step in sum_out[2:]:
        w_out_sum = step[1](step[0](after(w_out_sum, w_qkv_part)))
    gain_attn_part = jnp.sum(w_qkv_part * qkv_own.astype(F32), axis=1) / norm_gain_attn
    w_qkv_sum = sum_out[0][0](w_qkv_part.astype(BF16).reshape(-1, 2, 2, *w_qkv.shape))
    w_qkv_sum = sum_out[0][1](w_qkv_sum)
    middle_scale = lax.rsqrt(jnp.mean(middle * middle, axis=1, keepdims=True) + EPSILON)
    gain_moe_part = jnp.sum(
        after(grad_nm, w_qkv_part) * middle * middle_scale, axis=0, keepdims=True
    )
    gains = sum_all[1](sum_all[0](jnp.concatenate([gain_moe_part, gain_attn_part[None]], axis=0)))
    if paired:
        grad_w_in = add_pairs(own[2:pieces], after(far[2:pieces], w_qkv_part), 0, local)
        grad_w_down = add_pairs(own[:2], after(far[:2], w_qkv_part), 0, local)
    else:
        grad_w_in = lax.psum(
            jnp.stack([jnp.concatenate(own[e * pieces + 2 : (e + 1) * pieces]) for e in range(local)]), "dp"
        ).astype(F32)
        grad_w_down = lax.psum(
            jnp.stack([jnp.concatenate(own[e * pieces : e * pieces + 2]) for e in range(local)]), "dp"
        ).astype(F32)
    mixed_back, w_qkv_sum, w_out_sum, gains, grad_w_in, grad_w_down = arrived(
        lax.optimization_barrier(
            (mixed_back, w_qkv_sum, w_out_sum, gains, grad_w_in, grad_w_down)
        ),
        sent,
    )

    sent = exchange(1, mixed_back)
    w_qkv_sum = sum_out[1][1](sum_out[1][0](w_qkv_sum))
    gains = sum_all[3](sum_all[2](gains))
    lines = lax.all_to_all(
        jnp.stack([w_out_sum[..., k * head_cols : (k + 1) * head_cols] for k in range(cols)]),
        "col",
        split_axis=0,
        concat_axis=0,
        tiled=True,
    )
    grad_na = sum(dot_nt(mixed_back[k], qkv_all[k]) for k in range(cols))
    grad_hidden = grad_middle + norm_back(rows_in, norm_gain_attn, grad_na)
    result = middle + res.astype(F32)
    grad_hidden, w_qkv_sum, gains, lines, result = arrived(
        lax.optimization_barrier((grad_hidden, w_qkv_sum, gains, lines, result)), sent
    )
    small = jnp.concatenate([small, gains], axis=0)
    for step in sum_all[4:]:
        small = step(small)
    for step in sum_out[2:]:
        w_qkv_sum = step[1](step[0](w_qkv_sum))
    if paired:
        grad_w_in = add_pairs(own[pieces + 2 :], far[pieces + 2 :], 1, local, grad_w_in)
        grad_w_down = add_pairs(
            own[pieces : pieces + 2], far[pieces : pieces + 2], 1, local, grad_w_down
        )
    grad_w_qkv = w_qkv_sum.reshape(w_qkv.shape).astype(F32)
    grad_w_out = jnp.sum(lines.astype(F32), axis=0).reshape(w_out.shape)
    return (
        result,
        grad_hidden,
        small[experts + 1],
        small[experts],
        grad_w_qkv,
        grad_w_out,
        small[:experts].T,
        grad_w_in,
        grad_w_down,
    )


def solution(mesh):
    in_specs = (
        P(("dp", "row", "col"), None),
        P(),
        P(),
        P(("dp", "row"), "col"),
        P(("dp", "row"), "col"),
        P(),
        P(("row", "col"), None, None),
        P(("row", "col"), None, None),
        P(("dp", "row"), None),
        P(("dp", "row", "col"), None),
        P(("dp", "row", "col"), None),
    )
    out_specs = (
        P(("dp", "row", "col"), None),
        P(("dp", "row", "col"), None),
        P(),
        P(),
        P(("dp", "row"), "col"),
        P(("dp", "row"), "col"),
        P(),
        P(("row", "col"), None, None),
        P(("row", "col"), None, None),
    )
    return jax.shard_map(shards, mesh=mesh, in_specs=in_specs, out_specs=out_specs, check_vma=False)
```

```python
import functools
import math

import jax
import jax.numpy as jnp
from jax import lax
from jax.experimental import pallas as pl
from jax.experimental.pallas import tpu as pltpu
from jax.sharding import PartitionSpec as P

HD = 64
FFE = 512
TOP = 8
REP = 3
SEQ_MAX = 512

EPSILON = 1e-06
HIGHEST = lax.Precision.HIGHEST
MASKED_SCORE = -1e30
F32 = jnp.float32
BF16 = jnp.bfloat16


def dot_nn(left, right):
    return lax.dot_general(left, right, (((1,), (0,)), ((), ())), preferred_element_type=F32)


def dot_nt(left, right):
    return lax.dot_general(left, right, (((1,), (1,)), ((), ())), preferred_element_type=F32)


def dot_tn(left, right):
    return lax.dot_general(left, right, (((0,), (0,)), ((), ())), preferred_element_type=F32)


def lane_low(shape):
    return lax.broadcasted_iota(jnp.int32, shape, 1) < HD


def twist(tile_vals):
    width = tile_vals.shape[1]
    lane = lax.broadcasted_iota(jnp.int32, tile_vals.shape, 1)
    ahead = pltpu.roll(tile_vals, width - HD // 2, 1)
    behind = pltpu.roll(tile_vals, HD // 2, 1)
    return jnp.where(lane % HD < HD // 2, -ahead, behind)


def both_halves(tile_vals, low):
    kept = jnp.where(lane_low(tile_vals.shape) == low, tile_vals, 0.0)
    return kept + pltpu.roll(kept, HD, 1)


def head_places():
    per = REP + 2
    def at(index):
        return (index // 2, index % 2 == 0)
    groups = []
    for g in range(2):
        base = g * per
        groups.append(
            ([at(base + r) for r in range(REP)], at(base + REP), at(base + REP + 1))
        )
    return groups


def chunk_span(a, tok):
    reach = -(-(SEQ_MAX - 1) // tok)
    return max(0, a - reach) * tok, (a + 1) * tok


def mask_bias(start_row, a, tok):
    low, high = chunk_span(a, tok)
    shape = (high - low, tok)
    keys = lax.broadcasted_iota(jnp.int32, shape, 0) + low
    queries = lax.broadcasted_iota(jnp.int32, shape, 1) + a * tok
    allowed = (keys >= start_row) & (keys <= queries)
    return jnp.where(allowed, 0.0, MASKED_SCORE)


def attn_forward_body(
    chunks, here_ref, *refs,
):
    ins, (w_ref, cos_ref, sin_ref, start_ref, qkv_ref, kk_ref, vv_ref, lse_ref, heads_ref) = (
        refs[:chunks],
        refs[chunks:],
    )
    tok = ins[0].shape[0]
    here = here_ref[0]
    places = head_places()
    for k in range(chunks):
        a = lax.rem(here + (chunks - k), chunks)
        at = pl.ds(pl.multiple_of(a * tok, tok), tok)
        mixed = dot_nn(ins[k][...], w_ref[...])
        cos = cos_ref[at, :]
        sin = sin_ref[at, :]
        tiles = [mixed[:, 128 * i : 128 * (i + 1)] for i in range(mixed.shape[1] // 128)]
        turned = [t * cos + twist(t) * sin for t in tiles]
        for g, (queries, key, value) in enumerate(places):
            for r, (tile_at, low) in enumerate(queries):
                part = jnp.where(lane_low(tiles[0].shape) == low, turned[tile_at], 0.0)
                slot = 128 * (g * REP + r)
                qkv_ref[at, slot : slot + 128] = part.astype(BF16)
            kk_ref[at, 128 * g : 128 * (g + 1)] = both_halves(turned[key[0]], key[1]).astype(BF16)
            vv_ref[at, 128 * g : 128 * (g + 1)] = both_halves(tiles[value[0]], value[1]).astype(BF16)
    for a in range(chunks):
        low_key, high_key = chunk_span(a, tok)
        bias = mask_bias(start_ref[a : a + 1, :], a, tok)
        out = [None] * REP
        for g, (queries, _, _) in enumerate(places):
            keys = kk_ref[low_key:high_key, 128 * g : 128 * (g + 1)]
            vals = vv_ref[low_key:high_key, 128 * g : 128 * (g + 1)]
            for r in range(REP):
                head = g * REP + r
                q = qkv_ref[a * tok : (a + 1) * tok, 128 * head : 128 * (head + 1)]
                scores = dot_nt(keys, q) * HD ** (-0.5) + bias
                top = jnp.max(scores, axis=0, keepdims=True)
                terms = jnp.exp(scores - top)
                total = jnp.sum(terms, axis=0, keepdims=True)
                probs = (terms * (1.0 / total)).astype(BF16)
                lse_ref[head, a : a + 1, :] = top + jnp.log(total)
                mix = dot_tn(probs, vals)
                t = head // 2
                low = lane_low(mix.shape)
                out[t] = mix if head % 2 == 0 else jnp.where(low, out[t], mix)
        for t in range(REP):
            heads_ref[a * tok : (a + 1) * tok, 128 * t : 128 * (t + 1)] = out[t].astype(BF16)


def whole_block(values):
    zeros = (0,) * len(values.shape)
    return pl.BlockSpec(values.shape, lambda i: zeros, pipeline_mode=pl.Buffered(1))


def attn_forward(here, parts, w_cols, cos, sin, starts):
    chunks = len(parts)
    tok, feat = parts[0].shape
    total = chunks * tok
    cols = w_cols.shape[1]
    return pl.pallas_call(
        functools.partial(attn_forward_body, chunks),
        grid=(1,),
        in_specs=[pl.BlockSpec(memory_space=pltpu.SMEM)]
        + [whole_block(v) for v in (*parts, w_cols, cos, sin, starts)],
        out_specs=[
            whole_block(jax.ShapeDtypeStruct(s, F32))
            for s in (
                (total, 128 * 2 * REP), (total, 256), (total, 256), (2 * REP, 8, tok),
                (total, 2 * REP * HD),
            )
        ],
        out_shape=[
            jax.ShapeDtypeStruct((total, 128 * 2 * REP), BF16),
            jax.ShapeDtypeStruct((total, 256), BF16),
            jax.ShapeDtypeStruct((total, 256), BF16),
            jax.ShapeDtypeStruct((2 * REP, 8, tok), F32),
            jax.ShapeDtypeStruct((total, 2 * REP * HD), BF16),
        ],
        compiler_params=pltpu.CompilerParams(vmem_limit_bytes=60 * 1024 * 1024),
        cost_estimate=pl.CostEstimate(
            flops=2 * total * feat * cols * 4, bytes_accessed=8 * total * cols, transcendentals=0
        ),
        name="attn_forward",
    )(here, *parts, w_cols, cos, sin, starts)


def attn_backward_body(
    chunks, here_ref, grads_ref, q_ref, kk_ref, vv_ref, lse_ref, cos_ref, sin_ref, start_ref,
    turned_ref, dk, dv, dq,
):
    tok = q_ref.shape[0] // chunks
    here = here_ref[0]
    dk[...] = jnp.zeros_like(dk)
    dv[...] = jnp.zeros_like(dv)
    for a in range(chunks):
        low_key, high_key = chunk_span(a, tok)
        bias = mask_bias(start_ref[a : a + 1, :], a, tok)
        for g in range(2):
            keys = kk_ref[low_key:high_key, 128 * g : 128 * (g + 1)]
            vals = vv_ref[low_key:high_key, 128 * g : 128 * (g + 1)]
            for r in range(REP):
                head = g * REP + r
                q = q_ref[a * tok : (a + 1) * tok, 128 * head : 128 * (head + 1)]
                t, is_low = head // 2, head % 2 == 0
                pair = grads_ref[a * tok : (a + 1) * tok, 128 * t : 128 * (t + 1)]
                grad = jnp.where(lane_low(pair.shape) == is_low, pair, jnp.zeros_like(pair))
                scores = dot_nt(keys, q) * HD ** (-0.5) + bias
                probs = jnp.exp(scores - lse_ref[head, a : a + 1, :])
                grad_probs = dot_nt(vals, grad)
                dv[low_key:high_key, 128 * g : 128 * (g + 1)] += dot_nn(probs.astype(BF16), grad)
                inner = jnp.sum(probs * grad_probs, axis=0, keepdims=True)
                grad_scores = (probs * (grad_probs - inner)).astype(BF16)
                dk[low_key:high_key, 128 * g : 128 * (g + 1)] += dot_nn(grad_scores, q)
                part = dot_tn(grad_scores, keys)
                here_at = slice(128 * t, 128 * (t + 1))
                rows = slice(a * tok, (a + 1) * tok)
                if is_low:
                    dq[rows, here_at] = part
                else:
                    dq[rows, here_at] = jnp.where(lane_low(part.shape), dq[rows, here_at], part)
    for a in range(chunks):
        rows = slice(a * tok, (a + 1) * tok)
        to = pl.ds(pl.multiple_of(lax.rem(here + (chunks - a), chunks) * tok, tok), tok)
        cos = cos_ref[rows, :]
        sin = sin_ref[rows, :]

        def back(vals):
            return (vals * cos - twist(vals) * sin) * HD ** (-0.5)

        def whole(vals):
            return vals + pltpu.roll(vals, HD, 1)

        low = lane_low((tok, 128))
        keys = [back(whole(dk[rows, 128 * g : 128 * (g + 1)])) for g in range(2)]
        vals = [whole(dv[rows, 128 * g : 128 * (g + 1)]) for g in range(2)]
        qs = [back(dq[rows, 128 * t : 128 * (t + 1)]) for t in range(REP)]
        tiles = [
            qs[0],
            jnp.where(low, qs[1], keys[0]),
            jnp.where(low, vals[0], qs[1]),
            qs[2],
            jnp.where(low, keys[1], vals[1]),
        ]
        for i, vals_of in enumerate(tiles):
            turned_ref[to, 128 * i : 128 * (i + 1)] = vals_of.astype(BF16)


def attn_backward(here, grads, q_rows, key_rows, value_rows, lse, cos, sin, starts, chunks):
    total = q_rows.shape[0]
    cols = 2 * (REP + 2) * HD
    return pl.pallas_call(
        functools.partial(attn_backward_body, chunks),
        grid=(1,),
        in_specs=[pl.BlockSpec(memory_space=pltpu.SMEM)]
        + [
            whole_block(v)
            for v in (grads, q_rows, key_rows, value_rows, lse, cos, sin, starts)
        ],
        out_specs=whole_block(jax.ShapeDtypeStruct((total, cols), BF16)),
        out_shape=jax.ShapeDtypeStruct((total, cols), BF16),
        scratch_shapes=[
            pltpu.VMEM((total, 256), F32),
            pltpu.VMEM((total, 256), F32),
            pltpu.VMEM((total, 2 * REP * HD), F32),
        ],
        compiler_params=pltpu.CompilerParams(vmem_limit_bytes=60 * 1024 * 1024),
        cost_estimate=beside_transfers(),
        name="attn_backward",
    )(here, grads, q_rows, key_rows, value_rows, lse, cos, sin, starts)


def hot_rows(srow, cap, tok):
    places = lax.broadcasted_iota(jnp.int32, (cap, tok), 0).astype(F32)
    return srow == places


def one_zero(mask):
    return jnp.where(mask, 1.0, 0.0).astype(BF16)


def front_body(
    cap, tile, tiles, group, sources,
    first_ref, ids_ref, offs_ref, *refs,
):
    x_refs = refs[:sources]
    (
        rt_ref, rs_ref, win_ref, wdn_ref, res_ref, rows_ref, ab_ref, gate_ref, slot_ref,
        buf, gate, arena, sems,
    ) = refs[sources:]
    step = pl.program_id(0)
    tok, feat = arena.shape[1:]
    experts = rs_ref.shape[1] // 4
    local = buf.shape[0]
    ff = wdn_ref.shape[1]
    first_work = sources // group

    def fetch(at):
        where = at % 2 * group
        return [
            pltpu.make_async_copy(x_refs[at * group + s], arena.at[where + s], sems.at[where + s])
            for s in range(group)
        ]

    @pl.when(step < first_work)
    def _gather():
        @pl.when(step == 0)
        def _():
            for copy in fetch(0) + fetch(1):
                copy.start()

        here = step % 2 * group
        for s in range(group):
            pltpu.make_async_copy(x_refs[0], arena.at[here + s], sems.at[here + s]).wait()

        ids = lax.broadcasted_iota(jnp.int32, (experts, tok), 0)
        before = one_zero(
            lax.broadcasted_iota(jnp.int32, (tok, tok), 0)
            < lax.broadcasted_iota(jnp.int32, (tok, tok), 1)
        )
        srows, grows = [], []
        for s in range(group):
            thirds = dot_nn(arena[here + s], rs_ref[...]).T
            logits = (
                thirds[2 * experts : 3 * experts] + thirds[experts : 2 * experts]
            ) + thirds[:experts]
            rt = rt_ref[ids_ref[0, step * group + s]]
            used = ids == rt[0:1]
            for k in range(1, rt.shape[0]):
                used = used | (ids == rt[k : k + 1])
            top = jnp.max(jnp.where(used, logits, MASKED_SCORE), axis=0, keepdims=True)
            terms = jnp.where(used, jnp.exp(logits - top), 0.0)
            gates = terms / jnp.sum(terms, axis=0, keepdims=True)
            used_f = jnp.where(used, 1.0, 0.0)
            rank = dot_nn(used_f.astype(BF16), before)
            for e in range(local):
                mine = ids == first_ref[0] + e
                grows.append(jnp.sum(jnp.where(mine, gates, 0.0), axis=0, keepdims=True))
                srow = jnp.sum(jnp.where(mine & used, rank + 1.0, 0.0), axis=0, keepdims=True) - 1.0
                srows.append(srow)
        for s in range(group):
            hots = [hot_rows(srows[s * local + e], cap, tok) for e in range(local)]
            picked = dot_nn(one_zero(jnp.concatenate(hots, axis=0)), arena[here + s]).astype(BF16)
            for e in range(local):
                at = pl.ds(pl.multiple_of(offs_ref[e, step * group + s], 16), cap)
                slot_ref[e, pl.ds(step * group + s, 1), :] = srows[s * local + e]
                gcol = jnp.sum(
                    jnp.where(hots[e], grows[s * local + e], 0.0), axis=1, keepdims=True
                )
                gate[e, at, :] = jnp.broadcast_to(gcol, (cap, 128))
                buf[e, at, :] = picked[e * cap : (e + 1) * cap]

        for later in range(2, first_work):

            @pl.when(step + 2 == later)
            def _(later=later):
                for copy in fetch(later):
                    copy.start()

        @pl.when(step == first_work - 1)
        def _():
            for e in range(local):
                end = pl.multiple_of(offs_ref[e, sources], 16)
                buf[e, pl.ds(end, tile), :] = jnp.zeros((tile, feat), BF16)
                gate[e, pl.ds(end, tile), :] = jnp.zeros((tile, 128), F32)

    work = step - first_work
    e = work // tiles
    j = work % tiles

    @pl.when((work >= 0) & (work < local * tiles))
    def _experts():
        @pl.when(j * tile < offs_ref[e, sources])
        def _():
            at = pl.ds(pl.multiple_of(j * tile, tile), tile)
            rows = buf[e, at, :]
            g = gate[e, at, :]
            rows_ref[0] = rows
            gate_ref[0] = g
            a = dot_nn(rows, win_ref[0, :, :ff])
            b = dot_nn(rows, win_ref[0, :, ff:])
            ab_ref[0, :, :ff] = a
            ab_ref[0, :, ff:] = b
            act_g = (g[:, 0:1] * (a / (1.0 + jnp.exp(-a)) * b)).astype(BF16)
            buf[e, at, :] = dot_nn(act_g, wdn_ref[0]).astype(BF16)

    back = work - local * tiles

    @pl.when(back >= 0)
    def _scatter():
        for s in range(group):
            source = ids_ref[1, back * group + s]
            hots, terms = [], []
            for e in range(local):
                hots.append(hot_rows(slot_ref[e, pl.ds(source, 1), :], cap, tok))
                off = pl.multiple_of(offs_ref[e, source], 16)
                terms.append(buf[e, pl.ds(off, cap), :])
            total = dot_tn(
                one_zero(jnp.concatenate(hots, axis=0)), jnp.concatenate(terms, axis=0)
            )
            res_ref[s * tok : (s + 1) * tok, :] = total.astype(BF16)


def moe_front(first, ids, offs, x_parts, rt_all, router_parts, w_in, w_down, cap, group):
    sources, top, tok = rt_all.shape
    feat = x_parts[0].shape[1]
    local, _, ff2 = w_in.shape
    ff = ff2 // 2
    most = sources * cap
    tile = min(256, most)
    tiles = most // tile
    room = most + max(tile, cap)
    steps = sources // group
    middle = local * tiles

    def exp3(i, f, ids, offs):
        return (jnp.clip((i - steps) // tiles, 0, local - 1), 0, 0)

    def tile3(i, f, ids, offs):
        at = jnp.clip(i - steps, 0, middle - 1)
        return (at // tiles, at % tiles, 0)

    return pl.pallas_call(
        functools.partial(front_body, cap, tile, tiles, group, sources),
        grid_spec=pltpu.PrefetchScalarGridSpec(
            num_scalar_prefetch=3,
            grid=(2 * steps + middle,),
            in_specs=[pl.BlockSpec(memory_space=pl.ANY)] * sources
            + [
                pl.BlockSpec(rt_all.shape, lambda i, f, ids, offs: (0, 0, 0)),
                pl.BlockSpec(router_parts.shape, lambda i, f, ids, offs: (0, 0)),
                pl.BlockSpec((1, feat, ff2), exp3),
                pl.BlockSpec((1, ff, feat), exp3),
            ],
            out_specs=[
                pl.BlockSpec(
                    (group * tok, feat), lambda i, f, ids, offs: (jnp.maximum(i - steps - middle, 0), 0)
                ),
                pl.BlockSpec((1, tile, feat), tile3),
                pl.BlockSpec((1, tile, ff2), tile3),
                pl.BlockSpec((1, tile, 128), tile3),
                pl.BlockSpec((local, sources, tok), lambda i, f, ids, offs: (0, 0, 0)),
            ],
            scratch_shapes=[
                pltpu.VMEM((local, room, feat), BF16),
                pltpu.VMEM((local, room, 128), F32),
                pltpu.VMEM((2 * group, tok, feat), BF16),
                pltpu.SemaphoreType.DMA((2 * group,)),
            ],
        ),
        out_shape=[
            jax.ShapeDtypeStruct((sources * tok, feat), BF16),
            jax.ShapeDtypeStruct((local, most, feat), BF16),
            jax.ShapeDtypeStruct((local, most, ff2), F32),
            jax.ShapeDtypeStruct((local, most, 128), F32),
            jax.ShapeDtypeStruct((local, sources, tok), F32),
        ],
        compiler_params=pltpu.CompilerParams(vmem_limit_bytes=56 * 1024 * 1024),
        cost_estimate=pl.CostEstimate(
            flops=2 * most * feat * ff * 3, bytes_accessed=10 * most * feat, transcendentals=0
        ),
        name="moe_front",
    )(first, ids, offs, *x_parts, rt_all, router_parts, w_in, w_down)


def back_tile(rows, ab_ref, grads, g, win_ref, wdn_ref, acc_i, acc_d):
    ff = wdn_ref.shape[1]
    a = ab_ref[0, :, :ff]
    b = ab_ref[0, :, ff:]
    ga = dot_nt(grads, wdn_ref[0])
    sig = 1.0 / (1.0 + jnp.exp(-a))
    silu = a * sig
    act = silu * b
    gate_grad = jnp.sum(act * ga, axis=1, keepdims=True)
    gag = g * ga
    da = (gag * b * (sig * (1.0 + a * (1.0 - sig)))).astype(BF16)
    db = (gag * silu).astype(BF16)
    act_g = (g * act).astype(BF16)
    acc_d[...] += dot_tn(act_g, grads)
    acc_i[:, :ff] += dot_tn(rows, da)
    acc_i[:, ff:] += dot_tn(rows, db)
    pair = dot_nt(da, win_ref[0, :, :ff]) + dot_nt(db, win_ref[0, :, ff:])
    return pair.astype(BF16), gate_grad


def piece_shapes(feat, ff, first):
    down, rows = [ff // 2, ff // 2], [feat // 3] * 3
    if first:
        down, rows = [ff], [feat // 4, feat // 3, feat // 12 * 5]
    return [(n, feat) for n in down], [(n, 2 * ff) for n in rows]


def write_pieces(acc_i, acc_d, refs):
    at = 0
    for ref in refs:
        acc = acc_d if ref.shape[1] == acc_d.shape[1] else acc_i
        ref[...] = acc[at : at + ref.shape[0], :].astype(BF16)
        at = (at + ref.shape[0]) % acc.shape[0]


def back_first_body(
    cap, tile, tiles, group,
    offs_ref, ids_ref, *refs,
):
    dy_refs = refs[:group]
    (slot_ref, rows_ref, ab_ref, gate_ref, win_ref, wdn_ref, pair_ref, gg_ref, other_ref, *piece_refs, buf, acc_i, acc_d) = refs[group:]
    step = pl.program_id(0)
    sources = slot_ref.shape[1]
    local = buf.shape[0]
    tok, feat = dy_refs[0].shape
    first_work = sources // group

    @pl.when(step < first_work)
    def _gather():
        for s in range(group):
            source = step * group + s
            hots = [hot_rows(slot_ref[e, pl.ds(source, 1), :], cap, tok) for e in range(local)]
            picked = dot_nn(
                one_zero(jnp.concatenate(hots, axis=0)), dy_refs[s][...]
            ).astype(BF16)
            for e in range(local):
                off = pl.multiple_of(offs_ref[e, source], 16)
                buf[e, pl.ds(off, cap), :] = picked[e * cap : (e + 1) * cap]

        @pl.when(step == first_work - 1)
        def _():
            for e in range(local):
                end = pl.multiple_of(offs_ref[e, sources], 16)
                buf[e, pl.ds(end, tile), :] = jnp.zeros((tile, feat), BF16)
            acc_i[...] = jnp.zeros_like(acc_i)
            acc_d[...] = jnp.zeros_like(acc_d)

    j = step - first_work

    @pl.when(j >= 0)
    def _experts():
        at = pl.ds(pl.multiple_of(j * tile, tile), tile)

        @pl.when(j * tile < offs_ref[1, sources])
        def _():
            other_ref[0] = buf[1, at, :]

        @pl.when(j * tile < offs_ref[0, sources])
        def _():
            pair, gate_grad = back_tile(
                rows_ref[0], ab_ref, buf[0, at, :], gate_ref[0, :, 0:1], win_ref, wdn_ref, acc_i, acc_d
            )
            pair_ref[...] = pair
            gg_ref[...] = jnp.broadcast_to(gate_grad, (tile, 128))

        @pl.when(j * tile >= offs_ref[0, sources])
        def _():
            pair_ref[...] = jnp.zeros_like(pair_ref)
            gg_ref[...] = jnp.zeros_like(gg_ref)

        @pl.when(j == tiles - 1)
        def _():
            write_pieces(acc_i, acc_d, piece_refs)


def used_tile(j, offs, e, sources, tile):
    return jnp.clip(j, 0, jnp.maximum((offs[e, sources] + (tile - 1)) // tile - 1, 0))


def moe_back_first(offs, ids, dy_all, slot, rows, ab, gate, w_in, w_down, cap, group):
    local, sources, tok = slot.shape
    most, feat = rows.shape[1:]
    ff2 = w_in.shape[2]
    ff = ff2 // 2
    tile = min(256, most)
    tiles = most // tile
    room = most + max(tile, cap)
    steps = sources // group

    def in_tile(i, offs, ids):
        return (0, used_tile(i - steps, offs, 0, sources, tile), 0)

    def out_tile(i, offs, ids):
        return (jnp.maximum(i - steps, 0), 0)

    def other_tile(i, offs, ids):
        return (0, used_tile(i - steps, offs, 1, sources, tile), 0)

    def source(s):
        return lambda i, offs, ids: (ids[2, jnp.minimum(i, steps - 1) * group + s], 0)

    return pl.pallas_call(
        functools.partial(back_first_body, cap, tile, tiles, group),
        grid_spec=pltpu.PrefetchScalarGridSpec(
            num_scalar_prefetch=2,
            grid=(steps + tiles,),
            in_specs=[pl.BlockSpec((tok, feat), source(s)) for s in range(group)]
            + [
                pl.BlockSpec(slot.shape, lambda i, offs, ids: (0, 0, 0)),
                pl.BlockSpec((1, tile, feat), in_tile),
                pl.BlockSpec((1, tile, ff2), in_tile),
                pl.BlockSpec((1, tile, 128), in_tile),
                pl.BlockSpec((1, feat, ff2), lambda i, offs, ids: (0, 0, 0)),
                pl.BlockSpec((1, ff, feat), lambda i, offs, ids: (0, 0, 0)),
            ],
            out_specs=[
                pl.BlockSpec((tile, feat), out_tile),
                pl.BlockSpec((tile, 128), out_tile),
                pl.BlockSpec((1, tile, feat), other_tile),
                *[pl.BlockSpec(s, lambda i, offs, ids: (0, 0)) for s in sum(piece_shapes(feat, ff, True), [])],
            ],
            scratch_shapes=[
                pltpu.VMEM((local, room, feat), BF16),
                pltpu.VMEM((feat, ff2), F32),
                pltpu.VMEM((ff, feat), F32),
            ],
        ),
        out_shape=[
            jax.ShapeDtypeStruct((most, feat), BF16),
            jax.ShapeDtypeStruct((most, 128), F32),
            jax.ShapeDtypeStruct((1, most, feat), BF16),
            *[jax.ShapeDtypeStruct(s, BF16) for s in sum(piece_shapes(feat, ff, True), [])],
        ],
        compiler_params=pltpu.CompilerParams(vmem_limit_bytes=56 * 1024 * 1024),
        cost_estimate=pl.CostEstimate(
            flops=2 * most * feat * ff * 4, bytes_accessed=5 * dy_all.size * 2, transcendentals=0
        ),
        name="moe_back_first",
    )(offs, ids, *[dy_all] * group, slot, rows, ab, gate, w_in, w_down)


def back_last_body(
    cap, tile, tiles, group,
    offs_ref, ids_ref, slot_ref, rows_ref, ab_ref, grads_ref, gate_ref, win_ref, wdn_ref, pair0_any, gg0_any,
    far_ref, near_ref, dg_ref, *rest,
):
    *piece_refs, buf, gg, acc_i, acc_d, pair0_ref, gg0_ref, stage_d, stage_i, sems = rest
    step = pl.program_id(0)
    sources, tok = slot_ref.shape[1:]
    feat = far_ref.shape[1]

    def held_copies():
        return [
            pltpu.make_async_copy(pair0_any, pair0_ref, sems.at[0]),
            pltpu.make_async_copy(gg0_any, gg0_ref, sems.at[1]),
        ]

    def piece_copies():
        copies, at = [], 0
        for ref in piece_refs:
            stage = stage_d if ref.shape[1] == stage_d.shape[1] else stage_i
            copies.append(
                pltpu.make_async_copy(
                    stage.at[pl.ds(at, ref.shape[0]), :], ref, sems.at[2 + len(copies)]
                )
            )
            at = (at + ref.shape[0]) % stage.shape[0]
        return copies

    @pl.when(step == 0)
    def _():
        for copy in held_copies():
            copy.start()
        acc_i[...] = jnp.zeros_like(acc_i)
        acc_d[...] = jnp.zeros_like(acc_d)

    @pl.when(step < tiles)
    def _experts():
        at = pl.ds(pl.multiple_of(step * tile, tile), tile)

        @pl.when(step * tile < offs_ref[1, sources])
        def _():
            pair, gate_grad = back_tile(
                rows_ref[0], ab_ref, grads_ref[0], gate_ref[0, :, 0:1], win_ref, wdn_ref, acc_i, acc_d
            )
            buf[at, :] = pair
            gg[at, :] = jnp.broadcast_to(gate_grad, (tile, 128))

        @pl.when(step * tile >= offs_ref[1, sources])
        def _():
            buf[at, :] = jnp.zeros((tile, feat), BF16)
            gg[at, :] = jnp.zeros((tile, 128), F32)

        @pl.when(step == tiles - 1)
        def _():
            stage_d[...] = acc_d[...].astype(BF16)
            stage_i[...] = acc_i[...].astype(BF16)
            for copy in piece_copies():
                copy.start()
            for copy in held_copies():
                copy.wait()

    back = step - tiles

    @pl.when(back >= 0)
    def _scatter():
        for s in range(group):
            source = lax.rem(back * group + s + sources // 2, sources)
            to = ids_ref[3, source]
            hots, terms = [], []
            for e, (pair, grads) in enumerate(((pair0_ref, gg0_ref), (buf, gg))):
                hot = hot_rows(slot_ref[e, pl.ds(source, 1), :], cap, tok)
                at = pl.ds(pl.multiple_of(offs_ref[e, source], 16), cap)
                hots.append(hot)
                terms.append(pair[at, :])
                dg_ref[to, e : e + 1, :] = jnp.sum(
                    jnp.where(hot, grads[at, 0:1], 0.0), axis=0, keepdims=True
                )
            dg_ref[to, 2:, :] = jnp.zeros((dg_ref.shape[1] - 2, tok), F32)
            total = dot_tn(
                one_zero(jnp.concatenate(hots, axis=0)), jnp.concatenate(terms, axis=0)
            )
            total = total.astype(BF16)

            @pl.when(back < sources // (2 * group))
            def _(total=total, s=s):
                far_ref[s * tok : (s + 1) * tok, :] = total

            @pl.when(back >= sources // (2 * group))
            def _(total=total, s=s):
                near_ref[s * tok : (s + 1) * tok, :] = total

        @pl.when(step == pl.num_programs(0) - 1)
        def _():
            for copy in piece_copies():
                copy.wait()


def moe_back_last(offs, ids, slot, rows, ab, grads, gate, w_in, w_down, pair0, gg0, cap, group):
    local, sources, tok = slot.shape
    most, feat = rows.shape[1:]
    ff2 = w_in.shape[2]
    ff = ff2 // 2
    tile = min(256, most)
    tiles = most // tile
    steps = sources // group

    def in_tile(i, offs, ids):
        return (1, used_tile(i, offs, 1, sources, tile), 0)

    def own_tile(i, offs, ids):
        return (0, used_tile(i, offs, 1, sources, tile), 0)

    def whole(i, offs, ids):
        return (0, 0)

    def far(i, offs, ids):
        return (jnp.clip(i - tiles, 0, steps // 2 - 1), 0)

    def near(i, offs, ids):
        return (jnp.clip(i - tiles - steps // 2, 0, steps // 2 - 1), 0)

    return pl.pallas_call(
        functools.partial(back_last_body, cap, tile, tiles, group),
        grid_spec=pltpu.PrefetchScalarGridSpec(
            num_scalar_prefetch=2,
            grid=(steps + tiles,),
            in_specs=[
                pl.BlockSpec(slot.shape, lambda i, offs, ids: (0, 0, 0)),
                pl.BlockSpec((1, tile, feat), in_tile),
                pl.BlockSpec((1, tile, ff2), in_tile),
                pl.BlockSpec((1, tile, feat), own_tile),
                pl.BlockSpec((1, tile, 128), in_tile),
                pl.BlockSpec((1, feat, ff2), lambda i, offs, ids: (1, 0, 0)),
                pl.BlockSpec((1, ff, feat), lambda i, offs, ids: (1, 0, 0)),
                pl.BlockSpec(memory_space=pl.ANY),
                pl.BlockSpec(memory_space=pl.ANY),
            ],
            out_specs=[
                pl.BlockSpec((group * tok, feat), far),
                pl.BlockSpec((group * tok, feat), near),
                pl.BlockSpec((sources, 8, tok), lambda i, offs, ids: (0, 0, 0)),
                *[pl.BlockSpec(memory_space=pl.ANY)] * len(sum(piece_shapes(feat, ff, False), [])),
            ],
            scratch_shapes=[
                pltpu.VMEM((most, feat), BF16),
                pltpu.VMEM((most, 128), F32),
                pltpu.VMEM((feat, ff2), F32),
                pltpu.VMEM((ff, feat), F32),
                pltpu.VMEM((most, feat), BF16),
                pltpu.VMEM((most, 128), F32),
                pltpu.VMEM((ff, feat), BF16),
                pltpu.VMEM((feat, ff2), BF16),
                pltpu.SemaphoreType.DMA((2 + len(sum(piece_shapes(feat, ff, False), [])),)),
            ],
        ),
        out_shape=[
            jax.ShapeDtypeStruct((sources // 2 * tok, feat), BF16),
            jax.ShapeDtypeStruct((sources // 2 * tok, feat), BF16),
            jax.ShapeDtypeStruct((sources, 8, tok), F32),
            *[jax.ShapeDtypeStruct(s, BF16) for s in sum(piece_shapes(feat, ff, False), [])],
        ],
        compiler_params=pltpu.CompilerParams(vmem_limit_bytes=56 * 1024 * 1024),
        cost_estimate=pl.CostEstimate(
            flops=2 * most * feat * ff * 4, bytes_accessed=10 * most * feat, transcendentals=0
        ),
        name="moe_back_last",
    )(offs, ids, slot, rows, ab, grads, gate, w_in, w_down, pair0, gg0)


def split_router(router):
    one = router.astype(BF16)
    rest = router - one.astype(F32)
    two = rest.astype(BF16)
    three = (rest - two.astype(F32)).astype(BF16)
    return jnp.concatenate([one, two, three, jnp.zeros_like(one)], axis=1)


def add_body(starts, *refs):
    step = pl.program_id(0)
    pieces = len(starts) - 1
    own, far, out_ref = refs[:pieces], refs[pieces : 2 * pieces], refs[-1]
    for p in range(pieces):

        @pl.when((step >= starts[p]) & (step < starts[p + 1]))
        def _(p=p):
            out_ref[0] = own[p][...].astype(F32) + far[p][...].astype(F32)


def add_pairs(own, far, index, local, held=None):
    block = math.gcd(*[piece.shape[0] for piece in own])
    width = own[0].shape[1]
    starts = [0]
    for piece in own:
        starts.append(starts[-1] + piece.shape[0] // block)

    def piece(p):
        return lambda i: (jnp.clip(i - starts[p], 0, starts[p + 1] - starts[p] - 1), 0)

    return pl.pallas_call(
        functools.partial(add_body, starts),
        grid=(starts[-1],),
        in_specs=[pl.BlockSpec((block, width), piece(p)) for p in range(len(own))] * 2
        + ([] if held is None else [pl.BlockSpec(memory_space=pl.ANY)]),
        out_specs=pl.BlockSpec((1, block, width), lambda i: (index, i, 0)),
        out_shape=jax.ShapeDtypeStruct((local, starts[-1] * block, width), F32),
        input_output_aliases={} if held is None else {2 * len(own): 0},
        compiler_params=pltpu.CompilerParams(vmem_limit_bytes=40 * 1024 * 1024),
        cost_estimate=beside_transfers(),
        name="add_pairs",
    )(*own, *far, *([] if held is None else [held]))


def mid_back_body(
    gn_ref, term_ref, mid_ref, dy_ref, gain_ref, out_ref,
    grad_ref, low_ref, gain_grad_ref, block_ref,
):
    @pl.when(pl.program_id(0) == 0)
    def _():
        mid = mid_ref[...]
        scale = lax.rsqrt(jnp.mean(mid * mid, axis=1, keepdims=True) + EPSILON)
        grad = gn_ref[...] + term_ref[...]
        gain_grad_ref[...] = jnp.sum(grad * mid * scale, axis=0, keepdims=True)
        weighted = grad * gain_ref[...]
        inner = jnp.mean(weighted * mid, axis=1, keepdims=True)
        total = dy_ref[...].astype(F32) + scale * weighted - mid * (scale * scale * scale * inner)
        grad_ref[...] = total
        low_ref[...] = total.astype(BF16)

    block_ref[0] = dot_nn(low_ref[...], out_ref[0]).astype(BF16)


def mid_back(gn, router_term, middle, out_grad, gain, out_all):
    tok, feat = middle.shape
    groups, _, width = out_all.shape
    args = (gn, router_term, middle, out_grad, gain[None])
    outs = [
        jax.ShapeDtypeStruct((tok, feat), F32),
        jax.ShapeDtypeStruct((tok, feat), BF16),
        jax.ShapeDtypeStruct((1, feat), F32),
        jax.ShapeDtypeStruct((groups, tok, width), BF16),
    ]
    return pl.pallas_call(
        mid_back_body,
        grid=(groups,),
        in_specs=[whole_block(v) for v in args]
        + [pl.BlockSpec((1, feat, width), lambda i: (i, 0, 0))],
        out_specs=[whole_block(v) for v in outs[:-1]]
        + [pl.BlockSpec((1, tok, width), lambda i: (i, 0, 0))],
        out_shape=outs,
        compiler_params=pltpu.CompilerParams(vmem_limit_bytes=60 * 1024 * 1024),
        cost_estimate=pl.CostEstimate(
            flops=2 * tok * feat * feat, bytes_accessed=4 * feat * feat, transcendentals=0
        ),
        name="mid_back",
    )(*args, out_all)


def beside_transfers():
    return pl.CostEstimate(flops=12_000_000_000, bytes_accessed=1 << 20, transcendentals=0)


def near_terms_body(near_a, far_a, near_b, far_b, out_a, out_b):
    out_a[...] = (near_a[...].astype(F32) + far_a[...].astype(F32)).astype(BF16)
    out_b[...] = (near_b[...].astype(F32) + far_b[...].astype(F32)).astype(BF16)


def near_terms(near, far, first, second, tok):
    feat = near.shape[1]

    def block(index):
        return pl.BlockSpec((tok, feat), lambda i: (index, 0), pipeline_mode=pl.Buffered(1))

    return pl.pallas_call(
        near_terms_body,
        grid=(1,),
        in_specs=[block(first), block(first), block(second), block(second)],
        out_specs=[block(0), block(0)],
        out_shape=[jax.ShapeDtypeStruct((tok, feat), BF16)] * 2,
        compiler_params=pltpu.CompilerParams(vmem_limit_bytes=60 * 1024 * 1024),
        cost_estimate=beside_transfers(),
        name="near_terms",
    )(near, far, near, far)


def put_rows(part, first, core, kept_ref, given_ref):
    chunk = kept_ref.shape[1]
    for n in range(part.shape[0] // chunk):
        rows = part[n * chunk : (n + 1) * chunk]
        b = first + n

        @pl.when(core == b % 2)
        def _(rows=rows, b=b):
            kept_ref[b // 2] = rows

        @pl.when(core != b % 2)
        def _(rows=rows, b=b):
            given_ref[b // 2] = rows


def w_out_body(core_ref, low_ref, heads_ref, kept_ref, given_ref):
    step = low_ref.shape[1] // 4
    for c in range(4):
        part = dot_tn(low_ref[:, c * step : (c + 1) * step], heads_ref[...]).astype(BF16)
        put_rows(part, c * step // kept_ref.shape[1], core_ref[0], kept_ref, given_ref)


def w_out_part(core, low, heads, chunk):
    feat, width = low.shape[1], heads.shape[1]
    out = jax.ShapeDtypeStruct((feat // chunk // 2, chunk, width), BF16)
    return pl.pallas_call(
        w_out_body,
        grid=(1,),
        in_specs=[pl.BlockSpec(memory_space=pltpu.SMEM), whole_block(low), whole_block(heads)],
        out_specs=[whole_block(out)] * 2,
        out_shape=[out] * 2,
        compiler_params=pltpu.CompilerParams(vmem_limit_bytes=60 * 1024 * 1024),
        cost_estimate=beside_transfers(),
        name="w_out_part",
    )(core, low, heads)


def w_qkv_body(core_ref, rows_ref, mixed_ref, w_ref, gain_ref, kept_ref, given_ref, sum_ref):
    feat = rows_ref.shape[1]
    width = mixed_ref.shape[1]
    step = feat // 4
    ones = jnp.ones((8, width), F32)
    for c in range(4):
        at = slice(c * step, (c + 1) * step)
        part = dot_tn(rows_ref[:, at], mixed_ref[...])
        put_rows(
            part.astype(BF16), c * step // kept_ref.shape[1], core_ref[0], kept_ref, given_ref
        )
        sums = lax.dot_general(
            ones,
            part * w_ref[at, :].astype(F32),
            (((1,), (1,)), ((), ())),
            precision=HIGHEST,
            preferred_element_type=F32,
        )
        sum_ref[:, at] = sums[0:1] / gain_ref[:, at]


def w_qkv_part(core, rows, mixed, w_own, gain, chunk):
    feat, width = rows.shape[1], mixed.shape[1]
    out = jax.ShapeDtypeStruct((feat // chunk // 2, chunk, width), BF16)
    sums = jax.ShapeDtypeStruct((1, feat), F32)
    args = (rows, mixed, w_own, gain[None])
    return pl.pallas_call(
        w_qkv_body,
        grid=(1,),
        in_specs=[pl.BlockSpec(memory_space=pltpu.SMEM)] + [whole_block(v) for v in args],
        out_specs=[whole_block(out), whole_block(out), whole_block(sums)],
        out_shape=[out, out, sums],
        compiler_params=pltpu.CompilerParams(vmem_limit_bytes=60 * 1024 * 1024),
        cost_estimate=beside_transfers(),
        name="w_qkv_part",
    )(core, *args)


def row_places(first, local, rt_all, rt_ids):
    sources = rt_all.shape[0]
    mine = first[0] + jnp.arange(local, dtype=jnp.int32)
    named = rt_all[:, None, :, :] == mine[None, :, None, None]
    counts = jnp.sum(named.astype(jnp.int32), axis=(2, 3))
    order = rt_ids[:, None] == jnp.arange(sources, dtype=jnp.int32)[None, :]
    counts = jnp.sum(jnp.where(order[:, :, None], counts[None], 0), axis=1)
    rounded = (counts + 15) // 16 * 16
    before = (
        jnp.arange(sources, dtype=jnp.int32)[None, :]
        < jnp.arange(sources + 1, dtype=jnp.int32)[:, None]
    )
    return jnp.sum(jnp.where(before[:, :, None], rounded[None], 0), axis=1).T


def rope_rows(positions):
    freq_index = jnp.arange(HD // 2, dtype=F32)
    inverse = jnp.exp(freq_index * (-2.0 * math.log(10000.0) / HD))
    angles = positions.astype(F32)[:, None] * jnp.tile(inverse, 4)[None, :]
    return jnp.cos(angles), jnp.sin(angles)


def seq_layout(block_lengths, block_tok):
    seq_ends = jnp.cumsum(block_lengths)
    starts = seq_ends - block_lengths
    places = jnp.arange(block_tok, dtype=jnp.int32)
    segment = jnp.sum((places[:, None] >= seq_ends[None, :]).astype(jnp.int32), axis=1)
    owners = segment[:, None] == jnp.arange(block_lengths.shape[0], dtype=jnp.int32)[None, :]
    offset = jnp.sum(jnp.where(owners, starts[None, :], 0), axis=1)
    return places - offset, offset


def norm_apply(row_vals, gain_vec):
    scale_row = lax.rsqrt(jnp.mean(row_vals * row_vals, axis=1, keepdims=True) + EPSILON)
    return row_vals * scale_row * gain_vec


def norm_back(row_vals, gain_vec, grad):
    scale_row = lax.rsqrt(jnp.mean(row_vals * row_vals, axis=1, keepdims=True) + EPSILON)
    weighted = grad * gain_vec
    inner = jnp.mean(weighted * row_vals, axis=1, keepdims=True)
    return scale_row * weighted - row_vals * (scale_row * scale_row * scale_row * inner)


def shift(values, axis, by):
    size = lax.axis_size(axis)
    return lax.ppermute(values, axis, [(i, (i + by) % size) for i in range(size)])


def swap(values, axis, bit):
    size = lax.axis_size(axis)
    return lax.ppermute(values, axis, [(i, i ^ bit) for i in range(size)])


def plane_places(row, col):
    rows, cols = lax.axis_size("row"), lax.axis_size("col")
    index = jnp.arange(rows * cols, dtype=jnp.int32)
    core, side, back = index // (2 * cols), index // cols % 2, index % cols
    return row ^ (core + 2 * side), (col - back + cols) % cols


def gather_small_steps(row, col):
    rows = lax.axis_size("row")
    def over(values, axis, bits):
        for bit in bits:
            values = jnp.concatenate([values, swap(values, axis, bit)], axis=0)
        return values

    steps = [
        functools.partial(over, axis=axis, bits=bits)
        for axis, bits in (("row", (1, 2)), ("col", (1,)), ("col", (2,)))
    ]
    from_row, from_col = plane_places(row, col)
    return steps, (from_row ^ row) + rows * (from_col ^ col)


def in_step(stages, *chains):
    values = [value for value, _ in chains]
    for stage in range(stages):
        for index, (_, steps) in enumerate(chains):
            mine = steps[stage : stage + 1] if stage + 1 < stages else steps[stage:]
            for step in mine:
                values[index] = step(values[index])
        values = list(lax.optimization_barrier(tuple(values)))
    return values


def ring_steps(by):
    return [lambda held: held + [shift(held[-1], "col", by)]] * (lax.axis_size("col") - 1)


def gather_plane(values):
    cols = lax.axis_size("col")
    line, across = [values], []
    for k in range(cols):
        side = swap(line[k], "row", 2)
        later = shift(line[k], "col", 1) if k + 1 < cols else None
        side, later = lax.optimization_barrier((side, later))
        line.append(later)
        across.append(side)
    own = line[:cols] + across
    return own + [swap(part, "row", 1) for part in own]


def after(values, *earlier):
    return lax.optimization_barrier((values, *earlier))[0]


def sum_rows_steps(row):
    dps = lax.axis_size("dp")
    dp = lax.axis_index("dp").astype(jnp.int32)
    places = [("row", 1, row % 2, 2), ("row", 2, row // 2, 1)]
    bit = dps // 2
    while bit:
        places.append(("dp", bit, dp // bit % 2, 0))
        bit //= 2

    def cut(values, place, dim):
        half = values.shape[dim] // 2
        return [
            lax.dynamic_slice_in_dim(values, at * half, half, dim) for at in (place, 1 - place)
        ]

    def add(halves, axis, bit):
        kept, given = halves
        return (kept.astype(F32) + swap(given, axis, bit).astype(F32)).astype(BF16)

    return [
        (functools.partial(cut, place=p, dim=d), functools.partial(add, axis=a, bit=b))
        for a, b, p, d in places
    ]


def row_halves(row):
    def halve(values, bit, place, dim):
        kept, given = [
            lax.dynamic_slice_in_dim(values, at, 1, dim) for at in (place, 1 - place)
        ]
        return kept + swap(given, "row", bit)

    def spread(values, bit, place, dim):
        other = swap(values, "row", bit)
        return jnp.where(
            place == 0,
            jnp.concatenate([values, other], axis=dim),
            jnp.concatenate([other, values], axis=dim),
        )

    places = [(1, row % 2, 2), (2, row // 2, 1)]
    return (
        [functools.partial(halve, bit=b, place=p, dim=d) for b, p, d in places],
        [functools.partial(spread, bit=b, place=p, dim=d) for b, p, d in places[::-1]],
    )


def sum_steps():
    steps = []
    for axis in ("row", "col", "dp"):
        bit = 1
        while bit < lax.axis_size(axis):
            steps.append(lambda v, axis=axis, bit=bit: v + swap(v, axis, bit))
            bit *= 2
    return steps


def shards(
    hidden_in,
    norm_gain_attn,
    norm_gain_moe,
    w_qkv,
    w_out,
    router,
    w_in,
    w_down,
    lengths,
    routes,
    out_grad,
):
    tok, feat = hidden_in.shape
    cols = lax.axis_size("col")
    rows = lax.axis_size("row")
    block_tok = tok * cols
    experts = router.shape[1]
    sources = rows * cols
    local = w_in.shape[0]
    cap = tok * TOP * 2 // experts
    head_cols = w_out.shape[1]
    group = 4
    plane = ("row", "col")
    col = lax.axis_index("col").astype(jnp.int32)
    row = lax.axis_index("row").astype(jnp.int32)
    here = col.reshape(1)
    first = ((row * cols + col) * local).reshape(1)
    rows_in = hidden_in.astype(F32)
    grad_out = out_grad.astype(F32)

    normed_attn = norm_apply(rows_in, norm_gain_attn).astype(BF16)
    qkv_own = lax.all_gather(w_qkv, ("dp", "row"), axis=0, tiled=True)
    out_all = lax.all_gather(w_out, ("col", "dp", "row"), axis=0, tiled=True).reshape(
        cols, feat, head_cols
    )
    positions, seq_start = seq_layout(lengths[0], block_tok)
    cos, sin = rope_rows(positions)
    starts = jnp.pad(seq_start.reshape(cols, tok), ((0, -cols % 8), (0, 0)))
    small_steps, rt_ids = gather_small_steps(row, col)
    tables = (cos, sin, starts, split_router(router))
    parts, rt_all, tables = in_step(
        cols - 1, ([normed_attn], ring_steps(1)), (routes.T[None], small_steps), (tables, [])
    )
    cos, sin, starts, router_parts = tables

    q_rows, key_rows, value_rows, lse, heads_block = attn_forward(
        here, parts, qkv_own, cos, sin, starts
    )
    heads = lax.all_to_all(
        heads_block.reshape(cols, tok, head_cols), "col", split_axis=0, concat_axis=0, tiled=True
    )
    middle = rows_in + jnp.einsum(
        "ctj,cdj->td", heads, out_all, preferred_element_type=F32
    )
    normed_moe = norm_apply(middle, norm_gain_moe).astype(BF16)
    heads = jnp.concatenate([after(heads, normed_moe)[k] for k in range(cols)], axis=1)

    offs = row_places(first, local, rt_all, rt_ids)
    x_parts = gather_plane(normed_moe)
    block_rows = jnp.concatenate(after(parts, normed_moe), axis=0)
    x_parts[-1], heads, block_rows = lax.optimization_barrier((x_parts[-1], heads, block_rows))
    dy_all = lax.all_gather(after(out_grad, x_parts[2]), plane, axis=0, tiled=True)
    from_row, from_col = plane_places(row, col)
    whole_ids = from_row * cols + from_col
    index = jnp.arange(sources, dtype=jnp.int32)
    twist_row, back_col = index // cols ^ row, (col - index % cols + cols) % cols
    places = (twist_row % 2 * 2 + twist_row // 2) * cols + back_col
    ids = jnp.stack([rt_ids, places, whole_ids, whole_ids])

    res_part, rows_kept, ab_kept, gate, slot = moe_front(
        first, ids, offs, x_parts, rt_all, router_parts, w_in, w_down, cap, group
    )
    res = lax.psum_scatter(res_part, plane, scatter_dimension=0, tiled=True)
    pair0, gg0, dy_kept, *own0 = moe_back_first(
        offs, ids, dy_all, slot, rows_kept, ab_kept, gate, w_in, w_down, cap, group
    )
    paired = lax.axis_size("dp") == 2
    own = {0: list(own0)}
    far = {0: [None] * len(own0), 1: []}

    def exchange(e, p, *earlier):
        if not paired:
            return []
        far[e][p] = swap(after(own[e][p], *earlier), "dp", 1)
        return [(e, p)]

    def arrived(values, sent):
        if sent:
            values, kept = lax.optimization_barrier((values, [far[e][p] for e, p in sent]))
            for (e, p), piece in zip(sent, kept):
                far[e][p] = piece
        return values

    sent = exchange(0, 0, pair0)
    gn_far, gn_near, dg, *own1 = moe_back_last(
        offs, ids, slot, rows_kept, ab_kept, dy_kept, gate, w_in, w_down, pair0, gg0, cap,
        group,
    )
    own[1], far[1] = list(own1), [None] * len(own1)
    gn_far = arrived(gn_far, sent)

    from_far = swap(gn_far, "row", 1)
    sent = exchange(0, 1, gn_far)
    dg_back = lax.all_to_all(dg, plane, split_axis=0, concat_axis=0, tiled=True)
    from_far, dg_back = arrived(lax.optimization_barrier((from_far, dg_back)), sent)

    sum_out, sum_all = sum_rows_steps(row), sum_steps()
    halve, spread = row_halves(row)
    gn, terms = None, near_terms(gn_near, from_far, 2 * cols - 1, cols - 1, tok)
    for k in range(cols - 1, -1, -1):
        side = swap(terms[0], "row", 2)
        sent = exchange(*((0, 2), (0, 3), (1, 2), (1, 3))[cols - 1 - k], terms[0])
        total = terms[1].astype(F32)
        if gn is not None:
            total = total + shift(gn, "col", -1).astype(F32)
        if k:
            terms = near_terms(gn_near, after(from_far, terms[0]), cols + k - 1, k - 1, tok)
        if k == cols - 1:
            normed_wide = normed_moe.astype(F32)
            logits = jnp.dot(
                normed_wide, router, precision=HIGHEST, preferred_element_type=F32
            )
            expert_ids = jnp.arange(experts, dtype=jnp.int32)
            used = jnp.any(routes[:, :, None] == expert_ids[None, None, :], axis=1)
            top = jnp.max(jnp.where(used, logits, MASKED_SCORE), axis=1, keepdims=True)
            exps = jnp.where(used, jnp.exp(logits - top), 0.0)
            gates = exps / jnp.sum(exps, axis=1, keepdims=True)
            side, gates = lax.optimization_barrier((side, gates))
        if k == cols - 2:
            grad_gates = after(dg_back, gates)[:, :local].reshape(experts, tok).T
            grad_logits = gates * (
                grad_gates - jnp.sum(gates * grad_gates, axis=1, keepdims=True)
            )
            router_term = lax.dot_general(
                grad_logits,
                router,
                (((1,), (1,)), ((), ())),
                precision=HIGHEST,
                preferred_element_type=F32,
            )
            grad_router = lax.dot_general(
                grad_logits,
                normed_wide,
                (((0,), (0,)), ((), ())),
                precision=HIGHEST,
                preferred_element_type=F32,
            )
            small = halve[0](grad_router.reshape(1, 2, 2, experts // 4, feat))
            side, router_term, small = lax.optimization_barrier((side, router_term, small))
        if k == 1:
            side, res = lax.optimization_barrier((side, res))
        total, side, terms = arrived(lax.optimization_barrier((total, side, terms)), sent)
        gn = total + side.astype(F32)
        if k:
            gn = gn.astype(BF16)

    grad_middle, grad_attn, gain_moe_part, grad_heads = mid_back(
        gn, router_term, middle, out_grad, norm_gain_moe, out_all
    )
    sent = exchange(1, 4, gn)
    grads_block = lax.all_to_all(
        grad_heads, "col", split_axis=0, concat_axis=0, tiled=True
    )
    small = halve[1](after(small, grad_heads))
    core = (row % 2).reshape(1)
    w_out_sum = w_out_part(core, after(grad_attn, grad_heads), heads, w_out.shape[0])
    w_out_sum = [v.reshape(-1, 2, 1, w_out.shape[0], feat) for v in w_out_sum]
    w_out_sum = sum_out[1][0](sum_out[0][1](w_out_sum))
    grads_block, small, w_out_sum = arrived(
        lax.optimization_barrier((grads_block, small, w_out_sum)), sent
    )

    sent = exchange(1, 0, grads_block)
    small = sum_all[2](small)
    grad_mixed = attn_backward(
        here, grads_block.reshape(cols * tok, head_cols), q_rows, key_rows, value_rows, lse,
        cos, sin, starts, cols,
    )
    w_out_sum = sum_out[1][1](w_out_sum)
    grad_mixed, small = arrived(lax.optimization_barrier((grad_mixed, small)), sent)

    def na_part(k, *earlier):
        mixed = after(grad_mixed[k * tok : (k + 1) * tok], *earlier)
        return dot_nt(mixed, qkv_own)

    def held(*values):
        return arrived(lax.optimization_barrier(values), sent)

    sent = exchange(1, 1, grad_mixed)
    first_na = na_part(cols - 1).astype(BF16)
    grad_na = shift(first_na, "col", -1)
    small = sum_all[3](small)
    *w_qkv_sum, gain_attn_part = w_qkv_part(
        core, after(block_rows, first_na), grad_mixed, qkv_own, norm_gain_attn, w_qkv.shape[0]
    )
    w_qkv_sum = [v.reshape(-1, 2, 1, *w_qkv.shape) for v in w_qkv_sum]
    w_qkv_sum = sum_out[0][1](w_qkv_sum)
    gains = sum_all[0](jnp.concatenate([gain_moe_part, gain_attn_part], axis=0))
    next_na = na_part(cols - 2, first_na)
    grad_na, small, w_out_sum, w_qkv_sum, gains, next_na = held(
        grad_na, small, w_out_sum, w_qkv_sum, gains, next_na
    )

    grad_na = (grad_na.astype(F32) + next_na).astype(BF16)
    sent = []
    next_na = na_part(cols - 3, grad_na)
    grad_w_in = grad_w_down = next_na
    if paired:
        downs = len(piece_shapes(feat, FFE, True)[0])
        grad_w_in = add_pairs(own[0][downs:], after(far[0][downs:], next_na), 0, local)
        grad_w_down = add_pairs(own[0][:downs], after(far[0][:downs], next_na), 0, local)
    grad_na = shift(grad_na, "col", -1)
    gains = sum_all[1](gains)
    w_qkv_sum = sum_out[1][0](w_qkv_sum)
    for step in sum_out[2:]:
        w_out_sum = step[1](step[0](w_out_sum))
    for step in sum_all[4:]:
        small = step(small)
    gains = sum_all[2](gains)
    grad_na, next_na, gains, small, w_qkv_sum, grad_w_in, grad_w_down, w_out_sum = held(
        grad_na, next_na, gains, small, w_qkv_sum, grad_w_in, grad_w_down, w_out_sum
    )

    grad_na = (grad_na.astype(F32) + next_na).astype(BF16)
    next_na = na_part(cols - 4, grad_na)
    lines = lax.all_to_all(
        jnp.stack([w_out_sum[..., k * head_cols : (k + 1) * head_cols] for k in range(cols)]),
        "col",
        split_axis=0,
        concat_axis=0,
        tiled=True,
    )
    result = middle + after(res, next_na).astype(F32)
    grad_na = shift(grad_na, "col", -1)
    gains = sum_all[3](gains)
    small = spread[0](small)
    w_qkv_sum = sum_out[1][1](w_qkv_sum)
    if paired:
        downs = len(piece_shapes(feat, FFE, False)[0])
        grad_w_in = add_pairs(own[1][downs:], after(far[1][downs:], next_na), 1, local, grad_w_in)
        grad_w_down = add_pairs(own[1][:downs], far[1][:downs], 1, local, grad_w_down)
    else:
        ins, outs = [], []
        for e in range(local):
            downs = len(piece_shapes(feat, FFE, e == 0)[0])
            outs.append(jnp.concatenate(own[e][:downs]))
            ins.append(jnp.concatenate(own[e][downs:]))
        grad_w_in = lax.psum(jnp.stack(ins), "dp").astype(F32)
        grad_w_down = lax.psum(jnp.stack(outs), "dp").astype(F32)
    grad_na, next_na, gains, small, w_qkv_sum, lines, grad_w_in, grad_w_down, result = held(
        grad_na, next_na, gains, small, w_qkv_sum, lines, grad_w_in, grad_w_down, result
    )

    grad_na = grad_na.astype(F32) + next_na
    for step in sum_all[4:]:
        gains = step(gains)
    small = spread[1](small).reshape(experts, feat)
    for step in sum_out[2:]:
        w_qkv_sum = step[1](step[0](w_qkv_sum))
    grad_hidden = grad_middle + norm_back(rows_in, norm_gain_attn, grad_na)
    grad_w_qkv = w_qkv_sum.reshape(w_qkv.shape).astype(F32)
    grad_w_out = jnp.sum(lines.astype(F32), axis=0).reshape(w_out.shape)
    return (
        result,
        grad_hidden,
        gains[1],
        gains[0],
        grad_w_qkv,
        grad_w_out,
        small.T,
        grad_w_in,
        grad_w_down,
    )


def solution(mesh):
    in_specs = (
        P(("dp", "row", "col"), None),
        P(),
        P(),
        P(("dp", "row"), "col"),
        P(("dp", "row"), "col"),
        P(),
        P(("row", "col"), None, None),
        P(("row", "col"), None, None),
        P(("dp", "row"), None),
        P(("dp", "row", "col"), None),
        P(("dp", "row", "col"), None),
    )
    out_specs = (
        P(("dp", "row", "col"), None),
        P(("dp", "row", "col"), None),
        P(),
        P(),
        P(("dp", "row"), "col"),
        P(("dp", "row"), "col"),
        P(),
        P(("row", "col"), None, None),
        P(("row", "col"), None, None),
    )
    return jax.shard_map(shards, mesh=mesh, in_specs=in_specs, out_specs=out_specs, check_vma=False)
```

```python
import functools
import math

import jax
import jax.numpy as jnp
from jax import lax
from jax.experimental import pallas as pl
from jax.experimental.pallas import tpu as pltpu
from jax.sharding import PartitionSpec as P

HD = 64
FFE = 512
TOP = 8
REP = 3
SEQ_MAX = 512

EPSILON = 1e-06
HIGHEST = lax.Precision.HIGHEST
MASKED_SCORE = -1e30
F32 = jnp.float32
BF16 = jnp.bfloat16


def dot_nn(left, right):
    return lax.dot_general(left, right, (((1,), (0,)), ((), ())), preferred_element_type=F32)


def dot_nt(left, right):
    return lax.dot_general(left, right, (((1,), (1,)), ((), ())), preferred_element_type=F32)


def dot_tn(left, right):
    return lax.dot_general(left, right, (((0,), (0,)), ((), ())), preferred_element_type=F32)


def lane_low(shape):
    return lax.broadcasted_iota(jnp.int32, shape, 1) < HD


def twist(tile_vals):
    width = tile_vals.shape[1]
    lane = lax.broadcasted_iota(jnp.int32, tile_vals.shape, 1)
    ahead = pltpu.roll(tile_vals, width - HD // 2, 1)
    behind = pltpu.roll(tile_vals, HD // 2, 1)
    return jnp.where(lane % HD < HD // 2, -ahead, behind)


def both_halves(tile_vals, low):
    kept = jnp.where(lane_low(tile_vals.shape) == low, tile_vals, 0.0)
    return kept + pltpu.roll(kept, HD, 1)


def head_places():
    per = REP + 2
    def at(index):
        return (index // 2, index % 2 == 0)
    groups = []
    for g in range(2):
        base = g * per
        groups.append(
            ([at(base + r) for r in range(REP)], at(base + REP), at(base + REP + 1))
        )
    return groups


def chunk_span(a, tok):
    reach = -(-(SEQ_MAX - 1) // tok)
    return max(0, a - reach) * tok, (a + 1) * tok


def mask_bias(start_row, a, tok):
    low, high = chunk_span(a, tok)
    shape = (high - low, tok)
    keys = lax.broadcasted_iota(jnp.int32, shape, 0) + low
    queries = lax.broadcasted_iota(jnp.int32, shape, 1) + a * tok
    allowed = (keys >= start_row) & (keys <= queries)
    return jnp.where(allowed, 0.0, MASKED_SCORE)


def attn_forward_body(
    chunks, here_ref, *refs,
):
    ins, (w_ref, cos_ref, sin_ref, start_ref, qkv_ref, kk_ref, vv_ref, lse_ref, heads_ref) = (
        refs[:chunks],
        refs[chunks:],
    )
    tok = ins[0].shape[0]
    here = here_ref[0]
    places = head_places()
    for k in range(chunks):
        a = lax.rem(here + (chunks - k), chunks)
        at = pl.ds(pl.multiple_of(a * tok, tok), tok)
        mixed = dot_nn(ins[k][...], w_ref[...])
        cos = cos_ref[at, :]
        sin = sin_ref[at, :]
        tiles = [mixed[:, 128 * i : 128 * (i + 1)] for i in range(mixed.shape[1] // 128)]
        turned = [t * cos + twist(t) * sin for t in tiles]
        for g, (queries, key, value) in enumerate(places):
            for r, (tile_at, low) in enumerate(queries):
                part = jnp.where(lane_low(tiles[0].shape) == low, turned[tile_at], 0.0)
                slot = 128 * (g * REP + r)
                qkv_ref[at, slot : slot + 128] = part.astype(BF16)
            kk_ref[at, 128 * g : 128 * (g + 1)] = both_halves(turned[key[0]], key[1]).astype(BF16)
            vv_ref[at, 128 * g : 128 * (g + 1)] = both_halves(tiles[value[0]], value[1]).astype(BF16)
    for a in range(chunks):
        low_key, high_key = chunk_span(a, tok)
        bias = mask_bias(start_ref[a : a + 1, :], a, tok)
        out = [None] * REP
        for g, (queries, _, _) in enumerate(places):
            keys = kk_ref[low_key:high_key, 128 * g : 128 * (g + 1)]
            vals = vv_ref[low_key:high_key, 128 * g : 128 * (g + 1)]
            for r in range(REP):
                head = g * REP + r
                q = qkv_ref[a * tok : (a + 1) * tok, 128 * head : 128 * (head + 1)]
                scores = dot_nt(keys, q) * HD ** (-0.5) + bias
                top = jnp.max(scores, axis=0, keepdims=True)
                terms = jnp.exp(scores - top)
                total = jnp.sum(terms, axis=0, keepdims=True)
                probs = (terms * (1.0 / total)).astype(BF16)
                lse_ref[head, a : a + 1, :] = top + jnp.log(total)
                mix = dot_tn(probs, vals)
                t = head // 2
                low = lane_low(mix.shape)
                out[t] = mix if head % 2 == 0 else jnp.where(low, out[t], mix)
        for t in range(REP):
            heads_ref[a * tok : (a + 1) * tok, 128 * t : 128 * (t + 1)] = out[t].astype(BF16)


def whole_block(values):
    zeros = (0,) * len(values.shape)
    return pl.BlockSpec(values.shape, lambda i: zeros, pipeline_mode=pl.Buffered(1))


def attn_forward(here, parts, w_cols, cos, sin, starts):
    chunks = len(parts)
    tok, feat = parts[0].shape
    total = chunks * tok
    cols = w_cols.shape[1]
    return pl.pallas_call(
        functools.partial(attn_forward_body, chunks),
        grid=(1,),
        in_specs=[pl.BlockSpec(memory_space=pltpu.SMEM)]
        + [whole_block(v) for v in (*parts, w_cols, cos, sin, starts)],
        out_specs=[
            whole_block(jax.ShapeDtypeStruct(s, F32))
            for s in (
                (total, 128 * 2 * REP), (total, 256), (total, 256), (2 * REP, 8, tok),
                (total, 2 * REP * HD),
            )
        ],
        out_shape=[
            jax.ShapeDtypeStruct((total, 128 * 2 * REP), BF16),
            jax.ShapeDtypeStruct((total, 256), BF16),
            jax.ShapeDtypeStruct((total, 256), BF16),
            jax.ShapeDtypeStruct((2 * REP, 8, tok), F32),
            jax.ShapeDtypeStruct((total, 2 * REP * HD), BF16),
        ],
        compiler_params=pltpu.CompilerParams(vmem_limit_bytes=60 * 1024 * 1024),
        cost_estimate=pl.CostEstimate(
            flops=2 * total * feat * cols * 4, bytes_accessed=8 * total * cols, transcendentals=0
        ),
        name="attn_forward",
    )(here, *parts, w_cols, cos, sin, starts)


def attn_backward_body(
    chunks, here_ref, grads_ref, q_ref, kk_ref, vv_ref, lse_ref, cos_ref, sin_ref, start_ref,
    turned_ref, first_ref, dk, dv, dq,
):
    tok = q_ref.shape[0] // chunks
    here = here_ref[0]
    dk[...] = jnp.zeros_like(dk)
    dv[...] = jnp.zeros_like(dv)
    for a in range(chunks):
        low_key, high_key = chunk_span(a, tok)
        bias = mask_bias(start_ref[a : a + 1, :], a, tok)
        for g in range(2):
            keys = kk_ref[low_key:high_key, 128 * g : 128 * (g + 1)]
            vals = vv_ref[low_key:high_key, 128 * g : 128 * (g + 1)]
            for r in range(REP):
                head = g * REP + r
                q = q_ref[a * tok : (a + 1) * tok, 128 * head : 128 * (head + 1)]
                t, is_low = head // 2, head % 2 == 0
                pair = grads_ref[a * tok : (a + 1) * tok, 128 * t : 128 * (t + 1)]
                grad = jnp.where(lane_low(pair.shape) == is_low, pair, jnp.zeros_like(pair))
                scores = dot_nt(keys, q) * HD ** (-0.5) + bias
                probs = jnp.exp(scores - lse_ref[head, a : a + 1, :])
                grad_probs = dot_nt(vals, grad)
                dv[low_key:high_key, 128 * g : 128 * (g + 1)] += dot_nn(probs.astype(BF16), grad)
                inner = jnp.sum(probs * grad_probs, axis=0, keepdims=True)
                grad_scores = (probs * (grad_probs - inner)).astype(BF16)
                dk[low_key:high_key, 128 * g : 128 * (g + 1)] += dot_nn(grad_scores, q)
                part = dot_tn(grad_scores, keys)
                here_at = slice(128 * t, 128 * (t + 1))
                rows = slice(a * tok, (a + 1) * tok)
                if is_low:
                    dq[rows, here_at] = part
                else:
                    dq[rows, here_at] = jnp.where(lane_low(part.shape), dq[rows, here_at], part)
    for a in range(chunks):
        rows = slice(a * tok, (a + 1) * tok)
        to = pl.ds(pl.multiple_of(lax.rem(here + (chunks - a), chunks) * tok, tok), tok)
        cos = cos_ref[rows, :]
        sin = sin_ref[rows, :]

        def back(vals):
            return (vals * cos - twist(vals) * sin) * HD ** (-0.5)

        def whole(vals):
            return vals + pltpu.roll(vals, HD, 1)

        low = lane_low((tok, 128))
        keys = [back(whole(dk[rows, 128 * g : 128 * (g + 1)])) for g in range(2)]
        vals = [whole(dv[rows, 128 * g : 128 * (g + 1)]) for g in range(2)]
        qs = [back(dq[rows, 128 * t : 128 * (t + 1)]) for t in range(REP)]
        tiles = [
            qs[0],
            jnp.where(low, qs[1], keys[0]),
            jnp.where(low, vals[0], qs[1]),
            qs[2],
            jnp.where(low, keys[1], vals[1]),
        ]
        for i, vals_of in enumerate(tiles):
            turned_ref[to, 128 * i : 128 * (i + 1)] = vals_of.astype(BF16)

        @pl.when(lax.rem(here + (chunks - a), chunks) == chunks - 1)
        def _(tiles=tiles):
            for i, vals_of in enumerate(tiles):
                first_ref[:, 128 * i : 128 * (i + 1)] = vals_of.astype(BF16)


def attn_backward(here, grads, q_rows, key_rows, value_rows, lse, cos, sin, starts, chunks):
    total = q_rows.shape[0]
    cols = 2 * (REP + 2) * HD
    return pl.pallas_call(
        functools.partial(attn_backward_body, chunks),
        grid=(1,),
        in_specs=[pl.BlockSpec(memory_space=pltpu.SMEM)]
        + [
            whole_block(v)
            for v in (grads, q_rows, key_rows, value_rows, lse, cos, sin, starts)
        ],
        out_specs=[
            whole_block(jax.ShapeDtypeStruct((total, cols), BF16)),
            whole_block(jax.ShapeDtypeStruct((total // chunks, cols), BF16)),
        ],
        out_shape=[
            jax.ShapeDtypeStruct((total, cols), BF16),
            jax.ShapeDtypeStruct((total // chunks, cols), BF16),
        ],
        scratch_shapes=[
            pltpu.VMEM((total, 256), F32),
            pltpu.VMEM((total, 256), F32),
            pltpu.VMEM((total, 2 * REP * HD), F32),
        ],
        compiler_params=pltpu.CompilerParams(vmem_limit_bytes=60 * 1024 * 1024),
        cost_estimate=beside_transfers(),
        name="attn_backward",
    )(here, grads, q_rows, key_rows, value_rows, lse, cos, sin, starts)


def hot_rows(srow, cap, tok):
    places = lax.broadcasted_iota(jnp.int32, (cap, tok), 0).astype(F32)
    return srow == places


def one_zero(mask):
    return jnp.where(mask, 1.0, 0.0).astype(BF16)


def front_body(
    cap, tile, tiles, group, sources,
    first_ref, ids_ref, offs_ref, *refs,
):
    x_refs = refs[:sources]
    (
        rt_ref, rs_ref, win_ref, wdn_ref, res_ref, rows_ref, ab_ref, gate_ref, slot_ref,
        buf, gate, arena, sems,
    ) = refs[sources:]
    step = pl.program_id(0)
    tok, feat = arena.shape[1:]
    experts = rs_ref.shape[1] // 4
    local = buf.shape[0]
    ff = wdn_ref.shape[1]
    first_work = sources // group

    def fetch(at):
        where = at % 2 * group
        return [
            pltpu.make_async_copy(x_refs[at * group + s], arena.at[where + s], sems.at[where + s])
            for s in range(group)
        ]

    @pl.when(step < first_work)
    def _gather():
        @pl.when(step == 0)
        def _():
            for copy in fetch(0) + fetch(1):
                copy.start()

        here = step % 2 * group
        for s in range(group):
            pltpu.make_async_copy(x_refs[0], arena.at[here + s], sems.at[here + s]).wait()

        ids = lax.broadcasted_iota(jnp.int32, (experts, tok), 0)
        before = one_zero(
            lax.broadcasted_iota(jnp.int32, (tok, tok), 0)
            < lax.broadcasted_iota(jnp.int32, (tok, tok), 1)
        )
        srows, grows = [], []
        for s in range(group):
            thirds = dot_nn(arena[here + s], rs_ref[...]).T
            logits = (
                thirds[2 * experts : 3 * experts] + thirds[experts : 2 * experts]
            ) + thirds[:experts]
            rt = rt_ref[ids_ref[0, step * group + s]]
            used = ids == rt[0:1]
            for k in range(1, rt.shape[0]):
                used = used | (ids == rt[k : k + 1])
            top = jnp.max(jnp.where(used, logits, MASKED_SCORE), axis=0, keepdims=True)
            terms = jnp.where(used, jnp.exp(logits - top), 0.0)
            gates = terms / jnp.sum(terms, axis=0, keepdims=True)
            used_f = jnp.where(used, 1.0, 0.0)
            rank = dot_nn(used_f.astype(BF16), before)
            for e in range(local):
                mine = ids == first_ref[0] + e
                grows.append(jnp.sum(jnp.where(mine, gates, 0.0), axis=0, keepdims=True))
                srow = jnp.sum(jnp.where(mine & used, rank + 1.0, 0.0), axis=0, keepdims=True) - 1.0
                srows.append(srow)
        for s in range(group):
            hots = [hot_rows(srows[s * local + e], cap, tok) for e in range(local)]
            picked = dot_nn(one_zero(jnp.concatenate(hots, axis=0)), arena[here + s]).astype(BF16)
            for e in range(local):
                at = pl.ds(pl.multiple_of(offs_ref[e, step * group + s], 16), cap)
                slot_ref[e, pl.ds(step * group + s, 1), :] = srows[s * local + e]
                gcol = jnp.sum(
                    jnp.where(hots[e], grows[s * local + e], 0.0), axis=1, keepdims=True
                )
                gate[e, at, :] = jnp.broadcast_to(gcol, (cap, 128))
                buf[e, at, :] = picked[e * cap : (e + 1) * cap]

        for later in range(2, first_work):

            @pl.when(step + 2 == later)
            def _(later=later):
                for copy in fetch(later):
                    copy.start()

        @pl.when(step == first_work - 1)
        def _():
            for e in range(local):
                end = pl.multiple_of(offs_ref[e, sources], 16)
                buf[e, pl.ds(end, tile), :] = jnp.zeros((tile, feat), BF16)
                gate[e, pl.ds(end, tile), :] = jnp.zeros((tile, 128), F32)

    work = step - first_work
    e = work // tiles
    j = work % tiles

    @pl.when((work >= 0) & (work < local * tiles))
    def _experts():
        @pl.when(j * tile < offs_ref[e, sources])
        def _():
            at = pl.ds(pl.multiple_of(j * tile, tile), tile)
            rows = buf[e, at, :]
            g = gate[e, at, :]
            rows_ref[0] = rows
            gate_ref[0] = g
            a = dot_nn(rows, win_ref[0, :, :ff])
            b = dot_nn(rows, win_ref[0, :, ff:])
            ab_ref[0, :, :ff] = a
            ab_ref[0, :, ff:] = b
            act_g = (g[:, 0:1] * (a / (1.0 + jnp.exp(-a)) * b)).astype(BF16)
            buf[e, at, :] = dot_nn(act_g, wdn_ref[0]).astype(BF16)

    back = work - local * tiles

    @pl.when(back >= 0)
    def _scatter():
        for s in range(group):
            source = ids_ref[1, back * group + s]
            hots, terms = [], []
            for e in range(local):
                hots.append(hot_rows(slot_ref[e, pl.ds(source, 1), :], cap, tok))
                off = pl.multiple_of(offs_ref[e, source], 16)
                terms.append(buf[e, pl.ds(off, cap), :])
            total = dot_tn(
                one_zero(jnp.concatenate(hots, axis=0)), jnp.concatenate(terms, axis=0)
            )
            res_ref[s * tok : (s + 1) * tok, :] = total.astype(BF16)


def moe_front(first, ids, offs, x_parts, rt_all, router_parts, w_in, w_down, cap, group):
    sources, top, tok = rt_all.shape
    feat = x_parts[0].shape[1]
    local, _, ff2 = w_in.shape
    ff = ff2 // 2
    most = sources * cap
    tile = min(256, most)
    tiles = most // tile
    room = most + max(tile, cap)
    steps = sources // group
    middle = local * tiles

    def exp3(i, f, ids, offs):
        return (jnp.clip((i - steps) // tiles, 0, local - 1), 0, 0)

    def tile3(i, f, ids, offs):
        at = jnp.clip(i - steps, 0, middle - 1)
        return (at // tiles, at % tiles, 0)

    return pl.pallas_call(
        functools.partial(front_body, cap, tile, tiles, group, sources),
        grid_spec=pltpu.PrefetchScalarGridSpec(
            num_scalar_prefetch=3,
            grid=(2 * steps + middle,),
            in_specs=[pl.BlockSpec(memory_space=pl.ANY)] * sources
            + [
                pl.BlockSpec(rt_all.shape, lambda i, f, ids, offs: (0, 0, 0)),
                pl.BlockSpec(router_parts.shape, lambda i, f, ids, offs: (0, 0)),
                pl.BlockSpec((1, feat, ff2), exp3),
                pl.BlockSpec((1, ff, feat), exp3),
            ],
            out_specs=[
                pl.BlockSpec(
                    (group * tok, feat), lambda i, f, ids, offs: (jnp.maximum(i - steps - middle, 0), 0)
                ),
                pl.BlockSpec((1, tile, feat), tile3),
                pl.BlockSpec((1, tile, ff2), tile3),
                pl.BlockSpec((1, tile, 128), tile3),
                pl.BlockSpec((local, sources, tok), lambda i, f, ids, offs: (0, 0, 0)),
            ],
            scratch_shapes=[
                pltpu.VMEM((local, room, feat), BF16),
                pltpu.VMEM((local, room, 128), F32),
                pltpu.VMEM((2 * group, tok, feat), BF16),
                pltpu.SemaphoreType.DMA((2 * group,)),
            ],
        ),
        out_shape=[
            jax.ShapeDtypeStruct((sources * tok, feat), BF16),
            jax.ShapeDtypeStruct((local, most, feat), BF16),
            jax.ShapeDtypeStruct((local, most, ff2), F32),
            jax.ShapeDtypeStruct((local, most, 128), F32),
            jax.ShapeDtypeStruct((local, sources, tok), F32),
        ],
        compiler_params=pltpu.CompilerParams(vmem_limit_bytes=56 * 1024 * 1024),
        cost_estimate=pl.CostEstimate(
            flops=2 * most * feat * ff * 3, bytes_accessed=10 * most * feat, transcendentals=0
        ),
        name="moe_front",
    )(first, ids, offs, *x_parts, rt_all, router_parts, w_in, w_down)


def back_tile(rows, ab_ref, grads, g, win_ref, wdn_ref, acc_i, acc_d):
    ff = wdn_ref.shape[1]
    a = ab_ref[0, :, :ff]
    b = ab_ref[0, :, ff:]
    ga = dot_nt(grads, wdn_ref[0])
    sig = 1.0 / (1.0 + jnp.exp(-a))
    silu = a * sig
    act = silu * b
    gate_grad = jnp.sum(act * ga, axis=1, keepdims=True)
    gag = g * ga
    da = (gag * b * (sig * (1.0 + a * (1.0 - sig)))).astype(BF16)
    db = (gag * silu).astype(BF16)
    act_g = (g * act).astype(BF16)
    acc_d[...] += dot_tn(act_g, grads)
    acc_i[:, :ff] += dot_tn(rows, da)
    acc_i[:, ff:] += dot_tn(rows, db)
    pair = dot_nt(da, win_ref[0, :, :ff]) + dot_nt(db, win_ref[0, :, ff:])
    return pair.astype(BF16), gate_grad


def piece_shapes(feat, ff, first):
    down, rows = [ff // 2, ff // 2], [feat // 3] * 3
    if first:
        down, rows = [ff], [feat // 4, feat // 3, feat // 12 * 5]
    return [(n, feat) for n in down], [(n, 2 * ff) for n in rows]


def write_pieces(acc_i, acc_d, refs):
    at = 0
    for ref in refs:
        acc = acc_d if ref.shape[1] == acc_d.shape[1] else acc_i
        ref[...] = acc[at : at + ref.shape[0], :].astype(BF16)
        at = (at + ref.shape[0]) % acc.shape[0]


def back_first_body(
    cap, tile, tiles, group,
    offs_ref, ids_ref, *refs,
):
    dy_refs = refs[:group]
    (slot_ref, rows_ref, ab_ref, gate_ref, win_ref, wdn_ref, pair_ref, gg_ref, other_ref, *piece_refs, buf, acc_i, acc_d) = refs[group:]
    step = pl.program_id(0)
    sources = slot_ref.shape[1]
    local = buf.shape[0]
    tok, feat = dy_refs[0].shape
    first_work = sources // group

    @pl.when(step < first_work)
    def _gather():
        for s in range(group):
            source = step * group + s
            hots = [hot_rows(slot_ref[e, pl.ds(source, 1), :], cap, tok) for e in range(local)]
            picked = dot_nn(
                one_zero(jnp.concatenate(hots, axis=0)), dy_refs[s][...]
            ).astype(BF16)
            for e in range(local):
                off = pl.multiple_of(offs_ref[e, source], 16)
                buf[e, pl.ds(off, cap), :] = picked[e * cap : (e + 1) * cap]

        @pl.when(step == first_work - 1)
        def _():
            for e in range(local):
                end = pl.multiple_of(offs_ref[e, sources], 16)
                buf[e, pl.ds(end, tile), :] = jnp.zeros((tile, feat), BF16)
            acc_i[...] = jnp.zeros_like(acc_i)
            acc_d[...] = jnp.zeros_like(acc_d)

    j = step - first_work

    @pl.when(j >= 0)
    def _experts():
        at = pl.ds(pl.multiple_of(j * tile, tile), tile)

        @pl.when(j * tile < offs_ref[1, sources])
        def _():
            other_ref[0] = buf[1, at, :]

        @pl.when(j * tile < offs_ref[0, sources])
        def _():
            pair, gate_grad = back_tile(
                rows_ref[0], ab_ref, buf[0, at, :], gate_ref[0, :, 0:1], win_ref, wdn_ref, acc_i, acc_d
            )
            pair_ref[...] = pair
            gg_ref[...] = jnp.broadcast_to(gate_grad, (tile, 128))

        @pl.when(j * tile >= offs_ref[0, sources])
        def _():
            pair_ref[...] = jnp.zeros_like(pair_ref)
            gg_ref[...] = jnp.zeros_like(gg_ref)

        @pl.when(j == tiles - 1)
        def _():
            write_pieces(acc_i, acc_d, piece_refs)


def used_tile(j, offs, e, sources, tile):
    return jnp.clip(j, 0, jnp.maximum((offs[e, sources] + (tile - 1)) // tile - 1, 0))


def moe_back_first(offs, ids, dy_all, slot, rows, ab, gate, w_in, w_down, cap, group):
    local, sources, tok = slot.shape
    most, feat = rows.shape[1:]
    ff2 = w_in.shape[2]
    ff = ff2 // 2
    tile = min(256, most)
    tiles = most // tile
    room = most + max(tile, cap)
    steps = sources // group

    def in_tile(i, offs, ids):
        return (0, used_tile(i - steps, offs, 0, sources, tile), 0)

    def out_tile(i, offs, ids):
        return (jnp.maximum(i - steps, 0), 0)

    def other_tile(i, offs, ids):
        return (0, used_tile(i - steps, offs, 1, sources, tile), 0)

    def source(s):
        return lambda i, offs, ids: (ids[2, jnp.minimum(i, steps - 1) * group + s], 0)

    return pl.pallas_call(
        functools.partial(back_first_body, cap, tile, tiles, group),
        grid_spec=pltpu.PrefetchScalarGridSpec(
            num_scalar_prefetch=2,
            grid=(steps + tiles,),
            in_specs=[pl.BlockSpec((tok, feat), source(s)) for s in range(group)]
            + [
                pl.BlockSpec(slot.shape, lambda i, offs, ids: (0, 0, 0)),
                pl.BlockSpec((1, tile, feat), in_tile),
                pl.BlockSpec((1, tile, ff2), in_tile),
                pl.BlockSpec((1, tile, 128), in_tile),
                pl.BlockSpec((1, feat, ff2), lambda i, offs, ids: (0, 0, 0)),
                pl.BlockSpec((1, ff, feat), lambda i, offs, ids: (0, 0, 0)),
            ],
            out_specs=[
                pl.BlockSpec((tile, feat), out_tile),
                pl.BlockSpec((tile, 128), out_tile),
                pl.BlockSpec((1, tile, feat), other_tile),
                *[pl.BlockSpec(s, lambda i, offs, ids: (0, 0)) for s in sum(piece_shapes(feat, ff, True), [])],
            ],
            scratch_shapes=[
                pltpu.VMEM((local, room, feat), BF16),
                pltpu.VMEM((feat, ff2), F32),
                pltpu.VMEM((ff, feat), F32),
            ],
        ),
        out_shape=[
            jax.ShapeDtypeStruct((most, feat), BF16),
            jax.ShapeDtypeStruct((most, 128), F32),
            jax.ShapeDtypeStruct((1, most, feat), BF16),
            *[jax.ShapeDtypeStruct(s, BF16) for s in sum(piece_shapes(feat, ff, True), [])],
        ],
        compiler_params=pltpu.CompilerParams(vmem_limit_bytes=56 * 1024 * 1024),
        cost_estimate=pl.CostEstimate(
            flops=2 * most * feat * ff * 4, bytes_accessed=5 * dy_all.size * 2, transcendentals=0
        ),
        name="moe_back_first",
    )(offs, ids, *[dy_all] * group, slot, rows, ab, gate, w_in, w_down)


def back_last_body(
    cap, tile, tiles, group,
    offs_ref, ids_ref, slot_ref, rows_ref, ab_ref, grads_ref, gate_ref, win_ref, wdn_ref, pair0_any, gg0_any,
    far_ref, near_ref, dg_ref, *rest,
):
    *piece_refs, buf, gg, acc_i, acc_d, pair0_ref, gg0_ref, stage_d, stage_i, sems = rest
    step = pl.program_id(0)
    sources, tok = slot_ref.shape[1:]
    feat = far_ref.shape[1]

    def held_copies():
        return [
            pltpu.make_async_copy(pair0_any, pair0_ref, sems.at[0]),
            pltpu.make_async_copy(gg0_any, gg0_ref, sems.at[1]),
        ]

    def piece_copies():
        copies, at = [], 0
        for ref in piece_refs:
            stage = stage_d if ref.shape[1] == stage_d.shape[1] else stage_i
            copies.append(
                pltpu.make_async_copy(
                    stage.at[pl.ds(at, ref.shape[0]), :], ref, sems.at[2 + len(copies)]
                )
            )
            at = (at + ref.shape[0]) % stage.shape[0]
        return copies

    @pl.when(step == 0)
    def _():
        for copy in held_copies():
            copy.start()
        acc_i[...] = jnp.zeros_like(acc_i)
        acc_d[...] = jnp.zeros_like(acc_d)

    @pl.when(step < tiles)
    def _experts():
        at = pl.ds(pl.multiple_of(step * tile, tile), tile)

        @pl.when(step * tile < offs_ref[1, sources])
        def _():
            pair, gate_grad = back_tile(
                rows_ref[0], ab_ref, grads_ref[0], gate_ref[0, :, 0:1], win_ref, wdn_ref, acc_i, acc_d
            )
            buf[at, :] = pair
            gg[at, :] = jnp.broadcast_to(gate_grad, (tile, 128))

        @pl.when(step * tile >= offs_ref[1, sources])
        def _():
            buf[at, :] = jnp.zeros((tile, feat), BF16)
            gg[at, :] = jnp.zeros((tile, 128), F32)

        @pl.when(step == tiles - 1)
        def _():
            stage_d[...] = acc_d[...].astype(BF16)
            stage_i[...] = acc_i[...].astype(BF16)
            for copy in piece_copies():
                copy.start()
            for copy in held_copies():
                copy.wait()

    back = step - tiles

    @pl.when(back >= 0)
    def _scatter():
        for s in range(group):
            source = lax.rem(back * group + s + sources // 2, sources)
            to = ids_ref[3, source]
            hots, terms = [], []
            for e, (pair, grads) in enumerate(((pair0_ref, gg0_ref), (buf, gg))):
                hot = hot_rows(slot_ref[e, pl.ds(source, 1), :], cap, tok)
                at = pl.ds(pl.multiple_of(offs_ref[e, source], 16), cap)
                hots.append(hot)
                terms.append(pair[at, :])
                dg_ref[to, e : e + 1, :] = jnp.sum(
                    jnp.where(hot, grads[at, 0:1], 0.0), axis=0, keepdims=True
                )
            dg_ref[to, 2:, :] = jnp.zeros((dg_ref.shape[1] - 2, tok), F32)
            total = dot_tn(
                one_zero(jnp.concatenate(hots, axis=0)), jnp.concatenate(terms, axis=0)
            )
            total = total.astype(BF16)

            @pl.when(back < sources // (2 * group))
            def _(total=total, s=s):
                far_ref[s * tok : (s + 1) * tok, :] = total

            @pl.when(back >= sources // (2 * group))
            def _(total=total, s=s):
                near_ref[s * tok : (s + 1) * tok, :] = total

        @pl.when(step == pl.num_programs(0) - 1)
        def _():
            for copy in piece_copies():
                copy.wait()


def moe_back_last(offs, ids, slot, rows, ab, grads, gate, w_in, w_down, pair0, gg0, cap, group):
    local, sources, tok = slot.shape
    most, feat = rows.shape[1:]
    ff2 = w_in.shape[2]
    ff = ff2 // 2
    tile = min(256, most)
    tiles = most // tile
    steps = sources // group

    def in_tile(i, offs, ids):
        return (1, used_tile(i, offs, 1, sources, tile), 0)

    def own_tile(i, offs, ids):
        return (0, used_tile(i, offs, 1, sources, tile), 0)

    def whole(i, offs, ids):
        return (0, 0)

    def far(i, offs, ids):
        return (jnp.clip(i - tiles, 0, steps // 2 - 1), 0)

    def near(i, offs, ids):
        return (jnp.clip(i - tiles - steps // 2, 0, steps // 2 - 1), 0)

    return pl.pallas_call(
        functools.partial(back_last_body, cap, tile, tiles, group),
        grid_spec=pltpu.PrefetchScalarGridSpec(
            num_scalar_prefetch=2,
            grid=(steps + tiles,),
            in_specs=[
                pl.BlockSpec(slot.shape, lambda i, offs, ids: (0, 0, 0)),
                pl.BlockSpec((1, tile, feat), in_tile),
                pl.BlockSpec((1, tile, ff2), in_tile),
                pl.BlockSpec((1, tile, feat), own_tile),
                pl.BlockSpec((1, tile, 128), in_tile),
                pl.BlockSpec((1, feat, ff2), lambda i, offs, ids: (1, 0, 0)),
                pl.BlockSpec((1, ff, feat), lambda i, offs, ids: (1, 0, 0)),
                pl.BlockSpec(memory_space=pl.ANY),
                pl.BlockSpec(memory_space=pl.ANY),
            ],
            out_specs=[
                pl.BlockSpec((group * tok, feat), far),
                pl.BlockSpec((group * tok, feat), near),
                pl.BlockSpec((sources, 8, tok), lambda i, offs, ids: (0, 0, 0)),
                *[pl.BlockSpec(memory_space=pl.ANY)] * len(sum(piece_shapes(feat, ff, False), [])),
            ],
            scratch_shapes=[
                pltpu.VMEM((most, feat), BF16),
                pltpu.VMEM((most, 128), F32),
                pltpu.VMEM((feat, ff2), F32),
                pltpu.VMEM((ff, feat), F32),
                pltpu.VMEM((most, feat), BF16),
                pltpu.VMEM((most, 128), F32),
                pltpu.VMEM((ff, feat), BF16),
                pltpu.VMEM((feat, ff2), BF16),
                pltpu.SemaphoreType.DMA((2 + len(sum(piece_shapes(feat, ff, False), [])),)),
            ],
        ),
        out_shape=[
            jax.ShapeDtypeStruct((sources // 2 * tok, feat), BF16),
            jax.ShapeDtypeStruct((sources // 2 * tok, feat), BF16),
            jax.ShapeDtypeStruct((sources, 8, tok), F32),
            *[jax.ShapeDtypeStruct(s, BF16) for s in sum(piece_shapes(feat, ff, False), [])],
        ],
        compiler_params=pltpu.CompilerParams(vmem_limit_bytes=56 * 1024 * 1024),
        cost_estimate=pl.CostEstimate(
            flops=2 * most * feat * ff * 4, bytes_accessed=10 * most * feat, transcendentals=0
        ),
        name="moe_back_last",
    )(offs, ids, slot, rows, ab, grads, gate, w_in, w_down, pair0, gg0)


def split_router(router):
    one = router.astype(BF16)
    rest = router - one.astype(F32)
    two = rest.astype(BF16)
    three = (rest - two.astype(F32)).astype(BF16)
    return jnp.concatenate([one, two, three, jnp.zeros_like(one)], axis=1)


def add_body(starts, *refs):
    step = pl.program_id(0)
    pieces = len(starts) - 1
    own, far, out_ref = refs[:pieces], refs[pieces : 2 * pieces], refs[-1]
    for p in range(pieces):

        @pl.when((step >= starts[p]) & (step < starts[p + 1]))
        def _(p=p):
            out_ref[0] = own[p][...].astype(F32) + far[p][...].astype(F32)


def add_pairs(own, far, index, local, held=None):
    block = math.gcd(*[piece.shape[0] for piece in own])
    width = own[0].shape[1]
    starts = [0]
    for piece in own:
        starts.append(starts[-1] + piece.shape[0] // block)

    def piece(p):
        return lambda i: (jnp.clip(i - starts[p], 0, starts[p + 1] - starts[p] - 1), 0)

    return pl.pallas_call(
        functools.partial(add_body, starts),
        grid=(starts[-1],),
        in_specs=[pl.BlockSpec((block, width), piece(p)) for p in range(len(own))] * 2
        + ([] if held is None else [pl.BlockSpec(memory_space=pl.ANY)]),
        out_specs=pl.BlockSpec((1, block, width), lambda i: (index, i, 0)),
        out_shape=jax.ShapeDtypeStruct((local, starts[-1] * block, width), F32),
        input_output_aliases={} if held is None else {2 * len(own): 0},
        compiler_params=pltpu.CompilerParams(vmem_limit_bytes=40 * 1024 * 1024),
        cost_estimate=beside_transfers(),
        name="add_pairs",
    )(*own, *far, *([] if held is None else [held]))


def mid_back_body(
    own_ref, moved_ref, side_ref, term_ref, mid_ref, dy_ref, gain_ref, out_ref,
    grad_ref, low_ref, gain_grad_ref, block_ref,
):
    @pl.when(pl.program_id(0) == 0)
    def _():
        mid = mid_ref[...]
        scale = lax.rsqrt(jnp.mean(mid * mid, axis=1, keepdims=True) + EPSILON)
        grad = own_ref[...].astype(F32) + moved_ref[...].astype(F32)
        grad = grad + side_ref[...].astype(F32) + term_ref[...]
        gain_grad_ref[...] = jnp.sum(grad * mid * scale, axis=0, keepdims=True)
        weighted = grad * gain_ref[...]
        inner = jnp.mean(weighted * mid, axis=1, keepdims=True)
        total = dy_ref[...].astype(F32) + scale * weighted - mid * (scale * scale * scale * inner)
        grad_ref[...] = total
        low_ref[...] = total.astype(BF16)

    block_ref[0] = dot_nn(low_ref[...], out_ref[0]).astype(BF16)


def mid_back(sums, router_term, middle, out_grad, gain, out_all):
    tok, feat = middle.shape
    groups, _, width = out_all.shape
    args = (*sums, router_term, middle, out_grad, gain[None])
    outs = [
        jax.ShapeDtypeStruct((tok, feat), F32),
        jax.ShapeDtypeStruct((tok, feat), BF16),
        jax.ShapeDtypeStruct((1, feat), F32),
        jax.ShapeDtypeStruct((groups, tok, width), BF16),
    ]
    return pl.pallas_call(
        mid_back_body,
        grid=(groups,),
        in_specs=[whole_block(v) for v in args]
        + [pl.BlockSpec((1, feat, width), lambda i: (i, 0, 0))],
        out_specs=[whole_block(v) for v in outs[:-1]]
        + [pl.BlockSpec((1, tok, width), lambda i: (i, 0, 0))],
        out_shape=outs,
        compiler_params=pltpu.CompilerParams(vmem_limit_bytes=60 * 1024 * 1024),
        cost_estimate=pl.CostEstimate(
            flops=2 * tok * feat * feat, bytes_accessed=4 * feat * feat, transcendentals=0
        ),
        name="mid_back",
    )(*args, out_all)


def beside_transfers():
    return pl.CostEstimate(flops=12_000_000_000, bytes_accessed=1 << 20, transcendentals=0)


def near_terms_body(near_a, far_a, near_b, far_b, out_a, out_b):
    out_a[...] = (near_a[...].astype(F32) + far_a[...].astype(F32)).astype(BF16)
    out_b[...] = (near_b[...].astype(F32) + far_b[...].astype(F32)).astype(BF16)


def near_terms(near, far, first, second, tok):
    feat = near.shape[1]

    def block(index):
        return pl.BlockSpec((tok, feat), lambda i: (index, 0), pipeline_mode=pl.Buffered(1))

    return pl.pallas_call(
        near_terms_body,
        grid=(1,),
        in_specs=[block(first), block(first), block(second), block(second)],
        out_specs=[block(0), block(0)],
        out_shape=[jax.ShapeDtypeStruct((tok, feat), BF16)] * 2,
        compiler_params=pltpu.CompilerParams(vmem_limit_bytes=60 * 1024 * 1024),
        cost_estimate=beside_transfers(),
        name="near_terms",
    )(near, far, near, far)


def put_rows(part, first, core, kept_ref, given_ref):
    chunk = kept_ref.shape[1]
    for n in range(part.shape[0] // chunk):
        rows = part[n * chunk : (n + 1) * chunk]
        b = first + n

        @pl.when(core == b % 2)
        def _(rows=rows, b=b):
            kept_ref[b // 2] = rows

        @pl.when(core != b % 2)
        def _(rows=rows, b=b):
            given_ref[b // 2] = rows


def w_out_body(core_ref, low_ref, heads_ref, kept_ref, given_ref):
    step = low_ref.shape[1] // 4
    for c in range(4):
        part = dot_tn(low_ref[:, c * step : (c + 1) * step], heads_ref[...]).astype(BF16)
        put_rows(part, c * step // kept_ref.shape[1], core_ref[0], kept_ref, given_ref)


def w_out_part(core, low, heads, chunk):
    feat, width = low.shape[1], heads.shape[1]
    out = jax.ShapeDtypeStruct((feat // chunk // 2, chunk, width), BF16)
    return pl.pallas_call(
        w_out_body,
        grid=(1,),
        in_specs=[pl.BlockSpec(memory_space=pltpu.SMEM), whole_block(low), whole_block(heads)],
        out_specs=[whole_block(out)] * 2,
        out_shape=[out] * 2,
        compiler_params=pltpu.CompilerParams(vmem_limit_bytes=60 * 1024 * 1024),
        cost_estimate=beside_transfers(),
        name="w_out_part",
    )(core, low, heads)


def w_qkv_body(core_ref, rows_ref, mixed_ref, w_ref, gain_ref, kept_ref, given_ref, sum_ref):
    feat = rows_ref.shape[1]
    width = mixed_ref.shape[1]
    step = feat // 4
    ones = jnp.ones((8, width), F32)
    for c in range(4):
        at = slice(c * step, (c + 1) * step)
        part = dot_tn(rows_ref[:, at], mixed_ref[...])
        put_rows(
            part.astype(BF16), c * step // kept_ref.shape[1], core_ref[0], kept_ref, given_ref
        )
        sums = lax.dot_general(
            ones,
            part * w_ref[at, :].astype(F32),
            (((1,), (1,)), ((), ())),
            precision=HIGHEST,
            preferred_element_type=F32,
        )
        sum_ref[:, at] = sums[0:1] / gain_ref[:, at]


def w_qkv_part(core, rows, mixed, w_own, gain, chunk):
    feat, width = rows.shape[1], mixed.shape[1]
    out = jax.ShapeDtypeStruct((feat // chunk // 2, chunk, width), BF16)
    sums = jax.ShapeDtypeStruct((1, feat), F32)
    args = (rows, mixed, w_own, gain[None])
    return pl.pallas_call(
        w_qkv_body,
        grid=(1,),
        in_specs=[pl.BlockSpec(memory_space=pltpu.SMEM)] + [whole_block(v) for v in args],
        out_specs=[whole_block(out), whole_block(out), whole_block(sums)],
        out_shape=[out, out, sums],
        compiler_params=pltpu.CompilerParams(vmem_limit_bytes=60 * 1024 * 1024),
        cost_estimate=beside_transfers(),
        name="w_qkv_part",
    )(core, *args)


def row_places(first, local, rt_all, rt_ids):
    sources = rt_all.shape[0]
    mine = first[0] + jnp.arange(local, dtype=jnp.int32)
    named = rt_all[:, None, :, :] == mine[None, :, None, None]
    counts = jnp.sum(named.astype(jnp.int32), axis=(2, 3))
    order = rt_ids[:, None] == jnp.arange(sources, dtype=jnp.int32)[None, :]
    counts = jnp.sum(jnp.where(order[:, :, None], counts[None], 0), axis=1)
    rounded = (counts + 15) // 16 * 16
    before = (
        jnp.arange(sources, dtype=jnp.int32)[None, :]
        < jnp.arange(sources + 1, dtype=jnp.int32)[:, None]
    )
    return jnp.sum(jnp.where(before[:, :, None], rounded[None], 0), axis=1).T


def rope_rows(positions):
    freq_index = jnp.arange(HD // 2, dtype=F32)
    inverse = jnp.exp(freq_index * (-2.0 * math.log(10000.0) / HD))
    angles = positions.astype(F32)[:, None] * jnp.tile(inverse, 4)[None, :]
    return jnp.cos(angles), jnp.sin(angles)


def seq_layout(block_lengths, block_tok):
    seq_ends = jnp.cumsum(block_lengths)
    starts = seq_ends - block_lengths
    places = jnp.arange(block_tok, dtype=jnp.int32)
    segment = jnp.sum((places[:, None] >= seq_ends[None, :]).astype(jnp.int32), axis=1)
    owners = segment[:, None] == jnp.arange(block_lengths.shape[0], dtype=jnp.int32)[None, :]
    offset = jnp.sum(jnp.where(owners, starts[None, :], 0), axis=1)
    return places - offset, offset


def norm_apply(row_vals, gain_vec):
    scale_row = lax.rsqrt(jnp.mean(row_vals * row_vals, axis=1, keepdims=True) + EPSILON)
    return row_vals * scale_row * gain_vec


def norm_back(row_vals, gain_vec, grad):
    scale_row = lax.rsqrt(jnp.mean(row_vals * row_vals, axis=1, keepdims=True) + EPSILON)
    weighted = grad * gain_vec
    inner = jnp.mean(weighted * row_vals, axis=1, keepdims=True)
    return scale_row * weighted - row_vals * (scale_row * scale_row * scale_row * inner)


def shift(values, axis, by):
    size = lax.axis_size(axis)
    return lax.ppermute(values, axis, [(i, (i + by) % size) for i in range(size)])


def swap(values, axis, bit):
    size = lax.axis_size(axis)
    return lax.ppermute(values, axis, [(i, i ^ bit) for i in range(size)])


def plane_places(row, col):
    rows, cols = lax.axis_size("row"), lax.axis_size("col")
    index = jnp.arange(rows * cols, dtype=jnp.int32)
    core, side, back = index // (2 * cols), index // cols % 2, index % cols
    return row ^ (core + 2 * side), (col - back + cols) % cols


def gather_small_steps(row, col):
    rows = lax.axis_size("row")
    def over(values, axis, bits):
        for bit in bits:
            values = jnp.concatenate([values, swap(values, axis, bit)], axis=0)
        return values

    steps = [
        functools.partial(over, axis=axis, bits=bits)
        for axis, bits in (("row", (1, 2)), ("col", (1,)), ("col", (2,)))
    ]
    from_row, from_col = plane_places(row, col)
    return steps, (from_row ^ row) + rows * (from_col ^ col)


def in_step(stages, *chains):
    values = [value for value, _ in chains]
    for stage in range(stages):
        for index, (_, steps) in enumerate(chains):
            mine = steps[stage : stage + 1] if stage + 1 < stages else steps[stage:]
            for step in mine:
                values[index] = step(values[index])
        values = list(lax.optimization_barrier(tuple(values)))
    return values


def ring_steps(by):
    return [lambda held: held + [shift(held[-1], "col", by)]] * (lax.axis_size("col") - 1)


def gather_plane(values):
    cols = lax.axis_size("col")
    line, across = [values], []
    for k in range(cols):
        side = swap(line[k], "row", 2)
        later = shift(line[k], "col", 1) if k + 1 < cols else None
        side, later = lax.optimization_barrier((side, later))
        line.append(later)
        across.append(side)
    own = line[:cols] + across
    return own + [swap(part, "row", 1) for part in own]


def after(values, *earlier):
    return lax.optimization_barrier((values, *earlier))[0]


def sum_rows_steps(row):
    dps = lax.axis_size("dp")
    dp = lax.axis_index("dp").astype(jnp.int32)
    places = [("row", 1, row % 2, 2), ("row", 2, row // 2, 1)]
    bit = dps // 2
    while bit:
        places.append(("dp", bit, dp // bit % 2, 0))
        bit //= 2

    def cut(values, place, dim):
        half = values.shape[dim] // 2
        return [
            lax.dynamic_slice_in_dim(values, at * half, half, dim) for at in (place, 1 - place)
        ]

    def add(halves, axis, bit):
        kept, given = halves
        return (kept.astype(F32) + swap(given, axis, bit).astype(F32)).astype(BF16)

    return [
        (functools.partial(cut, place=p, dim=d), functools.partial(add, axis=a, bit=b))
        for a, b, p, d in places
    ]


def row_halves(row):
    def halve(values, bit, place, dim):
        kept, given = [
            lax.dynamic_slice_in_dim(values, at, 1, dim) for at in (place, 1 - place)
        ]
        return kept + swap(given, "row", bit)

    def spread(values, bit, place, dim):
        other = swap(values, "row", bit)
        return jnp.where(
            place == 0,
            jnp.concatenate([values, other], axis=dim),
            jnp.concatenate([other, values], axis=dim),
        )

    places = [(1, row % 2, 2), (2, row // 2, 1)]
    return (
        [functools.partial(halve, bit=b, place=p, dim=d) for b, p, d in places],
        [functools.partial(spread, bit=b, place=p, dim=d) for b, p, d in places[::-1]],
    )


def sum_steps():
    steps = []
    for axis in ("row", "col", "dp"):
        bit = 1
        while bit < lax.axis_size(axis):
            steps.append(lambda v, axis=axis, bit=bit: v + swap(v, axis, bit))
            bit *= 2
    return steps


def shards(
    hidden_in,
    norm_gain_attn,
    norm_gain_moe,
    w_qkv,
    w_out,
    router,
    w_in,
    w_down,
    lengths,
    routes,
    out_grad,
):
    tok, feat = hidden_in.shape
    cols = lax.axis_size("col")
    rows = lax.axis_size("row")
    block_tok = tok * cols
    experts = router.shape[1]
    sources = rows * cols
    local = w_in.shape[0]
    cap = tok * TOP * 2 // experts
    head_cols = w_out.shape[1]
    group = 4
    plane = ("row", "col")
    col = lax.axis_index("col").astype(jnp.int32)
    row = lax.axis_index("row").astype(jnp.int32)
    here = col.reshape(1)
    first = ((row * cols + col) * local).reshape(1)
    rows_in = hidden_in.astype(F32)
    grad_out = out_grad.astype(F32)

    normed_attn = norm_apply(rows_in, norm_gain_attn).astype(BF16)
    qkv_own = lax.all_gather(w_qkv, ("dp", "row"), axis=0, tiled=True)
    out_all = lax.all_gather(w_out, ("col", "dp", "row"), axis=0, tiled=True).reshape(
        cols, feat, head_cols
    )
    positions, seq_start = seq_layout(lengths[0], block_tok)
    cos, sin = rope_rows(positions)
    starts = jnp.pad(seq_start.reshape(cols, tok), ((0, -cols % 8), (0, 0)))
    small_steps, rt_ids = gather_small_steps(row, col)
    tables = (cos, sin, starts, split_router(router))
    parts, rt_all, tables = in_step(
        cols - 1, ([normed_attn], ring_steps(1)), (routes.T[None], small_steps), (tables, [])
    )
    cos, sin, starts, router_parts = tables

    q_rows, key_rows, value_rows, lse, heads_block = attn_forward(
        here, parts, qkv_own, cos, sin, starts
    )
    heads = lax.all_to_all(
        heads_block.reshape(cols, tok, head_cols), "col", split_axis=0, concat_axis=0, tiled=True
    )
    middle = rows_in + jnp.einsum(
        "ctj,cdj->td", heads, out_all, preferred_element_type=F32
    )
    normed_moe = norm_apply(middle, norm_gain_moe).astype(BF16)
    heads = jnp.concatenate([after(heads, normed_moe)[k] for k in range(cols)], axis=1)

    offs = row_places(first, local, rt_all, rt_ids)
    x_parts = gather_plane(normed_moe)
    block_rows = jnp.concatenate(after(parts, normed_moe), axis=0)
    x_parts[-1], heads, block_rows = lax.optimization_barrier((x_parts[-1], heads, block_rows))
    dy_all = lax.all_gather(after(out_grad, x_parts[2]), plane, axis=0, tiled=True)
    from_row, from_col = plane_places(row, col)
    whole_ids = from_row * cols + from_col
    index = jnp.arange(sources, dtype=jnp.int32)
    twist_row, back_col = index // cols ^ row, (col - index % cols + cols) % cols
    places = (twist_row % 2 * 2 + twist_row // 2) * cols + back_col
    ids = jnp.stack([rt_ids, places, whole_ids, whole_ids])

    res_part, rows_kept, ab_kept, gate, slot = moe_front(
        first, ids, offs, x_parts, rt_all, router_parts, w_in, w_down, cap, group
    )
    res = lax.psum_scatter(res_part, plane, scatter_dimension=0, tiled=True)
    pair0, gg0, dy_kept, *own0 = moe_back_first(
        offs, ids, dy_all, slot, rows_kept, ab_kept, gate, w_in, w_down, cap, group
    )
    paired = lax.axis_size("dp") == 2
    own = {0: list(own0)}
    far = {0: [None] * len(own0), 1: []}

    def exchange(e, p, *earlier):
        if not paired:
            return []
        far[e][p] = swap(after(own[e][p], *earlier), "dp", 1)
        return [(e, p)]

    def arrived(values, sent):
        if sent:
            values, kept = lax.optimization_barrier((values, [far[e][p] for e, p in sent]))
            for (e, p), piece in zip(sent, kept):
                far[e][p] = piece
        return values

    sent = exchange(0, 0, pair0)
    gn_far, gn_near, dg, *own1 = moe_back_last(
        offs, ids, slot, rows_kept, ab_kept, dy_kept, gate, w_in, w_down, pair0, gg0, cap,
        group,
    )
    own[1], far[1] = list(own1), [None] * len(own1)
    gn_far = arrived(gn_far, sent)

    from_far = swap(gn_far, "row", 1)
    sent = exchange(0, 1, gn_far)
    dg_back = lax.all_to_all(dg, plane, split_axis=0, concat_axis=0, tiled=True)
    from_far, dg_back = arrived(lax.optimization_barrier((from_far, dg_back)), sent)

    sum_out, sum_all = sum_rows_steps(row), sum_steps()
    halve, spread = row_halves(row)
    gn, terms = None, near_terms(gn_near, from_far, 2 * cols - 1, cols - 1, tok)
    for k in range(cols - 1, -1, -1):
        side = swap(terms[0], "row", 2)
        sent = exchange(*((0, 2), (0, 3), (1, 2), (1, 3))[cols - 1 - k], terms[0])
        own_term, moved = terms[1], None
        if gn is not None:
            moved = shift(gn, "col", -1)
        if k:
            terms = near_terms(gn_near, after(from_far, terms[0]), cols + k - 1, k - 1, tok)
        if k == cols - 1:
            normed_wide = normed_moe.astype(F32)
            logits = jnp.dot(
                normed_wide, router, precision=HIGHEST, preferred_element_type=F32
            )
            expert_ids = jnp.arange(experts, dtype=jnp.int32)
            used = jnp.any(routes[:, :, None] == expert_ids[None, None, :], axis=1)
            top = jnp.max(jnp.where(used, logits, MASKED_SCORE), axis=1, keepdims=True)
            exps = jnp.where(used, jnp.exp(logits - top), 0.0)
            gates = exps / jnp.sum(exps, axis=1, keepdims=True)
            side, gates = lax.optimization_barrier((side, gates))
        if k == cols - 2:
            grad_gates = after(dg_back, gates)[:, :local].reshape(experts, tok).T
            grad_logits = gates * (
                grad_gates - jnp.sum(gates * grad_gates, axis=1, keepdims=True)
            )
            router_term = lax.dot_general(
                grad_logits,
                router,
                (((1,), (1,)), ((), ())),
                precision=HIGHEST,
                preferred_element_type=F32,
            )
            grad_router = lax.dot_general(
                grad_logits,
                normed_wide,
                (((0,), (0,)), ((), ())),
                precision=HIGHEST,
                preferred_element_type=F32,
            )
            small = halve[0](grad_router.reshape(1, 2, 2, experts // 4, feat))
            side, router_term, small = lax.optimization_barrier((side, router_term, small))
        if k == 1:
            side, res = lax.optimization_barrier((side, res))
        own_term, moved, side, terms = arrived(
            lax.optimization_barrier((own_term, moved, side, terms)), sent
        )
        if k:
            gn = own_term.astype(F32) + side.astype(F32)
            if moved is not None:
                gn = gn + moved.astype(F32)
            gn = gn.astype(BF16)

    grad_middle, grad_attn, gain_moe_part, grad_heads = mid_back(
        (own_term, moved, side), router_term, middle, out_grad, norm_gain_moe, out_all
    )
    sent = exchange(1, 4, side)
    grads_block = lax.all_to_all(
        grad_heads, "col", split_axis=0, concat_axis=0, tiled=True
    )
    small = halve[1](after(small, grad_heads))
    core = (row % 2).reshape(1)
    w_out_sum = w_out_part(core, after(grad_attn, grad_heads), heads, w_out.shape[0])
    w_out_sum = [v.reshape(-1, 2, 1, w_out.shape[0], feat) for v in w_out_sum]
    w_out_sum = sum_out[1][0](sum_out[0][1](w_out_sum))
    grads_block, small, w_out_sum = arrived(
        lax.optimization_barrier((grads_block, small, w_out_sum)), sent
    )

    sent = exchange(1, 0, grads_block)
    small = sum_all[2](small)
    grad_mixed, first_mixed = attn_backward(
        here, grads_block.reshape(cols * tok, head_cols), q_rows, key_rows, value_rows, lse,
        cos, sin, starts, cols,
    )
    w_out_sum = sum_out[1][1](w_out_sum)
    grad_mixed, first_mixed, small = arrived(
        lax.optimization_barrier((grad_mixed, first_mixed, small)), sent
    )

    def na_part(k, *earlier):
        mixed = after(grad_mixed[k * tok : (k + 1) * tok], *earlier)
        return dot_nt(mixed, qkv_own)

    def held(*values):
        return arrived(lax.optimization_barrier(values), sent)

    sent = exchange(1, 1, grad_mixed)
    first_na = dot_nt(first_mixed, qkv_own).astype(BF16)
    grad_na = shift(first_na, "col", -1)
    small = sum_all[3](small)
    *w_qkv_sum, gain_attn_part = w_qkv_part(
        core, after(block_rows, first_na), grad_mixed, qkv_own, norm_gain_attn, w_qkv.shape[0]
    )
    w_qkv_sum = [v.reshape(-1, 2, 1, *w_qkv.shape) for v in w_qkv_sum]
    w_qkv_sum = sum_out[0][1](w_qkv_sum)
    gains = sum_all[0](jnp.concatenate([gain_moe_part, gain_attn_part], axis=0))
    next_na = na_part(cols - 2, first_na)
    grad_na, small, w_out_sum, w_qkv_sum, gains, next_na = held(
        grad_na, small, w_out_sum, w_qkv_sum, gains, next_na
    )

    grad_na = (grad_na.astype(F32) + next_na).astype(BF16)
    sent = []
    next_na = na_part(cols - 3, grad_na)
    grad_w_in = grad_w_down = next_na
    if paired:
        downs = len(piece_shapes(feat, FFE, True)[0])
        grad_w_in = add_pairs(own[0][downs:], after(far[0][downs:], next_na), 0, local)
        grad_w_down = add_pairs(own[0][:downs], after(far[0][:downs], next_na), 0, local)
    grad_na = shift(grad_na, "col", -1)
    gains = sum_all[1](gains)
    w_qkv_sum = sum_out[1][0](w_qkv_sum)
    for step in sum_out[2:]:
        w_out_sum = step[1](step[0](w_out_sum))
    for step in sum_all[4:]:
        small = step(small)
    gains = sum_all[2](gains)
    grad_na, next_na, gains, small, w_qkv_sum, grad_w_in, grad_w_down, w_out_sum = held(
        grad_na, next_na, gains, small, w_qkv_sum, grad_w_in, grad_w_down, w_out_sum
    )

    grad_na = (grad_na.astype(F32) + next_na).astype(BF16)
    next_na = na_part(cols - 4, grad_na)
    lines = lax.all_to_all(
        jnp.stack([w_out_sum[..., k * head_cols : (k + 1) * head_cols] for k in range(cols)]),
        "col",
        split_axis=0,
        concat_axis=0,
        tiled=True,
    )
    result = middle + after(res, next_na).astype(F32)
    grad_na = shift(grad_na, "col", -1)
    gains = sum_all[3](gains)
    small = spread[0](small)
    w_qkv_sum = sum_out[1][1](w_qkv_sum)
    if paired:
        downs = len(piece_shapes(feat, FFE, False)[0])
        grad_w_in = add_pairs(own[1][downs:], after(far[1][downs:], next_na), 1, local, grad_w_in)
        grad_w_down = add_pairs(own[1][:downs], far[1][:downs], 1, local, grad_w_down)
    else:
        ins, outs = [], []
        for e in range(local):
            downs = len(piece_shapes(feat, FFE, e == 0)[0])
            outs.append(jnp.concatenate(own[e][:downs]))
            ins.append(jnp.concatenate(own[e][downs:]))
        grad_w_in = lax.psum(jnp.stack(ins), "dp").astype(F32)
        grad_w_down = lax.psum(jnp.stack(outs), "dp").astype(F32)
    grad_na, next_na, gains, small, w_qkv_sum, lines, grad_w_in, grad_w_down, result = held(
        grad_na, next_na, gains, small, w_qkv_sum, lines, grad_w_in, grad_w_down, result
    )

    grad_na = grad_na.astype(F32) + next_na
    for step in sum_all[4:]:
        gains = step(gains)
    small = spread[1](small).reshape(experts, feat)
    for step in sum_out[2:]:
        w_qkv_sum = step[1](step[0](w_qkv_sum))
    grad_hidden = grad_middle + norm_back(rows_in, norm_gain_attn, grad_na)
    grad_w_qkv = w_qkv_sum.reshape(w_qkv.shape).astype(F32)
    grad_w_out = jnp.sum(lines.astype(F32), axis=0).reshape(w_out.shape)
    return (
        result,
        grad_hidden,
        gains[1],
        gains[0],
        grad_w_qkv,
        grad_w_out,
        small.T,
        grad_w_in,
        grad_w_down,
    )


def solution(mesh):
    in_specs = (
        P(("dp", "row", "col"), None),
        P(),
        P(),
        P(("dp", "row"), "col"),
        P(("dp", "row"), "col"),
        P(),
        P(("row", "col"), None, None),
        P(("row", "col"), None, None),
        P(("dp", "row"), None),
        P(("dp", "row", "col"), None),
        P(("dp", "row", "col"), None),
    )
    out_specs = (
        P(("dp", "row", "col"), None),
        P(("dp", "row", "col"), None),
        P(),
        P(),
        P(("dp", "row"), "col"),
        P(("dp", "row"), "col"),
        P(),
        P(("row", "col"), None, None),
        P(("row", "col"), None, None),
    )
    return jax.shard_map(shards, mesh=mesh, in_specs=in_specs, out_specs=out_specs, check_vma=False)
```
